32 devices in a mesh: ens: 2 (over y), cell: 4 (over z), win: 4 (over x, core).
Axes of the slice: x: 2, y: 2, z: 4, core: 2. Of those that a mesh axis runs over, the one named last changes fastest.
Arguments:
- prior_flux: float32 [64, 2048], P(('ens', 'win'), 'cell'), parts along dimension 0, may hold values from -6 to 6
- observed: float32 [8, 512], P(('ens', 'cell')), parts along dimension 0, may hold values from -6 to 6
- obs_weight: float32 [8, 512], P(('ens', 'cell')), parts along dimension 0, may hold values from 1 to 10
- footprint: float32 [4, 4, 4, 16, 4096], P('cell', 'win'), may hold values from -0.1875 to 0.1875
- flux_slot: int32 [4, 4, 4, 16], P('cell', 'win'), may hold values from 0 to 63
- obs_slot: int32 [4, 4, 4, 16], P('cell', 'win'), may hold values from 0 to 7
- slot_count: int32 [4, 4, 4], P('cell', 'win'), may hold values from 1 to 16, as said below
Outputs:
- increment: float32 [64, 2048], P(('ens', 'win'), 'cell'), parts along dimension 0
- departure: float32 [8, 512], P(('ens', 'cell')), parts along dimension 0
The draws below stay inside these ranges and needn't reach their ends.
There are 2 independent parts, one for each index of `ens`. The reference program is written for one: setup_inputs(seed, part) draws one part's arguments, and reference() takes and returns one part's arrays. A program takes and returns all parts, laid end to end along the dimension named above; an argument that names none is the same for every part. Nothing has to cross between parts.
Inputs may be any that keep to these rules, and one draw needn't show every extreme that they name: `slot_count`: some owner receives 16 live slots from every device of a window group, and every device sends 16 live slots to some owner.
All inputs are finite; a program needn't handle non-finite values.
Results may differ from the reference program's by a relative error of at most 0.0001.
Values sent between devices are 32-bit elements; how exact they have to be, the bound alone decides.
No kernel may reach another device: no remote copies, remote signals or barrier semaphores. Data moves between devices by JAX's collectives and lax.ppermute only.
A program may use at most 128 MiB of HBM per device.

```python
import math
import jax
import jax.numpy as jnp
from jax import lax

CB = 64
OB = 64
CBLK_DEV = 8
WIN_DEV = 8
OBLK_DEV = 8
CAP = 16
ITERS = 2
WINDOWS = 32
CELLS = 2048
OBS_DEV = 512
N_CELL = 4
N_WIN = 4


def draw_slot_count(key, part):
    key = jax.random.fold_in(key, 11)
    first_key, second_key, third_key = jax.random.split(key, 3)
    counts_base = jax.random.randint(first_key, (N_CELL, N_WIN, N_CELL), 1, CAP // 2 + 1)
    hot_receiver = jax.random.randint(second_key, (N_WIN,), 0, N_CELL)
    hot_sender = jax.random.randint(third_key, (N_CELL, N_WIN), 0, N_CELL)
    owners_row = jnp.arange(N_CELL, dtype=jnp.int32)[None, None, :]
    is_full = (owners_row == hot_receiver[None, :, None]) | (owners_row == hot_sender[:, :, None])
    return jnp.where(is_full, CAP, counts_base).astype(jnp.int32)


def set_ends(result, own_key, smallest, high):
    longest = result.shape.index(max(result.shape))
    spots = []
    for shift in (0, 1):
        where = [jax.random.randint(jax.random.fold_in(own_key, axis), (), 0, length) for axis, length in enumerate(result.shape)]
        where[longest] = (where[longest] + shift) % result.shape[longest]
        spots.append(tuple(where))
    return result.at[spots[0]].set(smallest).at[spots[1]].set(high)


def level_of(own_key, extent, pieces, low, largest):
    gain, own = 1.0, jax.random.fold_in(own_key, 6)
    for position, blocks in pieces:
        draws = jnp.exp(jax.random.uniform(jax.random.fold_in(own, position), (blocks,), jnp.float32, low / len(pieces), largest / len(pieces)))
        gain = gain * jnp.repeat(draws, extent[position] // blocks).reshape([-1 if axis == position else 1 for axis in range(len(extent))])
    return gain


def centred(stream_key, extent, width, bound, shards=(), kind=jnp.bfloat16):
    array = jax.random.normal(stream_key, extent, jnp.float32) * width
    if len(shards) > 0:
        array = level_of(stream_key, extent, shards, -0.22, 0.18) * array
    return jnp.clip(array, min=-bound, max=bound).astype(kind)


def setup_inputs(seed: int = 0, part: int = 0) -> dict:
    key_list = jax.random.split(jax.random.key(seed), 8)
    part_splits = jax.random.split(jax.random.fold_in(key_list[7], part), 8)
    prior_flux = centred(part_splits[0], (WINDOWS, CELLS), 1.0, 6.0, ((0, 4), (1, 4)), jnp.float32)
    observed = centred(part_splits[1], (N_CELL, OBS_DEV), 1.0, 6.0, ((0, 4),), jnp.float32)
    obs_weight = jnp.clip(jnp.exp(math.log(10.0) - 2.3025851 * jax.random.uniform(part_splits[2], (N_CELL, OBS_DEV), jnp.float32) ** level_of(part_splits[2], (N_CELL, OBS_DEV), ((0, 4),), -0.2, 0.2)), 1.0, 10.0)
    footprint = centred(key_list[3], (N_CELL, N_WIN, N_CELL, CAP, OB * CB), (CB * N_WIN * N_CELL * CAP // (2 * OBLK_DEV)) ** -0.5, 0.1875, ((0, 4), (1, 4)), jnp.float32)
    flux_slot = set_ends(jax.random.randint(key_list[4], (N_CELL, N_WIN, N_CELL, CAP), 0, WIN_DEV * CBLK_DEV), jax.random.fold_in(key_list[4], 1), 0, (WIN_DEV * CBLK_DEV) - 1).astype(jnp.int32)
    obs_slot = set_ends(jax.random.randint(key_list[5], (N_CELL, N_WIN, N_CELL, CAP), 0, OBLK_DEV), jax.random.fold_in(key_list[5], 1), 0, OBLK_DEV - 1).astype(jnp.int32)
    slot_count = draw_slot_count(jax.random.fold_in(key_list[7], 71), part)
    return {"prior_flux": prior_flux, "observed": observed, "obs_weight": obs_weight, "footprint": footprint, "flux_slot": flux_slot, "obs_slot": obs_slot, "slot_count": slot_count}


def forward_model(matrices, selected, live_mask, obs_pick):
    partial_value = jnp.einsum("cwojik,cwojk->cwoji", matrices, selected, precision=lax.Precision.HIGHEST) * live_mask[..., None]
    block_sums = jnp.einsum("cwojb,cwoji->cbi", obs_pick, partial_value, precision=lax.Precision.HIGHEST)
    return block_sums.reshape(N_CELL, OBLK_DEV * OB)


def reference(prior_flux, observed, obs_weight, footprint, flux_slot, obs_slot, slot_count):
    matrices = footprint.reshape(N_CELL, N_WIN, N_CELL, CAP, OB, CB)
    slot_ids = jnp.arange(CAP, dtype=jnp.int32)
    live_mask = (slot_ids[None, None, None, :] < slot_count[..., None]).astype(jnp.float32)
    window_index = jnp.arange(N_WIN, dtype=jnp.int32)[None, :, None, None] * WIN_DEV + flux_slot // CBLK_DEV
    cell_block = jnp.arange(N_CELL, dtype=jnp.int32)[None, None, :, None] * CBLK_DEV + flux_slot % CBLK_DEV
    flat_index = (window_index * (N_CELL * CBLK_DEV) + cell_block).astype(jnp.int32)
    obs_pick = (obs_slot[..., None] == jnp.arange(OBLK_DEV, dtype=jnp.int32)).astype(jnp.float32)
    current = prior_flux
    departure = jnp.zeros_like(observed)
    for step in range(ITERS):
        flux_blocks = current.reshape(WINDOWS * N_CELL * CBLK_DEV, CB)
        selected = flux_blocks[flat_index]
        modeled = forward_model(matrices, selected, live_mask, obs_pick)
        departure = obs_weight * (modeled - observed)
        picked = jnp.einsum("cwojb,cbi->cwoji", obs_pick, departure.reshape(N_CELL, OBLK_DEV, OB), precision=lax.Precision.HIGHEST)
        returned = jnp.einsum("cwojik,cwoji->cwojk", matrices, picked, precision=lax.Precision.HIGHEST) * live_mask[..., None]
        gradient = jax.ops.segment_sum(returned.reshape(-1, CB), flat_index.reshape(-1), num_segments=WINDOWS * N_CELL * CBLK_DEV)
        gradient = gradient.reshape(WINDOWS, CELLS)
        current = current - 0.5 * ((current - prior_flux) + gradient)
    return current - prior_flux, departure
```

```python
import jax
import jax.numpy as jnp
from jax import lax
from jax.sharding import PartitionSpec as P

CB = 64
OB = 64
CBLK_DEV = 8
WIN_DEV = 8
OBLK_DEV = 8

HI = lax.Precision.HIGHEST


def local(prior_flux, observed, obs_weight, footprint, flux_slot, obs_slot, slot_count):
    owners = footprint.shape[2]
    capacity = footprint.shape[3]
    slots = owners * capacity
    blocks = WIN_DEV * CBLK_DEV
    live = (
        lax.broadcasted_iota(jnp.int32, (owners, capacity), 1)
        < slot_count.reshape(owners, 1)
    ).astype(jnp.float32)
    matrices = footprint.reshape(owners, capacity, OB, CB)
    obs_pick = (
        obs_slot.reshape(slots, 1) == lax.broadcasted_iota(jnp.int32, (1, OBLK_DEV), 1)
    ).astype(jnp.float32) * live.reshape(slots, 1)
    flux_pick = (
        flux_slot.reshape(owners, capacity, 1)
        == lax.broadcasted_iota(jnp.int32, (1, 1, blocks), 2)
    ).astype(jnp.float32)

    def forward(flux):
        selected = jnp.einsum("ocb,obj->ocj", flux_pick, flux, precision=HI)
        value = jnp.einsum("ocij,ocj->oci", matrices, selected, precision=HI)
        sums = jnp.dot(obs_pick.T, value.reshape(slots, OB), precision=HI)
        return lax.psum(sums.reshape(1, OBLK_DEV * OB), "win")

    def adjoint(departure):
        picked = jnp.dot(obs_pick, departure.reshape(OBLK_DEV, OB), precision=HI)
        picked = picked.reshape(owners, capacity, OB)
        returned = jnp.einsum("ocij,oci->ocj", matrices, picked, precision=HI)
        return jnp.einsum("ocb,ocj->obj", flux_pick, returned, precision=HI)

    flux = lax.all_gather(prior_flux.reshape(blocks, CB), "cell")
    model0 = forward(flux)
    departure0 = obs_weight * (model0 - observed)
    adjoint0 = lax.psum(adjoint(departure0), "cell")
    model1 = forward(flux - 0.5 * adjoint0)
    departure1 = obs_weight * (model1 - observed)
    increment = lax.psum_scatter(
        adjoint(-0.25 * departure0 - 0.5 * departure1), "cell", scatter_dimension=0
    )
    return increment.reshape(WIN_DEV, CBLK_DEV * CB), departure1


def solution(mesh):
    placed = (
        P(("ens", "win"), "cell"),
        P(("ens", "cell"), None),
        P(("ens", "cell"), None),
        P("cell", "win", None, None, None),
        P("cell", "win", None, None),
        P("cell", "win", None, None),
        P("cell", "win", None),
    )
    return jax.shard_map(
        local,
        mesh=mesh,
        in_specs=placed,
        out_specs=(P(("ens", "win"), "cell"), P(("ens", "cell"), None)),
        check_vma=False,
    )
```

```python
import jax
import jax.numpy as jnp
from jax import lax
from jax.sharding import PartitionSpec as P

CB = 64
OB = 64
CBLK_DEV = 8
WIN_DEV = 8
OBLK_DEV = 8

HI = lax.Precision.HIGHEST


def others(value, axis, size):
    return [
        lax.ppermute(value, axis, [(i, (i + k) % size) for i in range(size)])
        for k in range(1, size)
    ]


def make_local(cells, wins):
    def local(prior_flux, observed, obs_weight, footprint, flux_slot, obs_slot, slot_count):
        owners = footprint.shape[2]
        capacity = footprint.shape[3]
        slots = owners * capacity
        blocks = WIN_DEV * CBLK_DEV
        me = lax.axis_index("cell")
        live = (
            lax.broadcasted_iota(jnp.int32, (owners, capacity), 1)
            < slot_count.reshape(owners, 1)
        ).astype(jnp.float32)
        matrices = footprint.reshape(owners, capacity, OB, CB)
        obs_pick = (
            obs_slot.reshape(slots, 1) == lax.broadcasted_iota(jnp.int32, (1, OBLK_DEV), 1)
        ).astype(jnp.float32) * live.reshape(slots, 1)
        owner_of = lax.broadcasted_iota(jnp.int32, (owners, capacity), 0)
        my_target = (owner_of * blocks + flux_slot.reshape(owners, capacity)).reshape(slots)

        def forward_part(selected):
            value = jnp.einsum("sij,sj->si", matrices.reshape(slots, OB, CB), selected, precision=HI)
            return jnp.dot(obs_pick.T, value, precision=HI).reshape(1, OBLK_DEV * OB)

        def adjoint(departure):
            picked = jnp.dot(obs_pick, departure.reshape(OBLK_DEV, OB), precision=HI)
            return jnp.einsum("sij,si->sj", matrices.reshape(slots, OB, CB), picked, precision=HI)

        flux_parts = [prior_flux] + others(prior_flux, "cell", cells)
        targets = jnp.concatenate([my_target] + others(my_target, "cell", cells))
        flux = jnp.concatenate([part.reshape(blocks, CB) for part in flux_parts])
        ring_target = (
            lax.rem(me - my_target // blocks + cells, cells) * blocks + my_target % blocks
        )
        pick = (
            ring_target[:, None]
            == lax.broadcasted_iota(jnp.int32, (1, cells * blocks), 1)
        ).astype(jnp.float32)
        selected0 = jnp.dot(pick, flux, precision=HI)
        part0 = forward_part(selected0)
        model0 = lax.psum(part0, "win")
        departure0 = obs_weight * (model0 - observed)
        returned0 = adjoint(departure0)
        all_returned = jnp.concatenate([returned0] + others(returned0, "cell", cells))
        match = (my_target[:, None] == targets[None, :]).astype(jnp.float32)
        selected1 = selected0 - 0.5 * jnp.dot(match, all_returned, precision=HI)
        part1 = forward_part(selected1)
        model1 = sum(others(part1, "win", wins), part1)
        departure1 = obs_weight * (model1 - observed)
        returned1 = adjoint(-0.25 * departure0 - 0.5 * departure1).reshape(owners, capacity, CB)
        pieces = [lax.dynamic_index_in_dim(returned1, me, 0, keepdims=False)]
        for k in range(1, cells):
            piece = lax.dynamic_index_in_dim(returned1, lax.rem(me + k, cells), 0, keepdims=False)
            pieces.append(
                lax.ppermute(piece, "cell", [(i, (i + k) % cells) for i in range(cells)])
            )
        mine = lax.dynamic_index_in_dim(
            targets.reshape(cells, owners, capacity), me, 1, keepdims=False
        ).reshape(cells * capacity) - me * blocks
        scatter = (
            mine[None, :] == lax.broadcasted_iota(jnp.int32, (blocks, 1), 0)
        ).astype(jnp.float32)
        increment = jnp.dot(scatter, jnp.concatenate(pieces), precision=HI)
        return increment.reshape(WIN_DEV, CBLK_DEV * CB), departure1

    return local


def solution(mesh):
    placed = (
        P(("ens", "win"), "cell"),
        P(("ens", "cell"), None),
        P(("ens", "cell"), None),
        P("cell", "win", None, None, None),
        P("cell", "win", None, None),
        P("cell", "win", None, None),
        P("cell", "win", None),
    )
    return jax.shard_map(
        make_local(mesh.shape["cell"], mesh.shape["win"]),
        mesh=mesh,
        in_specs=placed,
        out_specs=(P(("ens", "win"), "cell"), P(("ens", "cell"), None)),
        check_vma=False,
    )
```

```python
import functools
import jax
import jax.numpy as jnp
from jax import lax
from jax.experimental import pallas as pl
from jax.experimental.pallas import tpu as pltpu
from jax.sharding import PartitionSpec as P

CB = 64
OB = 64
CBLK_DEV = 8
WIN_DEV = 8
OBLK_DEV = 8
BLOCKS = WIN_DEV * CBLK_DEV
LANES = 128
TILES = OB * CB // LANES

F32 = jnp.float32
BF16 = jnp.bfloat16
VMEM = pl.BlockSpec(memory_space=pltpu.VMEM)


def iota(shape, dim):
    return lax.broadcasted_iota(jnp.int32, shape, dim)


def one_hot(where):
    return jnp.where(where, 1.0, 0.0).astype(BF16)


def three(value):
    first = value.astype(BF16)
    rest = value - first.astype(F32)
    second = rest.astype(BF16)
    third = (rest - second.astype(F32)).astype(BF16)
    return [first, second, third]


def pick_rows(pick3, value):
    return jnp.dot(pick3, jnp.concatenate(three(value), axis=0), preferred_element_type=F32)


def swap(value, distance):
    return jnp.take_along_axis(
        value, iota(value.shape, 1) ^ distance, axis=1, mode="promise_in_bounds"
    )


def half_swap(value):
    return pltpu.roll(value, LANES // 2, 1)


def low(shape):
    return iota(shape, 1) < LANES // 2


def tree_sum(parts):
    parts = list(parts)
    while len(parts) > 1:
        parts = [sum(parts[i + 1 : i + 2], parts[i]) for i in range(0, len(parts), 2)]
    return parts[0]


def spread_obs(row):
    out = jnp.zeros((OBLK_DEV, LANES), F32)
    block = iota((OBLK_DEV, LANES), 0)
    lower = low((OBLK_DEV, LANES))
    for t in range(OBLK_DEV // 2):
        tile = jnp.broadcast_to(row[:, LANES * t : LANES * (t + 1)], (OBLK_DEV, LANES))
        turned = half_swap(tile)
        out = jnp.where(block == 2 * t, jnp.where(lower, tile, turned), out)
        out = jnp.where(block == 2 * t + 1, jnp.where(lower, turned, tile), out)
    return out


def forward_tree(h_ref, owner, x, bits, base):
    if bits == 0:
        return h_ref[0, 0, owner, :, LANES * base : LANES * (base + 1)] * x
    a = forward_tree(h_ref, owner, x, bits - 1, base)
    b = forward_tree(h_ref, owner, x, bits - 1, base + 2 ** (bits - 1))
    distance = 2**bits
    clear = (iota(a.shape, 1) & distance) == 0
    return jnp.where(clear, a, b) + swap(jnp.where(clear, b, a), distance)


def for_owners(owners, body):
    lax.fori_loop(0, owners, lambda o, c: (body(o), c)[1], 0, unroll=owners <= 4)


def forward(h_ref, pick_obs, x_scr, value_scr):
    owners, capacity = h_ref.shape[2], h_ref.shape[3]

    def body(o):
        rows = pl.ds(pl.multiple_of(o * capacity, capacity), capacity)
        value_scr[rows, :] = forward_tree(h_ref, o, x_scr[rows, :], 5, 0)

    for_owners(owners, body)
    m = pick_rows(pick_obs, value_scr[...])[:OBLK_DEV]
    m = m + swap(m, 1)
    even = (iota(m.shape, 1) & 1) == 0
    return jnp.where(even == low(m.shape), m, half_swap(m))


def adjoint(h_ref, slot_obs, d, picked_scr, store):
    owners, capacity = h_ref.shape[2], h_ref.shape[3]
    picked_scr[...] = pick_rows(slot_obs, d)

    def body(o):
        rows = pl.ds(pl.multiple_of(o * capacity, capacity), capacity)
        picked = picked_scr[rows, :]
        upper = jnp.where(low(picked.shape), 0, 1)
        total = None
        for t in range(TILES):
            spread = jnp.take_along_axis(picked, upper + 2 * t, axis=1, mode="promise_in_bounds")
            term = h_ref[0, 0, o, :, LANES * t : LANES * (t + 1)] * spread
            total = term if total is None else total + term
        total = total + half_swap(total)
        pair = total[: capacity // 2], total[capacity // 2 :]
        store(o, jnp.where(low(pair[0].shape), *pair))

    for_owners(owners, body)


def prepare(
    fslot_ref, oslot_ref, count_ref, observed_ref, weight_ref,
    pick_flux_ref, target_ref, slot_obs_ref, pick_obs_ref, index_ref, observed_out, weight_out,
):
    me = lax.axis_index("cell")
    owners, capacity = fslot_ref.shape[2:]
    slots = owners * capacity
    eye = iota((capacity, capacity), 0) == iota((capacity, capacity), 1)

    def column(ref):
        return jnp.concatenate(
            [
                jnp.sum(
                    jnp.where(eye, jnp.broadcast_to(ref[0, 0, o : o + 1, :], eye.shape), 0),
                    axis=1,
                    keepdims=True,
                )
                for o in range(owners)
            ],
            axis=0,
        )

    fslot, oslot = column(fslot_ref), column(oslot_ref)
    counts = jnp.concatenate(
        [
            jnp.broadcast_to(count_ref[0, 0:1, o : o + 1], (capacity, 1))
            for o in range(owners)
        ],
        axis=0,
    )
    slot = iota((slots, 1), 0)
    owner = slot // capacity
    live = (slot - owner * capacity) < counts
    oslot = jnp.where(live, oslot, OBLK_DEV)
    target = owner * BLOCKS + fslot
    target_ref[...] = jnp.broadcast_to(target.astype(F32), target_ref.shape)

    depth = owners * BLOCKS // 2
    row = (owner ^ me) * (BLOCKS // 2) + ((fslot & 7) >> 1) * WIN_DEV + (fslot >> 3)
    pick_flux_ref[...] = one_hot(iota((slots, 3 * depth), 1) % depth == row)
    slot_obs_ref[...] = one_hot((iota((slots, 3 * OBLK_DEV), 1) % OBLK_DEV) == oslot)

    eye3 = iota((slots, 3 * slots), 1) % slots == iota((slots, 3 * slots), 0)
    obs_row = jnp.sum(jnp.where(eye3, oslot, 0), axis=0, keepdims=True)
    pick_obs_ref[...] = one_hot(iota((16, 3 * slots), 0) == obs_row) * one_hot(
        iota((16, 3 * slots), 0) < OBLK_DEV
    )

    half = slots // 2
    count = max(1, half // LANES)
    index_ref[...] = jnp.zeros(index_ref.shape, F32)
    for part in range(2):
        for q in range(count):
            r = (iota((slots, LANES), 1) + LANES * q) % half
            at = (r // (capacity // 2)) * capacity + r % (capacity // 2) + part * (capacity // 2)
            index_ref[pl.ds(part * count + q, 1), :] = jnp.sum(
                jnp.where(iota((slots, LANES), 0) == at, target.astype(F32), 0.0),
                axis=0,
                keepdims=True,
            )
    observed_out[...] = spread_obs(observed_ref[...])
    weight_out[...] = spread_obs(weight_ref[...])


def first_model(parts, *refs):
    x_parts = refs[:parts]
    h_ref, pick_flux_ref, target_ref, pick_obs_ref, m_ref, x_ref, value_scr = refs[parts:]
    flux = jnp.concatenate(
        [
            ref[:, LANES * t : LANES * (t + 1)]
            for ref in x_parts
            for t in range(CBLK_DEV // 2)
        ],
        axis=0,
    )
    pair = pick_rows(pick_flux_ref[...], flux)
    odd = (target_ref[...].astype(jnp.int32) & 1) == 1
    x_ref[...] = jnp.where(odd != low(pair.shape), pair, half_swap(pair))
    m_ref[...] = forward(h_ref, pick_obs_ref[...], x_ref, value_scr)


def first_adjoint(parts, *refs):
    m_parts = refs[:parts]
    observed_ref, weight_ref, slot_obs_ref, index_ref, h_ref, message_ref, d_ref, picked_scr = refs[parts:]
    d = weight_ref[...] * (tree_sum([m[...] for m in m_parts]) - observed_ref[...])
    d_ref[...] = d
    rows = h_ref.shape[3] // 2
    half = h_ref.shape[2] * rows

    def store(o, block):
        message_ref[pl.ds(pl.multiple_of(o * rows, rows), rows), :] = block

    adjoint(h_ref, slot_obs_ref[...], d, picked_scr, store)
    message_ref[half:, :] = index_ref[...]


def second_model(parts, *refs):
    messages = refs[:parts]
    target_ref, x_ref, h_ref, pick_obs_ref, m_ref, next_scr, value_scr = refs[parts:]
    slots = target_ref.shape[0]
    half = slots // 2
    count = max(1, half // LANES)
    group = max(1, min(parts, LANES // half))
    total = None
    for first in range(0, parts, group):
        members = messages[first : first + group]
        picks = []
        for part in range(2):
            rows = []
            for q in range(count):
                at = half + part * count + q
                row = members[0][at : at + 1, :]
                for k in range(1, group):
                    row = jnp.where(iota((1, LANES), 1) // half == k, members[k][at : at + 1, :], row)
                rows.append(one_hot(target_ref[...] == row))
            picks.append(jnp.concatenate(rows, axis=1)[:, : group * half])
        pick = jnp.concatenate(picks, axis=0)
        values = jnp.concatenate([ref[:half, :] for ref in members], axis=0)
        found = pick_rows(jnp.concatenate([pick] * 3, axis=1), values)
        total = found if total is None else total + found
    change = jnp.where(low((slots, LANES)), total[:slots], total[slots:])
    next_scr[...] = x_ref[...] - 0.5 * (change + half_swap(change))
    m_ref[...] = forward(h_ref, pick_obs_ref[...], next_scr, value_scr)


def second_adjoint(parts, owners, *refs):
    m_parts = refs[:parts]
    observed_ref, weight_ref, d_ref, slot_obs_ref, h_ref = refs[parts : parts + 5]
    outs = refs[parts + 5 : parts + 5 + owners]
    departure_ref, picked_scr, block_scr = refs[parts + 5 + owners :]
    me = lax.axis_index("cell")
    d = weight_ref[...] * (tree_sum([m[...] for m in m_parts]) - observed_ref[...])
    for t in range(OBLK_DEV // 2):
        departure_ref[:, LANES * t : LANES * (t + 1)] = jnp.where(
            low((1, LANES)), d[2 * t : 2 * t + 1], d[2 * t + 1 : 2 * t + 2]
        )

    def store(o, block):
        block_scr[o] = block

    adjoint(h_ref, slot_obs_ref[...], -0.25 * d_ref[...] - 0.5 * d, picked_scr, store)
    for k in range(owners):
        outs[k][...] = block_scr[me ^ k]


def gather_increment(parts, *refs):
    values, messages, out_ref = refs[:parts], refs[parts : 2 * parts], refs[2 * parts]
    me = lax.axis_index("cell")
    rows = values[0].shape[0]
    half = parts * rows
    count = max(1, half // LANES)
    place = me * rows
    lane = iota((1, LANES), 1)
    row = iota((BLOCKS, LANES), 0)
    block = me * BLOCKS + (row % WIN_DEV) * CBLK_DEV + 2 * ((row // WIN_DEV) % 4) + row // (BLOCKS // 2)
    block = block.astype(F32)
    picks = []
    for part in range(2):
        tiles = []
        for first in range(0, half, LANES):
            index = jnp.zeros((1, LANES), F32)
            for k in range(first // rows, min(parts, (first + LANES) // rows)):
                turned = pltpu.roll(
                    messages[k][half:, :], lax.rem(k * rows - place % LANES + 2 * LANES - first, LANES), 1
                )
                chosen = turned[part * count : part * count + 1]
                for q in range(1, count):
                    chosen = jnp.where(
                        place // LANES == q, turned[part * count + q : part * count + q + 1], chosen
                    )
                index = jnp.where((lane // rows) % parts == k - first // rows, chosen, index)
            tiles.append(one_hot(block == index))
        picks.append(jnp.concatenate(tiles, axis=1))
    pick = jnp.concatenate(picks, axis=0)
    terms = three(jnp.concatenate([ref[...] for ref in values], axis=0))
    if 3 * half <= LANES:
        terms.append(jnp.zeros((LANES - 3 * half, LANES), BF16))
    else:
        pick = jnp.concatenate([pick[:, :half]] * 3, axis=1)
    found = jnp.dot(pick, jnp.concatenate(terms, axis=0), preferred_element_type=F32)
    found = jnp.where(low((BLOCKS, LANES)), found[:BLOCKS], found[BLOCKS:])
    found = found + half_swap(found)
    for t in range(CBLK_DEV // 2):
        even = found[WIN_DEV * t : WIN_DEV * (t + 1)]
        odd = found[BLOCKS // 2 + WIN_DEV * t : BLOCKS // 2 + WIN_DEV * (t + 1)]
        out_ref[:, LANES * t : LANES * (t + 1)] = jnp.where(low(even.shape), even, odd)


def exchange(value, axis, size):
    return [value] + [send(value, axis, size, k) for k in range(size - 1, 0, -1)][::-1]


def send(value, axis, size, k):
    return lax.ppermute(value, axis, [(i, i ^ k) for i in range(size)])


def make_local(cells, wins):
    def local(prior_flux, observed, obs_weight, footprint, flux_slot, obs_slot, slot_count):
        owners, capacity = footprint.shape[2:4]
        slots = owners * capacity
        half = slots // 2
        index_rows = -(-2 * max(1, half // LANES) // 8) * 8
        params = pltpu.CompilerParams(vmem_limit_bytes=4 * footprint.size * 4 + 8 * 2**20)

        def call(body, outs, ins, scratch=()):
            return pl.pallas_call(
                body,
                out_shape=[jax.ShapeDtypeStruct(s, t) for s, t in outs],
                in_specs=[VMEM] * len(ins),
                out_specs=[VMEM] * len(outs),
                scratch_shapes=[pltpu.VMEM(s, F32) for s in scratch],
                compiler_params=params,
            )(*ins)

        obs_tile = ((OBLK_DEV, LANES), F32)
        slot_tile = ((slots, LANES), F32)
        flux_parts = exchange(prior_flux, "cell", cells)
        pick_flux, target, slot_obs, pick_obs, index, observed_t, weight_t = call(
            prepare,
            [
                ((slots, 3 * owners * BLOCKS // 2), BF16),
                slot_tile,
                ((slots, 3 * OBLK_DEV), BF16),
                ((16, 3 * slots), BF16),
                ((index_rows, LANES), F32),
                obs_tile,
                obs_tile,
            ],
            (flux_slot, obs_slot, slot_count, observed, obs_weight),
        )
        m0, x0 = call(
            functools.partial(first_model, cells),
            [obs_tile, slot_tile],
            (*flux_parts, footprint, pick_flux, target, pick_obs),
            [slot_tile[0]],
        )
        message, d0 = call(
            functools.partial(first_adjoint, wins),
            [((half + index_rows, LANES), F32), obs_tile],
            (*exchange(m0, "win", wins), observed_t, weight_t, slot_obs, index, footprint),
            [slot_tile[0]],
        )
        messages = exchange(message, "cell", cells)
        (m1,) = call(
            functools.partial(second_model, cells),
            [obs_tile],
            (*messages, target, x0, footprint, pick_obs),
            [slot_tile[0], slot_tile[0]],
        )
        *blocks, departure = call(
            functools.partial(second_adjoint, wins, owners),
            [((capacity // 2, LANES), F32)] * owners + [((1, OBLK_DEV * OB), F32)],
            (*exchange(m1, "win", wins), observed_t, weight_t, d0, slot_obs, footprint),
            [slot_tile[0], (owners, capacity // 2, LANES)],
        )
        arrived = [send(blocks[k], "cell", cells, k) for k in range(cells - 1, 0, -1)][::-1]
        (increment,) = call(
            functools.partial(gather_increment, cells),
            [((WIN_DEV, CBLK_DEV * CB), F32)],
            (blocks[0], *arrived, *messages),
        )
        return increment, departure

    return local


def solution(mesh):
    placed = (
        P(("ens", "win"), "cell"),
        P(("ens", "cell"), None),
        P(("ens", "cell"), None),
        P("cell", "win", None, None, None),
        P("cell", "win", None, None),
        P("cell", "win", None, None),
        P("cell", "win", None),
    )
    return jax.shard_map(
        make_local(mesh.shape["cell"], mesh.shape["win"]),
        mesh=mesh,
        in_specs=placed,
        out_specs=(P(("ens", "win"), "cell"), P(("ens", "cell"), None)),
        check_vma=False,
    )
```

```python
import functools
import jax
import jax.numpy as jnp
from jax import lax
from jax.experimental import pallas as pl
from jax.experimental.pallas import tpu as pltpu
from jax.sharding import PartitionSpec as P

CB = 64
OB = 64
CBLK_DEV = 8
WIN_DEV = 8
OBLK_DEV = 8
BLOCKS = WIN_DEV * CBLK_DEV
LANES = 128
TILES = OB * CB // LANES

F32 = jnp.float32
BF16 = jnp.bfloat16
VMEM = pl.BlockSpec(memory_space=pltpu.VMEM)


def iota(shape, dim):
    return lax.broadcasted_iota(jnp.int32, shape, dim)


def one_hot(where):
    return jnp.where(where, 1.0, 0.0).astype(BF16)


def three(value):
    first = value.astype(BF16)
    rest = value - first.astype(F32)
    second = rest.astype(BF16)
    third = (rest - second.astype(F32)).astype(BF16)
    return [first, second, third]


def pick_rows(pick3, value):
    return jnp.dot(pick3, jnp.concatenate(three(value), axis=0), preferred_element_type=F32)


def swap(value, distance):
    return jnp.take_along_axis(
        value, iota(value.shape, 1) ^ distance, axis=1, mode="promise_in_bounds"
    )


def half_swap(value):
    return pltpu.roll(value, LANES // 2, 1)


def low(shape):
    return iota(shape, 1) < LANES // 2


def entries(refs):
    return [(ref, i) for ref in refs for i in range(ref.shape[0])]


def spread_obs(row):
    out = jnp.zeros((OBLK_DEV, LANES), F32)
    block = iota((OBLK_DEV, LANES), 0)
    lower = low((OBLK_DEV, LANES))
    for t in range(OBLK_DEV // 2):
        tile = jnp.broadcast_to(row[:, LANES * t : LANES * (t + 1)], (OBLK_DEV, LANES))
        turned = half_swap(tile)
        out = jnp.where(block == 2 * t, jnp.where(lower, tile, turned), out)
        out = jnp.where(block == 2 * t + 1, jnp.where(lower, turned, tile), out)
    return out


def forward_tree(h_ref, owner, x, bits, base):
    if bits == 0:
        return h_ref[0, 0, owner, :, LANES * base : LANES * (base + 1)] * x
    a = forward_tree(h_ref, owner, x, bits - 1, base)
    b = forward_tree(h_ref, owner, x, bits - 1, base + 2 ** (bits - 1))
    distance = 2**bits
    clear = (iota(a.shape, 1) & distance) == 0
    return jnp.where(clear, a, b) + swap(jnp.where(clear, b, a), distance)


def for_owners(owners, body):
    lax.fori_loop(0, owners, lambda o, c: (body(o), c)[1], 0, unroll=owners <= 4)


def forward(h_ref, pick_obs, x_scr, value_scr):
    owners, capacity = h_ref.shape[2], h_ref.shape[3]

    def body(o):
        rows = pl.ds(pl.multiple_of(o * capacity, capacity), capacity)
        value_scr[rows, :] = forward_tree(h_ref, o, x_scr[rows, :], 5, 0)

    for_owners(owners, body)
    m = pick_rows(pick_obs, value_scr[...])[:OBLK_DEV]
    m = m + swap(m, 1)
    even = (iota(m.shape, 1) & 1) == 0
    return jnp.where(even == low(m.shape), m, half_swap(m))


def adjoint(h_ref, slot_obs, d, picked_scr, store):
    owners, capacity = h_ref.shape[2], h_ref.shape[3]
    picked_scr[...] = pick_rows(slot_obs, d)

    def body(o):
        rows = pl.ds(pl.multiple_of(o * capacity, capacity), capacity)
        picked = picked_scr[rows, :]
        upper = jnp.where(low(picked.shape), 0, 1)
        total = None
        for t in range(TILES):
            spread = jnp.take_along_axis(picked, upper + 2 * t, axis=1, mode="promise_in_bounds")
            term = h_ref[0, 0, o, :, LANES * t : LANES * (t + 1)] * spread
            total = term if total is None else total + term
        total = total + half_swap(total)
        pair = total[: capacity // 2], total[capacity // 2 :]
        store(o, jnp.where(low(pair[0].shape), *pair))

    for_owners(owners, body)


def prepare(
    fslot_hbm, oslot_hbm, count_hbm, observed_hbm, weight_hbm, flux_hbm, h_hbm,
    pick_flux_ref, target_ref, slot_obs_ref, pick_obs_ref, index_ref, observed_out, weight_out, flux_ref, h_ref,
    fslot_ref, oslot_ref, count_ref, observed_ref, weight_ref, sems, h_sems,
):
    me = lax.axis_index("cell")
    owners, capacity = fslot_ref.shape[2:]
    pairs = (
        (fslot_hbm, fslot_ref),
        (oslot_hbm, oslot_ref),
        (count_hbm, count_ref),
        (observed_hbm, observed_ref),
        (weight_hbm, weight_ref),
        (flux_hbm, flux_ref),
    )
    small = [pltpu.make_async_copy(src, dst, sems.at[i]) for i, (src, dst) in enumerate(pairs)]
    large = [
        pltpu.make_async_copy(h_hbm.at[:, :, o], h_ref.at[:, :, o], h_sems.at[o])
        for o in range(owners)
    ]
    for copy in small + large:
        copy.start()
    for copy in small:
        copy.wait()
    slots = owners * capacity
    eye = iota((capacity, capacity), 0) == iota((capacity, capacity), 1)

    def column(ref):
        return jnp.concatenate(
            [
                jnp.sum(
                    jnp.where(eye, jnp.broadcast_to(ref[0, 0, o : o + 1, :], eye.shape), 0),
                    axis=1,
                    keepdims=True,
                )
                for o in range(owners)
            ],
            axis=0,
        )

    fslot, oslot = column(fslot_ref), column(oslot_ref)
    counts = jnp.concatenate(
        [
            jnp.broadcast_to(count_ref[0, 0:1, o : o + 1], (capacity, 1))
            for o in range(owners)
        ],
        axis=0,
    )
    slot = iota((slots, 1), 0)
    owner = slot // capacity
    live = (slot - owner * capacity) < counts
    oslot = jnp.where(live, oslot, OBLK_DEV)
    target = owner * BLOCKS + fslot
    target_ref[...] = jnp.broadcast_to(target.astype(F32), target_ref.shape)

    depth = owners * BLOCKS // 2
    row = (owner ^ me) * (BLOCKS // 2) + ((fslot & 7) >> 1) * WIN_DEV + (fslot >> 3)
    pick_flux_ref[...] = one_hot(iota((slots, 3 * depth), 1) % depth == row)
    slot_obs_ref[...] = one_hot((iota((slots, 3 * OBLK_DEV), 1) % OBLK_DEV) == oslot)

    eye3 = iota((slots, 3 * slots), 1) % slots == iota((slots, 3 * slots), 0)
    obs_row = jnp.sum(jnp.where(eye3, oslot, 0), axis=0, keepdims=True)
    pick_obs_ref[...] = one_hot(iota((16, 3 * slots), 0) == obs_row) * one_hot(
        iota((16, 3 * slots), 0) < OBLK_DEV
    )

    half = slots // 2
    count = max(1, half // LANES)
    index_ref[...] = jnp.zeros(index_ref.shape, F32)
    for part in range(2):
        for q in range(count):
            r = (iota((slots, LANES), 1) + LANES * q) % half
            at = (r // (capacity // 2)) * capacity + r % (capacity // 2) + part * (capacity // 2)
            index_ref[pl.ds(part * count + q, 1), :] = jnp.sum(
                jnp.where(iota((slots, LANES), 0) == at, target.astype(F32), 0.0),
                axis=0,
                keepdims=True,
            )
    observed_out[...] = spread_obs(observed_ref[...])
    weight_out[...] = spread_obs(weight_ref[...])
    for copy in large:
        copy.wait()


def first_model(parts, *refs):
    h_ref, pick_flux_ref, target_ref, pick_obs_ref, m_ref, x_ref, value_scr = refs[parts:]
    flux = jnp.concatenate(
        [
            ref[i, :, LANES * t : LANES * (t + 1)]
            for ref, i in entries(refs[:parts])
            for t in range(CBLK_DEV // 2)
        ],
        axis=0,
    )
    pair = pick_rows(pick_flux_ref[...], flux)
    odd = (target_ref[...].astype(jnp.int32) & 1) == 1
    x_ref[...] = jnp.where(odd != low(pair.shape), pair, half_swap(pair))
    m_ref[...] = forward(h_ref, pick_obs_ref[...], x_ref, value_scr)


def first_adjoint(
    m_ref, other_ref, observed_ref, weight_ref, slot_obs_ref, index_ref, h_ref, message_ref, d_ref, picked_scr
):
    d = weight_ref[...] * (m_ref[...] + other_ref[...] - observed_ref[...])
    d_ref[...] = d
    rows = h_ref.shape[3] // 2
    half = h_ref.shape[2] * rows

    def store(o, block):
        message_ref[0, pl.ds(pl.multiple_of(o * rows, rows), rows), :] = block

    adjoint(h_ref, slot_obs_ref[...], d, picked_scr, store)
    message_ref[0, half:, :] = index_ref[...]


def second_model(parts, *refs):
    messages = entries(refs[:parts])
    cells = len(messages)
    target_ref, x_ref, h_ref, pick_obs_ref, m_ref, next_scr, value_scr = refs[parts:]
    slots = target_ref.shape[0]
    half = slots // 2
    count = max(1, half // LANES)
    group = max(1, min(cells, LANES // half))
    total = None
    for first in range(0, cells, group):
        members = messages[first : first + group]
        picks = []
        for part in range(2):
            rows = []
            for q in range(count):
                at = half + part * count + q
                row = jnp.zeros((1, LANES), F32)
                for k, (ref, i) in enumerate(members):
                    row = jnp.where(iota((1, LANES), 1) // half % group == k, ref[i, at : at + 1, :], row)
                rows.append(one_hot(target_ref[...] == row))
            picks.append(jnp.concatenate(rows, axis=1)[:, : group * half])
        pick = jnp.concatenate(picks, axis=0)
        values = jnp.concatenate([ref[i, :half, :] for ref, i in members], axis=0)
        found = pick_rows(jnp.concatenate([pick] * 3, axis=1), values)
        total = found if total is None else total + found
    change = jnp.where(low((slots, LANES)), total[:slots], total[slots:])
    next_scr[...] = x_ref[...] - 0.5 * (change + half_swap(change))
    m_ref[...] = forward(h_ref, pick_obs_ref[...], next_scr, value_scr)


def second_adjoint(
    m_ref, other_ref, observed_ref, weight_ref, first_ref, slot_obs_ref, h_ref,
    near_ref, far_ref, d_ref, picked_scr, block_scr,
):
    me = lax.axis_index("cell")
    owners = h_ref.shape[2]
    d = weight_ref[...] * (m_ref[...] + other_ref[...] - observed_ref[...])
    d_ref[...] = d

    def store(o, block):
        block_scr[o] = block

    adjoint(h_ref, slot_obs_ref[...], -0.25 * first_ref[...] - 0.5 * d, picked_scr, store)
    for k in range(owners // 2):
        near_ref[k] = block_scr[me ^ k]
        far_ref[k] = block_scr[me ^ (k + owners // 2)]


def prepare_increment(parts, rows, *refs):
    d_ref, pick_ref, departure_ref = refs[parts:]
    messages = entries(refs[:parts])
    cells = len(messages)
    me = lax.axis_index("cell")
    half = cells * rows
    count = max(1, half // LANES)
    place = me * rows
    lane = iota((1, LANES), 1)
    row = iota((BLOCKS, LANES), 0)
    block = me * BLOCKS + (row % WIN_DEV) * CBLK_DEV + 2 * ((row // WIN_DEV) % 4) + row // (BLOCKS // 2)
    block = block.astype(F32)
    for part in range(2):
        for first in range(0, half, LANES):
            index = jnp.zeros((1, LANES), F32)
            for k in range(first // rows, min(cells, (first + LANES) // rows)):
                ref, i = messages[k]
                turned = pltpu.roll(
                    ref[i, half:, :], lax.rem(k * rows - place % LANES + 2 * LANES - first, LANES), 1
                )
                chosen = turned[part * count : part * count + 1]
                for q in range(1, count):
                    chosen = jnp.where(
                        place // LANES == q, turned[part * count + q : part * count + q + 1], chosen
                    )
                index = jnp.where((lane // rows) % cells == k - first // rows, chosen, index)
            pick_ref[BLOCKS * part : BLOCKS * (part + 1), first : first + LANES] = one_hot(block == index)
    for t in range(OBLK_DEV // 2):
        departure_ref[:, LANES * t : LANES * (t + 1)] = jnp.where(
            low((1, LANES)), d_ref[2 * t : 2 * t + 1, :], d_ref[2 * t + 1 : 2 * t + 2, :]
        )


def gather_increment(places, *refs):
    *arrays, pick_ref, out_ref = refs
    values = jnp.concatenate([arrays[n][i] for n, i in places], axis=0)
    half = values.shape[0]
    terms = three(values)
    pick = pick_ref[...]
    if 3 * half <= LANES:
        terms.append(jnp.zeros((LANES - 3 * half, LANES), BF16))
    else:
        pick = jnp.concatenate([pick[:, :half]] * 3, axis=1)
    found = jnp.dot(pick, jnp.concatenate(terms, axis=0), preferred_element_type=F32)
    found = jnp.where(low((BLOCKS, LANES)), found[:BLOCKS], found[BLOCKS:])
    found = found + half_swap(found)
    for t in range(CBLK_DEV // 2):
        even = found[WIN_DEV * t : WIN_DEV * (t + 1)]
        odd = found[BLOCKS // 2 + WIN_DEV * t : BLOCKS // 2 + WIN_DEV * (t + 1)]
        out_ref[:, LANES * t : LANES * (t + 1)] = jnp.where(low(even.shape), even, odd)


def send(value, axis, size, k):
    return lax.ppermute(value, axis, [(i, i ^ k) for i in range(size)])


def gather_doubling(own, first, axis, size):
    held, arrived = own, send(first, axis, size, 1)
    distance = 2
    while distance < size:
        held = jnp.concatenate([held, arrived], axis=0)
        arrived = send(held, axis, size, distance)
        distance *= 2
    return held, arrived


def sum_doubling(value, axis, size):
    distance = 1
    while 2 * distance < size:
        value = value + send(value, axis, size, distance)
        distance *= 2
    return value, send(value, axis, size, distance)


def scatter_halving(near, far, axis, size):
    arrays = [near, far]
    place = {(0, e): divmod(e, size // 2) for e in range(size)}
    sources = [0]
    distance = size // 2
    out = far
    while distance:
        arrays.append(send(out, axis, size, distance))
        moved = [(s ^ distance, e) for s in sources for e in range(distance)]
        for n, key in enumerate(moved):
            place[key] = (len(arrays) - 1, n)
        sources = sources + [s ^ distance for s in sources]
        distance //= 2
        spots = [place[s, e] for s in sources for e in range(distance, 2 * distance)]
        if distance:
            out = jnp.concatenate([arrays[n][i : i + 1] for n, i in spots], axis=0)
    return arrays, [place[e, 0] for e in range(size)]


def make_local(cells, wins):
    def local(prior_flux, observed, obs_weight, footprint, flux_slot, obs_slot, slot_count):
        owners, capacity = footprint.shape[2:4]
        slots = owners * capacity
        half = slots // 2
        index_rows = -(-2 * max(1, half // LANES) // 8) * 8
        params = pltpu.CompilerParams(vmem_limit_bytes=4 * footprint.size * 4 + 8 * 2**20)
        hbm = pl.BlockSpec(memory_space=pltpu.HBM)

        def call(body, outs, ins, scratch=(), space=VMEM):
            if space is hbm:
                ins = [pltpu.with_memory_space_constraint(value, pltpu.HBM) for value in ins]
                outs_at = [pltpu.VMEM(s, t) for s, t in outs]
            else:
                outs_at = [jax.ShapeDtypeStruct(s, t) for s, t in outs]
            return pl.pallas_call(
                body,
                out_shape=outs_at,
                in_specs=[space] * len(ins),
                out_specs=[VMEM] * len(outs),
                scratch_shapes=list(scratch),
                compiler_params=params,
            )(*ins)

        def like(value):
            return (value.shape, value.dtype)

        obs_tile = ((OBLK_DEV, LANES), F32)
        slot_tile = ((slots, LANES), F32)
        slot_scratch = pltpu.VMEM(*slot_tile)
        block_pair = ((owners // 2, capacity // 2, LANES), F32)
        flux_in = prior_flux[None]
        small = (flux_slot, obs_slot, slot_count, observed, obs_weight)
        pick_flux, target, slot_obs, pick_obs, index, observed_t, weight_t, flux, matrices = call(
            prepare,
            [
                ((slots, 3 * owners * BLOCKS // 2), BF16),
                slot_tile,
                ((slots, 3 * OBLK_DEV), BF16),
                ((16, 3 * slots), BF16),
                ((index_rows, LANES), F32),
                obs_tile,
                obs_tile,
                like(flux_in),
                like(footprint),
            ],
            (*small, flux_in, footprint),
            [
                *(pltpu.VMEM(*like(value)) for value in small),
                pltpu.SemaphoreType.DMA((len(small) + 1,)),
                pltpu.SemaphoreType.DMA((owners,)),
            ],
            hbm,
        )
        fluxes = gather_doubling(flux, flux_in, "cell", cells)
        m0, x0 = call(
            functools.partial(first_model, len(fluxes)),
            [obs_tile, slot_tile],
            (*fluxes, matrices, pick_flux, target, pick_obs),
            [slot_scratch],
        )
        message, d0 = call(
            first_adjoint,
            [((1, half + index_rows, LANES), F32), obs_tile],
            (*sum_doubling(m0, "win", wins), observed_t, weight_t, slot_obs, index, matrices),
            [slot_scratch],
        )
        messages = gather_doubling(message, message, "cell", cells)
        (m1,) = call(
            functools.partial(second_model, len(messages)),
            [obs_tile],
            (*messages, target, x0, matrices, pick_obs),
            [slot_scratch, slot_scratch],
        )
        near, far, d1 = call(
            second_adjoint,
            [block_pair, block_pair, obs_tile],
            (*sum_doubling(m1, "win", wins), observed_t, weight_t, d0, slot_obs, matrices),
            [slot_scratch, pltpu.VMEM((owners, capacity // 2, LANES), F32)],
        )
        arrays, places = scatter_halving(near, far, "cell", cells)
        pick, departure = call(
            functools.partial(prepare_increment, len(messages), capacity // 2),
            [((2 * BLOCKS, max(LANES, half)), BF16), ((1, OBLK_DEV * OB), F32)],
            (*messages, d1),
        )
        (increment,) = call(
            functools.partial(gather_increment, places),
            [((WIN_DEV, CBLK_DEV * CB), F32)],
            (*arrays, pick),
        )
        return increment, departure

    return local


def solution(mesh):
    placed = (
        P(("ens", "win"), "cell"),
        P(("ens", "cell"), None),
        P(("ens", "cell"), None),
        P("cell", "win", None, None, None),
        P("cell", "win", None, None),
        P("cell", "win", None, None),
        P("cell", "win", None),
    )
    return jax.shard_map(
        make_local(mesh.shape["cell"], mesh.shape["win"]),
        mesh=mesh,
        in_specs=placed,
        out_specs=(P(("ens", "win"), "cell"), P(("ens", "cell"), None)),
        check_vma=False,
    )
```

```python
import functools
import jax
import jax.numpy as jnp
from jax import lax
from jax.experimental import pallas as pl
from jax.experimental.pallas import tpu as pltpu
from jax.sharding import PartitionSpec as P

CB = 64
OB = 64
CBLK_DEV = 8
WIN_DEV = 8
OBLK_DEV = 8
BLOCKS = WIN_DEV * CBLK_DEV
LANES = 128
TILES = OB * CB // LANES

F32 = jnp.float32
BF16 = jnp.bfloat16
VMEM = pl.BlockSpec(memory_space=pltpu.VMEM)


def iota(shape, dim):
    return lax.broadcasted_iota(jnp.int32, shape, dim)


def one_hot(where):
    return jnp.where(where, 1.0, 0.0).astype(BF16)


def three(value):
    first = value.astype(BF16)
    rest = value - first.astype(F32)
    second = rest.astype(BF16)
    third = (rest - second.astype(F32)).astype(BF16)
    return [first, second, third]


def pick_rows(pick3, value):
    return jnp.dot(pick3, jnp.concatenate(three(value), axis=0), preferred_element_type=F32)


def swap(value, distance):
    return jnp.take_along_axis(
        value, iota(value.shape, 1) ^ distance, axis=1, mode="promise_in_bounds"
    )


def half_swap(value):
    return pltpu.roll(value, LANES // 2, 1)


def low(shape):
    return iota(shape, 1) < LANES // 2


def tree_sum(parts):
    parts = list(parts)
    while len(parts) > 1:
        parts = [sum(parts[i + 1 : i + 2], parts[i]) for i in range(0, len(parts), 2)]
    return parts[0]


def spread_obs(row):
    out = jnp.zeros((OBLK_DEV, LANES), F32)
    block = iota((OBLK_DEV, LANES), 0)
    lower = low((OBLK_DEV, LANES))
    for t in range(OBLK_DEV // 2):
        tile = jnp.broadcast_to(row[:, LANES * t : LANES * (t + 1)], (OBLK_DEV, LANES))
        turned = half_swap(tile)
        out = jnp.where(block == 2 * t, jnp.where(lower, tile, turned), out)
        out = jnp.where(block == 2 * t + 1, jnp.where(lower, turned, tile), out)
    return out


def forward_tree(h_ref, owner, x, bits, base):
    if bits == 0:
        return h_ref[0, 0, owner, :, LANES * base : LANES * (base + 1)] * x
    a = forward_tree(h_ref, owner, x, bits - 1, base)
    b = forward_tree(h_ref, owner, x, bits - 1, base + 2 ** (bits - 1))
    distance = 2**bits
    clear = (iota(a.shape, 1) & distance) == 0
    return jnp.where(clear, a, b) + swap(jnp.where(clear, b, a), distance)


def for_owners(owners, body):
    lax.fori_loop(0, owners, lambda o, c: (body(o), c)[1], 0, unroll=owners <= 4)


def forward(h_ref, pick_obs, x_scr, value_scr):
    owners, capacity = h_ref.shape[2], h_ref.shape[3]

    def body(o):
        rows = pl.ds(pl.multiple_of(o * capacity, capacity), capacity)
        value_scr[rows, :] = forward_tree(h_ref, o, x_scr[rows, :], 5, 0)

    for_owners(owners, body)
    m = pick_rows(pick_obs, value_scr[...])[:OBLK_DEV]
    m = m + swap(m, 1)
    even = (iota(m.shape, 1) & 1) == 0
    return jnp.where(even == low(m.shape), m, half_swap(m))


def adjoint(h_ref, slot_obs, d, picked_scr, store):
    owners, capacity = h_ref.shape[2], h_ref.shape[3]
    picked_scr[...] = pick_rows(slot_obs, d)

    def body(o):
        rows = pl.ds(pl.multiple_of(o * capacity, capacity), capacity)
        picked = picked_scr[rows, :]
        upper = jnp.where(low(picked.shape), 0, 1)
        total = None
        for t in range(TILES):
            spread = jnp.take_along_axis(picked, upper + 2 * t, axis=1, mode="promise_in_bounds")
            term = h_ref[0, 0, o, :, LANES * t : LANES * (t + 1)] * spread
            total = term if total is None else total + term
        total = total + half_swap(total)
        pair = total[: capacity // 2], total[capacity // 2 :]
        store(o, jnp.where(low(pair[0].shape), *pair))

    for_owners(owners, body)


def prepare(
    fslot_hbm, oslot_hbm, count_hbm, observed_hbm, weight_hbm, flux_hbm, h_hbm,
    pick_flux_ref, target_ref, slot_obs_ref, pick_obs_ref, index_ref, observed_out, weight_out, flux_ref, h_ref,
    fslot_ref, oslot_ref, count_ref, observed_ref, weight_ref, sems, h_sems,
):
    me = lax.axis_index("cell")
    owners, capacity = fslot_ref.shape[2:]
    pairs = (
        (fslot_hbm, fslot_ref),
        (oslot_hbm, oslot_ref),
        (count_hbm, count_ref),
        (observed_hbm, observed_ref),
        (weight_hbm, weight_ref),
        (flux_hbm, flux_ref),
    )
    small = [pltpu.make_async_copy(src, dst, sems.at[i]) for i, (src, dst) in enumerate(pairs)]
    large = [
        pltpu.make_async_copy(h_hbm.at[:, :, o], h_ref.at[:, :, o], h_sems.at[o])
        for o in range(owners)
    ]
    for copy in small + large:
        copy.start()
    for copy in small:
        copy.wait()
    slots = owners * capacity
    eye = iota((capacity, capacity), 0) == iota((capacity, capacity), 1)

    def column(ref):
        return jnp.concatenate(
            [
                jnp.sum(
                    jnp.where(eye, jnp.broadcast_to(ref[0, 0, o : o + 1, :], eye.shape), 0),
                    axis=1,
                    keepdims=True,
                )
                for o in range(owners)
            ],
            axis=0,
        )

    fslot, oslot = column(fslot_ref), column(oslot_ref)
    counts = jnp.concatenate(
        [
            jnp.broadcast_to(count_ref[0, 0:1, o : o + 1], (capacity, 1))
            for o in range(owners)
        ],
        axis=0,
    )
    slot = iota((slots, 1), 0)
    owner = slot // capacity
    live = (slot - owner * capacity) < counts
    oslot = jnp.where(live, oslot, OBLK_DEV)
    target = owner * BLOCKS + fslot
    target_ref[...] = jnp.broadcast_to(target.astype(F32), target_ref.shape)

    depth = owners * BLOCKS // 2
    row = (owner ^ me) * (BLOCKS // 2) + ((fslot & 7) >> 1) * WIN_DEV + (fslot >> 3)
    pick_flux_ref[...] = one_hot(iota((slots, 3 * depth), 1) % depth == row)
    slot_obs_ref[...] = one_hot((iota((slots, 3 * OBLK_DEV), 1) % OBLK_DEV) == oslot)

    eye3 = iota((slots, 3 * slots), 1) % slots == iota((slots, 3 * slots), 0)
    obs_row = jnp.sum(jnp.where(eye3, oslot, 0), axis=0, keepdims=True)
    pick_obs_ref[...] = one_hot(iota((16, 3 * slots), 0) == obs_row) * one_hot(
        iota((16, 3 * slots), 0) < OBLK_DEV
    )

    half = slots // 2
    count = max(1, half // LANES)
    index_ref[...] = jnp.zeros(index_ref.shape, F32)
    for part in range(2):
        for q in range(count):
            r = (iota((slots, LANES), 1) + LANES * q) % half
            at = (r // (capacity // 2)) * capacity + r % (capacity // 2) + part * (capacity // 2)
            index_ref[pl.ds(part * count + q, 1), :] = jnp.sum(
                jnp.where(iota((slots, LANES), 0) == at, target.astype(F32), 0.0),
                axis=0,
                keepdims=True,
            )
    observed_out[...] = spread_obs(observed_ref[...])
    weight_out[...] = spread_obs(weight_ref[...])
    for copy in large:
        copy.wait()


def first_model(order, *refs):
    parts = len(order)
    h_ref, pick_flux_ref, target_ref, pick_obs_ref, m_ref, x_ref, value_scr = refs[parts:]
    flux = jnp.concatenate(
        [
            ref[:, LANES * t : LANES * (t + 1)]
            for ref in [refs[order.index(k)] for k in range(parts)]
            for t in range(CBLK_DEV // 2)
        ],
        axis=0,
    )
    pair = pick_rows(pick_flux_ref[...], flux)
    odd = (target_ref[...].astype(jnp.int32) & 1) == 1
    x_ref[...] = jnp.where(odd != low(pair.shape), pair, half_swap(pair))
    m_ref[...] = forward(h_ref, pick_obs_ref[...], x_ref, value_scr)


def first_adjoint(parts, *refs):
    observed_ref, weight_ref, slot_obs_ref, index_ref, h_ref, message_ref, d_ref, picked_scr = refs[parts:]
    d = weight_ref[...] * (tree_sum([m[...] for m in refs[:parts]]) - observed_ref[...])
    d_ref[...] = d
    rows = h_ref.shape[3] // 2
    half = h_ref.shape[2] * rows

    def store(o, block):
        message_ref[pl.ds(pl.multiple_of(o * rows, rows), rows), :] = block

    adjoint(h_ref, slot_obs_ref[...], d, picked_scr, store)
    message_ref[half:, :] = index_ref[...]


def second_model(parts, *refs):
    messages = refs[:parts]
    cells = parts
    target_ref, x_ref, h_ref, pick_obs_ref, m_ref, next_scr, value_scr = refs[parts:]
    slots = target_ref.shape[0]
    half = slots // 2
    count = max(1, half // LANES)
    group = max(1, min(cells, LANES // half))
    total = None
    for first in range(0, cells, group):
        members = messages[first : first + group]
        picks = []
        for part in range(2):
            rows = []
            for q in range(count):
                at = half + part * count + q
                row = jnp.zeros((1, LANES), F32)
                for k, ref in enumerate(members):
                    row = jnp.where(iota((1, LANES), 1) // half % group == k, ref[at : at + 1, :], row)
                rows.append(one_hot(target_ref[...] == row))
            picks.append(jnp.concatenate(rows, axis=1)[:, : group * half])
        pick = jnp.concatenate(picks, axis=0)
        values = jnp.concatenate([ref[:half, :] for ref in members], axis=0)
        found = pick_rows(jnp.concatenate([pick] * 3, axis=1), values)
        total = found if total is None else total + found
    change = jnp.where(low((slots, LANES)), total[:slots], total[slots:])
    next_scr[...] = x_ref[...] - 0.5 * (change + half_swap(change))
    m_ref[...] = forward(h_ref, pick_obs_ref[...], next_scr, value_scr)


def second_adjoint(parts, *refs):
    observed_ref, weight_ref, first_ref, slot_obs_ref, h_ref = refs[parts : parts + 5]
    *outs, d_ref, picked_scr, block_scr = refs[parts + 5 :]
    me = lax.axis_index("cell")
    owners = h_ref.shape[2]
    d = weight_ref[...] * (tree_sum([m[...] for m in refs[:parts]]) - observed_ref[...])
    d_ref[...] = d

    def store(o, block):
        block_scr[o] = block

    adjoint(h_ref, slot_obs_ref[...], -0.25 * first_ref[...] - 0.5 * d, picked_scr, store)
    for k in range(owners):
        outs[owners - 1 - k][...] = block_scr[me ^ k]


def prepare_increment(parts, rows, *refs):
    d_ref, pick_ref, departure_ref = refs[parts:]
    messages = refs[:parts]
    cells = parts
    me = lax.axis_index("cell")
    half = cells * rows
    count = max(1, half // LANES)
    place = me * rows
    lane = iota((1, LANES), 1)
    row = iota((BLOCKS, LANES), 0)
    block = me * BLOCKS + (row % WIN_DEV) * CBLK_DEV + 2 * ((row // WIN_DEV) % 4) + row // (BLOCKS // 2)
    block = block.astype(F32)
    for part in range(2):
        for first in range(0, half, LANES):
            index = jnp.zeros((1, LANES), F32)
            for k in range(first // rows, min(cells, (first + LANES) // rows)):
                turned = pltpu.roll(
                    messages[k][half:, :], lax.rem(k * rows - place % LANES + 2 * LANES - first, LANES), 1
                )
                chosen = turned[part * count : part * count + 1]
                for q in range(1, count):
                    chosen = jnp.where(
                        place // LANES == q, turned[part * count + q : part * count + q + 1], chosen
                    )
                index = jnp.where((lane // rows) % cells == k - first // rows, chosen, index)
            pick_ref[BLOCKS * part : BLOCKS * (part + 1), first : first + LANES] = one_hot(block == index)
    for t in range(OBLK_DEV // 2):
        departure_ref[:, LANES * t : LANES * (t + 1)] = jnp.where(
            low((1, LANES)), d_ref[2 * t : 2 * t + 1, :], d_ref[2 * t + 1 : 2 * t + 2, :]
        )


def gather_increment(*refs):
    *arrays, pick_ref, out_ref = refs
    values = jnp.concatenate([ref[...] for ref in arrays[::-1]], axis=0)
    half = values.shape[0]
    terms = three(values)
    pick = pick_ref[...]
    if 3 * half <= LANES:
        terms.append(jnp.zeros((LANES - 3 * half, LANES), BF16))
    else:
        pick = jnp.concatenate([pick[:, :half]] * 3, axis=1)
    found = jnp.dot(pick, jnp.concatenate(terms, axis=0), preferred_element_type=F32)
    found = jnp.where(low((BLOCKS, LANES)), found[:BLOCKS], found[BLOCKS:])
    found = found + half_swap(found)
    for t in range(CBLK_DEV // 2):
        even = found[WIN_DEV * t : WIN_DEV * (t + 1)]
        odd = found[BLOCKS // 2 + WIN_DEV * t : BLOCKS // 2 + WIN_DEV * (t + 1)]
        out_ref[:, LANES * t : LANES * (t + 1)] = jnp.where(low(even.shape), even, odd)


def send(value, axis, size, k):
    return lax.ppermute(value, axis, [(i, i ^ k) for i in range(size)])


def exchange(own, sent, axis, size):
    return [own] + [send(sent, axis, size, k) for k in range(size - 1, 0, -1)][::-1]


def make_local(cells, wins):
    def local(prior_flux, observed, obs_weight, footprint, flux_slot, obs_slot, slot_count):
        owners, capacity = footprint.shape[2:4]
        slots = owners * capacity
        half = slots // 2
        index_rows = -(-2 * max(1, half // LANES) // 8) * 8
        params = pltpu.CompilerParams(vmem_limit_bytes=4 * footprint.size * 4 + 8 * 2**20)
        hbm = pl.BlockSpec(memory_space=pltpu.HBM)

        def call(body, outs, ins, scratch=(), space=VMEM):
            if space is hbm:
                ins = [pltpu.with_memory_space_constraint(value, pltpu.HBM) for value in ins]
                outs_at = [pltpu.VMEM(s, t) for s, t in outs]
            else:
                outs_at = [jax.ShapeDtypeStruct(s, t) for s, t in outs]
            return pl.pallas_call(
                body,
                out_shape=outs_at,
                in_specs=[space] * len(ins),
                out_specs=[VMEM] * len(outs),
                scratch_shapes=list(scratch),
                compiler_params=params,
            )(*ins)

        def like(value):
            return (value.shape, value.dtype)

        obs_tile = ((OBLK_DEV, LANES), F32)
        slot_tile = ((slots, LANES), F32)
        slot_scratch = pltpu.VMEM(*slot_tile)
        small = (flux_slot, obs_slot, slot_count, observed, obs_weight)
        pick_flux, target, slot_obs, pick_obs, index, observed_t, weight_t, flux, matrices = call(
            prepare,
            [
                ((slots, 3 * owners * BLOCKS // 2), BF16),
                slot_tile,
                ((slots, 3 * OBLK_DEV), BF16),
                ((16, 3 * slots), BF16),
                ((index_rows, LANES), F32),
                obs_tile,
                obs_tile,
                like(prior_flux),
                like(footprint),
            ],
            (*small, prior_flux, footprint),
            [
                *(pltpu.VMEM(*like(value)) for value in small),
                pltpu.SemaphoreType.DMA((len(small) + 1,)),
                pltpu.SemaphoreType.DMA((owners,)),
            ],
            hbm,
        )
        order = [0, cells - 1, *range(1, cells - 1)]
        fluxes = exchange(flux, prior_flux, "cell", cells)
        m0, x0 = call(
            functools.partial(first_model, order),
            [obs_tile, slot_tile],
            (*(fluxes[k] for k in order), matrices, pick_flux, target, pick_obs),
            [slot_scratch],
        )
        message, d0 = call(
            functools.partial(first_adjoint, wins),
            [((half + index_rows, LANES), F32), obs_tile],
            (*exchange(m0, m0, "win", wins), observed_t, weight_t, slot_obs, index, matrices),
            [slot_scratch],
        )
        messages = exchange(message, message, "cell", cells)
        (m1,) = call(
            functools.partial(second_model, cells),
            [obs_tile],
            (*messages, target, x0, matrices, pick_obs),
            [slot_scratch, slot_scratch],
        )
        *blocks, d1 = call(
            functools.partial(second_adjoint, wins),
            [((capacity // 2, LANES), F32)] * owners + [obs_tile],
            (*exchange(m1, m1, "win", wins), observed_t, weight_t, d0, slot_obs, matrices),
            [slot_scratch, pltpu.VMEM((owners, capacity // 2, LANES), F32)],
        )
        arrays = [send(block, "cell", cells, cells - 1 - i) for i, block in enumerate(blocks[:-1])]
        arrays = [blocks[-1]] + arrays[::-1]
        pick, departure = call(
            functools.partial(prepare_increment, cells, capacity // 2),
            [((2 * BLOCKS, max(LANES, half)), BF16), ((1, OBLK_DEV * OB), F32)],
            (*messages, d1),
        )
        (increment,) = call(
            gather_increment,
            [((WIN_DEV, CBLK_DEV * CB), F32)],
            (*arrays[::-1], pick),
        )
        return increment, departure

    return local


def solution(mesh):
    placed = (
        P(("ens", "win"), "cell"),
        P(("ens", "cell"), None),
        P(("ens", "cell"), None),
        P("cell", "win", None, None, None),
        P("cell", "win", None, None),
        P("cell", "win", None, None),
        P("cell", "win", None),
    )
    return jax.shard_map(
        make_local(mesh.shape["cell"], mesh.shape["win"]),
        mesh=mesh,
        in_specs=placed,
        out_specs=(P(("ens", "win"), "cell"), P(("ens", "cell"), None)),
        check_vma=False,
    )
```

```python
import functools
import jax
import jax.numpy as jnp
from jax import lax
from jax.experimental import pallas as pl
from jax.experimental.pallas import tpu as pltpu
from jax.sharding import PartitionSpec as P

CB = 64
OB = 64
CBLK_DEV = 8
WIN_DEV = 8
OBLK_DEV = 8
BLOCKS = WIN_DEV * CBLK_DEV
LANES = 128
TILES = OB * CB // LANES

F32 = jnp.float32
BF16 = jnp.bfloat16
VMEM = pl.BlockSpec(memory_space=pltpu.VMEM)


def iota(shape, dim):
    return lax.broadcasted_iota(jnp.int32, shape, dim)


def one_hot(where):
    return jnp.where(where, 1.0, 0.0).astype(BF16)


def three(value):
    first = value.astype(BF16)
    rest = value - first.astype(F32)
    second = rest.astype(BF16)
    third = (rest - second.astype(F32)).astype(BF16)
    return [first, second, third]


def pick_rows(pick3, value):
    return jnp.dot(pick3, jnp.concatenate(three(value), axis=0), preferred_element_type=F32)


def swap(value, distance):
    return jnp.take_along_axis(
        value, iota(value.shape, 1) ^ distance, axis=1, mode="promise_in_bounds"
    )


def half_swap(value):
    return pltpu.roll(value, LANES // 2, 1)


def low(shape):
    return iota(shape, 1) < LANES // 2


def tree_sum(parts):
    parts = list(parts)
    while len(parts) > 1:
        parts = [sum(parts[i + 1 : i + 2], parts[i]) for i in range(0, len(parts), 2)]
    return parts[0]


def spread_obs(row):
    out = jnp.zeros((OBLK_DEV, LANES), F32)
    block = iota((OBLK_DEV, LANES), 0)
    lower = low((OBLK_DEV, LANES))
    for t in range(OBLK_DEV // 2):
        tile = jnp.broadcast_to(row[:, LANES * t : LANES * (t + 1)], (OBLK_DEV, LANES))
        turned = half_swap(tile)
        out = jnp.where(block == 2 * t, jnp.where(lower, tile, turned), out)
        out = jnp.where(block == 2 * t + 1, jnp.where(lower, turned, tile), out)
    return out


def merge_tree(tiles):
    distance = 2
    while len(tiles) > 1:
        clear = (iota(tiles[0].shape, 1) & distance) == 0
        tiles = [
            jnp.where(clear, a, b) + swap(jnp.where(clear, b, a), distance)
            for a, b in zip(tiles[::2], tiles[1::2])
        ]
        distance *= 2
    return tiles[0]


def h_columns(h_ref, first, last, start, size):
    return jnp.concatenate([h_ref[0, 0, o, :, start : start + size] for o in range(first, last)], axis=0)


def forward(h_ref, pick_obs, x):
    x = jnp.concatenate([x, x], axis=1)
    tiles = []
    for t in range(TILES // 2):
        sums = pick_rows(pick_obs, h_columns(h_ref, 0, h_ref.shape[2], 2 * LANES * t, 2 * LANES) * x)
        tiles += [sums[:OBLK_DEV, :LANES], sums[:OBLK_DEV, LANES:]]
    m = merge_tree(tiles)
    m = m + swap(m, 1)
    even = (iota(m.shape, 1) & 1) == 0
    return jnp.where(even == low(m.shape), m, half_swap(m))


def adjoint(h_ref, slot_obs, d, store):
    owners, capacity = h_ref.shape[2], h_ref.shape[3]
    upper = jnp.where(low(d.shape), 0, 1)
    spread = jnp.concatenate(
        [
            jnp.take_along_axis(d, upper + 2 * t, axis=1, mode="promise_in_bounds")
            for t in range(TILES)
        ],
        axis=1,
    )
    spread = jnp.concatenate([term.astype(F32) for term in three(spread)], axis=0).astype(BF16)
    group = min(owners, 4)
    for first in range(0, owners, group):
        rows = slice(first * capacity, (first + group) * capacity)
        total = None
        for t in range(TILES // 2):
            columns = slice(2 * LANES * t, 2 * LANES * (t + 1))
            given = jnp.dot(slot_obs[rows], spread[:, columns], preferred_element_type=F32)
            terms = h_columns(h_ref, first, first + group, 2 * LANES * t, 2 * LANES) * given
            total = terms if total is None else total + terms
        total = total[:, :LANES] + total[:, LANES:]
        total = total + half_swap(total)
        for o in range(group):
            upper_half = o * capacity + capacity // 2
            pair = total[o * capacity : upper_half], total[upper_half : (o + 1) * capacity]
            store(first + o, jnp.where(low(pair[0].shape), *pair))


def prepare(
    fslot_hbm, oslot_hbm, count_hbm, observed_hbm, weight_hbm, flux_hbm, h_hbm,
    pick_flux_ref, target_ref, slot_obs_ref, pick_obs_ref, index_ref, observed_out, weight_out, flux_ref, h_ref,
    fslot_ref, oslot_ref, count_ref, observed_ref, weight_ref, sems, h_sems,
):
    me = lax.axis_index("cell")
    owners, capacity = fslot_ref.shape[2:]
    pairs = (
        (fslot_hbm, fslot_ref),
        (oslot_hbm, oslot_ref),
        (count_hbm, count_ref),
        (observed_hbm, observed_ref),
        (weight_hbm, weight_ref),
        (flux_hbm, flux_ref),
    )
    small = [pltpu.make_async_copy(src, dst, sems.at[i]) for i, (src, dst) in enumerate(pairs)]
    large = [
        pltpu.make_async_copy(h_hbm.at[:, :, o], h_ref.at[:, :, o], h_sems.at[o])
        for o in range(owners)
    ]
    for copy in small + large:
        copy.start()
    for copy in small:
        copy.wait()
    slots = owners * capacity
    eye = iota((capacity, capacity), 0) == iota((capacity, capacity), 1)

    def column(ref):
        return jnp.concatenate(
            [
                jnp.sum(
                    jnp.where(eye, jnp.broadcast_to(ref[0, 0, o : o + 1, :], eye.shape), 0),
                    axis=1,
                    keepdims=True,
                )
                for o in range(owners)
            ],
            axis=0,
        )

    fslot, oslot = column(fslot_ref), column(oslot_ref)
    counts = jnp.concatenate(
        [
            jnp.broadcast_to(count_ref[0, 0:1, o : o + 1], (capacity, 1))
            for o in range(owners)
        ],
        axis=0,
    )
    slot = iota((slots, 1), 0)
    owner = slot // capacity
    live = (slot - owner * capacity) < counts
    oslot = jnp.where(live, oslot, OBLK_DEV)
    target = owner * BLOCKS + fslot
    target_ref[...] = jnp.broadcast_to(target.astype(F32), target_ref.shape)

    depth = owners * BLOCKS // 2
    row = (owner ^ me) * (BLOCKS // 2) + ((fslot & 7) >> 1) * WIN_DEV + (fslot >> 3)
    pick_flux_ref[...] = one_hot(iota((slots, 3 * depth), 1) % depth == row)
    slot_obs_ref[...] = one_hot((iota((slots, 3 * OBLK_DEV), 1) % OBLK_DEV) == oslot)

    eye3 = iota((slots, 3 * slots), 1) % slots == iota((slots, 3 * slots), 0)
    obs_row = jnp.sum(jnp.where(eye3, oslot, 0), axis=0, keepdims=True)
    pick_obs_ref[...] = one_hot(iota((16, 3 * slots), 0) == obs_row) * one_hot(
        iota((16, 3 * slots), 0) < OBLK_DEV
    )

    half = slots // 2
    count = max(1, half // LANES)
    index_ref[...] = jnp.zeros(index_ref.shape, F32)
    for part in range(2):
        for q in range(count):
            r = (iota((slots, LANES), 1) + LANES * q) % half
            at = (r // (capacity // 2)) * capacity + r % (capacity // 2) + part * (capacity // 2)
            index_ref[pl.ds(part * count + q, 1), :] = jnp.sum(
                jnp.where(iota((slots, LANES), 0) == at, target.astype(F32), 0.0),
                axis=0,
                keepdims=True,
            )
    observed_out[...] = spread_obs(observed_ref[...])
    weight_out[...] = spread_obs(weight_ref[...])
    for copy in large:
        copy.wait()


def first_model(order, *refs):
    parts = len(order)
    h_ref, pick_flux_ref, target_ref, pick_obs_ref, m_ref, x_ref = refs[parts:]
    flux = jnp.concatenate(
        [
            ref[:, LANES * t : LANES * (t + 1)]
            for ref in [refs[order.index(k)] for k in range(parts)]
            for t in range(CBLK_DEV // 2)
        ],
        axis=0,
    )
    pair = pick_rows(pick_flux_ref[...], flux)
    odd = (target_ref[...].astype(jnp.int32) & 1) == 1
    x = jnp.where(odd != low(pair.shape), pair, half_swap(pair))
    x_ref[...] = x
    m_ref[...] = forward(h_ref, pick_obs_ref[...], x)


def first_adjoint(parts, *refs):
    observed_ref, weight_ref, slot_obs_ref, index_ref, h_ref, message_ref, d_ref = refs[parts:]
    d = weight_ref[...] * (tree_sum([m[...] for m in refs[:parts]]) - observed_ref[...])
    d_ref[...] = d
    rows = h_ref.shape[3] // 2
    half = h_ref.shape[2] * rows

    def store(o, block):
        message_ref[o * rows : (o + 1) * rows, :] = block

    adjoint(h_ref, slot_obs_ref[...], d, store)
    message_ref[half:, :] = index_ref[...]


def second_model(parts, *refs):
    messages = refs[:parts]
    cells = parts
    target_ref, x_ref, h_ref, pick_obs_ref, m_ref = refs[parts:]
    slots = target_ref.shape[0]
    half = slots // 2
    count = max(1, half // LANES)
    group = max(1, min(cells, LANES // half))
    total = None
    for first in range(0, cells, group):
        members = messages[first : first + group]
        picks = []
        for part in range(2):
            rows = []
            for q in range(count):
                at = half + part * count + q
                row = jnp.zeros((1, LANES), F32)
                for k, ref in enumerate(members):
                    row = jnp.where(iota((1, LANES), 1) // half % group == k, ref[at : at + 1, :], row)
                rows.append(one_hot(target_ref[...] == row))
            picks.append(jnp.concatenate(rows, axis=1)[:, : group * half])
        pick = jnp.concatenate(picks, axis=0)
        values = jnp.concatenate([ref[:half, :] for ref in members], axis=0)
        found = pick_rows(jnp.concatenate([pick] * 3, axis=1), values)
        total = found if total is None else total + found
    change = jnp.where(low((slots, LANES)), total[:slots], total[slots:])
    m_ref[...] = forward(h_ref, pick_obs_ref[...], x_ref[...] - 0.5 * (change + half_swap(change)))


def second_adjoint(parts, *refs):
    observed_ref, weight_ref, first_ref, slot_obs_ref, h_ref = refs[parts : parts + 5]
    *outs, d_ref, block_scr = refs[parts + 5 :]
    me = lax.axis_index("cell")
    owners = h_ref.shape[2]
    d = weight_ref[...] * (tree_sum([m[...] for m in refs[:parts]]) - observed_ref[...])
    d_ref[...] = d

    def store(o, block):
        block_scr[o] = block

    adjoint(h_ref, slot_obs_ref[...], -0.25 * first_ref[...] - 0.5 * d, store)
    for k in range(owners):
        outs[owners - 1 - k][...] = block_scr[me ^ k]


def prepare_increment(parts, rows, *refs):
    d_ref, pick_ref, departure_ref = refs[parts:]
    messages = refs[:parts]
    cells = parts
    me = lax.axis_index("cell")
    half = cells * rows
    count = max(1, half // LANES)
    place = me * rows
    lane = iota((1, LANES), 1)
    row = iota((BLOCKS, LANES), 0)
    block = me * BLOCKS + (row % WIN_DEV) * CBLK_DEV + 2 * ((row // WIN_DEV) % 4) + row // (BLOCKS // 2)
    block = block.astype(F32)
    for part in range(2):
        for first in range(0, half, LANES):
            index = jnp.zeros((1, LANES), F32)
            for k in range(first // rows, min(cells, (first + LANES) // rows)):
                turned = pltpu.roll(
                    messages[k][half:, :], lax.rem(k * rows - place % LANES + 2 * LANES - first, LANES), 1
                )
                chosen = turned[part * count : part * count + 1]
                for q in range(1, count):
                    chosen = jnp.where(
                        place // LANES == q, turned[part * count + q : part * count + q + 1], chosen
                    )
                index = jnp.where((lane // rows) % cells == k - first // rows, chosen, index)
            pick_ref[BLOCKS * part : BLOCKS * (part + 1), first : first + LANES] = one_hot(block == index)
    for t in range(OBLK_DEV // 2):
        departure_ref[:, LANES * t : LANES * (t + 1)] = jnp.where(
            low((1, LANES)), d_ref[2 * t : 2 * t + 1, :], d_ref[2 * t + 1 : 2 * t + 2, :]
        )


def gather_increment(*refs):
    *arrays, pick_ref, out_ref = refs
    values = jnp.concatenate([ref[...] for ref in arrays[::-1]], axis=0)
    half = values.shape[0]
    terms = three(values)
    pick = pick_ref[...]
    if 3 * half <= LANES:
        terms.append(jnp.zeros((LANES - 3 * half, LANES), BF16))
    else:
        pick = jnp.concatenate([pick[:, :half]] * 3, axis=1)
    found = jnp.dot(pick, jnp.concatenate(terms, axis=0), preferred_element_type=F32)
    found = jnp.where(low((BLOCKS, LANES)), found[:BLOCKS], found[BLOCKS:])
    found = found + half_swap(found)
    for t in range(CBLK_DEV // 2):
        even = found[WIN_DEV * t : WIN_DEV * (t + 1)]
        odd = found[BLOCKS // 2 + WIN_DEV * t : BLOCKS // 2 + WIN_DEV * (t + 1)]
        out_ref[:, LANES * t : LANES * (t + 1)] = jnp.where(low(even.shape), even, odd)


def send(value, axis, size, k):
    return lax.ppermute(value, axis, [(i, i ^ k) for i in range(size)])


def exchange(own, sent, axis, size):
    return [own] + [send(sent, axis, size, k) for k in range(size - 1, 0, -1)][::-1]


def make_local(cells, wins):
    def local(prior_flux, observed, obs_weight, footprint, flux_slot, obs_slot, slot_count):
        owners, capacity = footprint.shape[2:4]
        slots = owners * capacity
        half = slots // 2
        index_rows = -(-2 * max(1, half // LANES) // 8) * 8
        params = pltpu.CompilerParams(vmem_limit_bytes=4 * footprint.size * 4 + 8 * 2**20)
        hbm = pl.BlockSpec(memory_space=pltpu.HBM)

        def call(body, outs, ins, scratch=(), space=VMEM):
            if space is hbm:
                ins = [pltpu.with_memory_space_constraint(value, pltpu.HBM) for value in ins]
                outs_at = [pltpu.VMEM(s, t) for s, t in outs]
            else:
                outs_at = [jax.ShapeDtypeStruct(s, t) for s, t in outs]
            return pl.pallas_call(
                body,
                out_shape=outs_at,
                in_specs=[space] * len(ins),
                out_specs=[VMEM] * len(outs),
                scratch_shapes=list(scratch),
                compiler_params=params,
            )(*ins)

        def like(value):
            return (value.shape, value.dtype)

        obs_tile = ((OBLK_DEV, LANES), F32)
        slot_tile = ((slots, LANES), F32)
        small = (flux_slot, obs_slot, slot_count, observed, obs_weight)
        pick_flux, target, slot_obs, pick_obs, index, observed_t, weight_t, flux, matrices = call(
            prepare,
            [
                ((slots, 3 * owners * BLOCKS // 2), BF16),
                slot_tile,
                ((slots, 3 * OBLK_DEV), BF16),
                ((16, 3 * slots), BF16),
                ((index_rows, LANES), F32),
                obs_tile,
                obs_tile,
                like(prior_flux),
                like(footprint),
            ],
            (*small, prior_flux, footprint),
            [
                *(pltpu.VMEM(*like(value)) for value in small),
                pltpu.SemaphoreType.DMA((len(small) + 1,)),
                pltpu.SemaphoreType.DMA((owners,)),
            ],
            hbm,
        )
        order = [0, cells // 2, *range(1, cells // 2), *range(cells // 2 + 1, cells)]
        fluxes = exchange(flux, prior_flux, "cell", cells)
        m0, x0 = call(
            functools.partial(first_model, order),
            [obs_tile, slot_tile],
            (*(fluxes[k] for k in order), matrices, pick_flux, target, pick_obs),
        )
        message, d0 = call(
            functools.partial(first_adjoint, wins),
            [((half + index_rows, LANES), F32), obs_tile],
            (*exchange(m0, m0, "win", wins), observed_t, weight_t, slot_obs, index, matrices),
        )
        messages = exchange(message, message, "cell", cells)
        (m1,) = call(
            functools.partial(second_model, cells),
            [obs_tile],
            (*messages, target, x0, matrices, pick_obs),
        )
        *blocks, d1 = call(
            functools.partial(second_adjoint, wins),
            [((capacity // 2, LANES), F32)] * owners + [obs_tile],
            (*exchange(m1, m1, "win", wins), observed_t, weight_t, d0, slot_obs, matrices),
            [pltpu.VMEM((owners, capacity // 2, LANES), F32)],
        )
        arrays = [send(block, "cell", cells, cells - 1 - i) for i, block in enumerate(blocks[:-1])]
        arrays = [blocks[-1]] + arrays[::-1]
        pick, departure = call(
            functools.partial(prepare_increment, cells, capacity // 2),
            [((2 * BLOCKS, max(LANES, half)), BF16), ((1, OBLK_DEV * OB), F32)],
            (*messages, d1),
        )
        (increment,) = call(
            gather_increment,
            [((WIN_DEV, CBLK_DEV * CB), F32)],
            (*arrays[::-1], pick),
        )
        return increment, departure

    return local


def solution(mesh):
    placed = (
        P(("ens", "win"), "cell"),
        P(("ens", "cell"), None),
        P(("ens", "cell"), None),
        P("cell", "win", None, None, None),
        P("cell", "win", None, None),
        P("cell", "win", None, None),
        P("cell", "win", None),
    )
    return jax.shard_map(
        make_local(mesh.shape["cell"], mesh.shape["win"]),
        mesh=mesh,
        in_specs=placed,
        out_specs=(P(("ens", "win"), "cell"), P(("ens", "cell"), None)),
        check_vma=False,
    )
```

```python
import functools
import jax
import jax.numpy as jnp
from jax import lax
from jax.experimental import pallas as pl
from jax.experimental.pallas import tpu as pltpu
from jax.sharding import PartitionSpec as P

CB = 64
OB = 64
CBLK_DEV = 8
WIN_DEV = 8
OBLK_DEV = 8
BLOCKS = WIN_DEV * CBLK_DEV
LANES = 128
TILES = OB * CB // LANES

F32 = jnp.float32
BF16 = jnp.bfloat16
VMEM = pl.BlockSpec(memory_space=pltpu.VMEM)

GATHER_FLUX = [[(3, 2), (1, 0)], [(1, 2), (2, 0), (3, 1)], [(3, 0), (0, 2), (2, 3)], [(0, 3), (2, 1)], [(0, 1), (1, 3)]]
GATHER_BLOCKS = [[(2, 0), (3, 2)], [(3, 1), (2, 3), (1, 0)], [(3, 0), (0, 1)], [(1, 2), (0, 3), (2, 1)], [(0, 2), (1, 3)]]
SCATTER_BLOCKS = [[(3, 0), (2, 1)], [(2, 0), (0, 1)], [(1, 0), (3, 1), (0, 2), (2, 3)], [(0, 3), (1, 2)], [(3, 2), (1, 3)]]
ORDERS = ([2, 1, 0, 4, 3], [4, 3, 2, 1, 0], [0, 1, 2, 3, 4])


def iota(shape, dim):
    return lax.broadcasted_iota(jnp.int32, shape, dim)


def one_hot(where):
    return jnp.where(where, 1.0, 0.0).astype(BF16)


def three(value):
    first = value.astype(BF16)
    rest = value - first.astype(F32)
    second = rest.astype(BF16)
    third = (rest - second.astype(F32)).astype(BF16)
    return [first, second, third]


def pick_rows(pick3, value):
    return jnp.dot(pick3, jnp.concatenate(three(value), axis=0), preferred_element_type=F32)


def swap(value, distance):
    return jnp.take_along_axis(
        value, iota(value.shape, 1) ^ distance, axis=1, mode="promise_in_bounds"
    )


def half_swap(value):
    return pltpu.roll(value, LANES // 2, 1)


def low(shape):
    return iota(shape, 1) < LANES // 2


def in_turn(refs, order):
    return [refs[0]] + [refs[1 + order.index(j)] for j in range(len(order))]


def readers(refs, ops, me):
    if ops is None:
        return [functools.partial(lambda ref, at: ref[at], ref) for ref in refs]

    def read(source, at):
        value = refs[0][at]
        for ref, op in zip(refs[1:], ops):
            for src, dst in op:
                if src == source:
                    value = jnp.where(me == dst, ref[at], value)
        return value

    cells = 1 + max(src for op in ops for src, _ in op)
    return [functools.partial(read, c) for c in range(cells)]


def tree_sum(parts):
    parts = list(parts)
    while len(parts) > 1:
        parts = [sum(parts[i + 1 : i + 2], parts[i]) for i in range(0, len(parts), 2)]
    return parts[0]


def spread_obs(row):
    out = jnp.zeros((OBLK_DEV, LANES), F32)
    block = iota((OBLK_DEV, LANES), 0)
    lower = low((OBLK_DEV, LANES))
    for t in range(OBLK_DEV // 2):
        tile = jnp.broadcast_to(row[:, LANES * t : LANES * (t + 1)], (OBLK_DEV, LANES))
        turned = half_swap(tile)
        out = jnp.where(block == 2 * t, jnp.where(lower, tile, turned), out)
        out = jnp.where(block == 2 * t + 1, jnp.where(lower, turned, tile), out)
    return out


def merge_tree(tiles):
    distance = 2
    while len(tiles) > 1:
        clear = (iota(tiles[0].shape, 1) & distance) == 0
        tiles = [
            jnp.where(clear, a, b) + swap(jnp.where(clear, b, a), distance)
            for a, b in zip(tiles[::2], tiles[1::2])
        ]
        distance *= 2
    return tiles[0]


def h_columns(h_ref, first, last, start, size):
    return jnp.concatenate([h_ref[0, 0, o, :, start : start + size] for o in range(first, last)], axis=0)


def forward(h_ref, pick_obs, x):
    x = jnp.concatenate([x, x], axis=1)
    tiles = []
    for t in range(TILES // 2):
        sums = pick_rows(pick_obs, h_columns(h_ref, 0, h_ref.shape[2], 2 * LANES * t, 2 * LANES) * x)
        tiles += [sums[:OBLK_DEV, :LANES], sums[:OBLK_DEV, LANES:]]
    m = merge_tree(tiles)
    m = m + swap(m, 1)
    even = (iota(m.shape, 1) & 1) == 0
    return jnp.where(even == low(m.shape), m, half_swap(m))


def adjoint(h_ref, slot_obs, d, store):
    owners, capacity = h_ref.shape[2], h_ref.shape[3]
    upper = jnp.where(low(d.shape), 0, 1)
    spread = jnp.concatenate(
        [
            jnp.take_along_axis(d, upper + 2 * t, axis=1, mode="promise_in_bounds")
            for t in range(TILES)
        ],
        axis=1,
    )
    spread = jnp.concatenate([term.astype(F32) for term in three(spread)], axis=0).astype(BF16)
    group = min(owners, 4)
    for first in range(0, owners, group):
        rows = slice(first * capacity, (first + group) * capacity)
        total = None
        for t in range(TILES // 2):
            columns = slice(2 * LANES * t, 2 * LANES * (t + 1))
            given = jnp.dot(slot_obs[rows], spread[:, columns], preferred_element_type=F32)
            terms = h_columns(h_ref, first, first + group, 2 * LANES * t, 2 * LANES) * given
            total = terms if total is None else total + terms
        total = total[:, :LANES] + total[:, LANES:]
        total = total + half_swap(total)
        for o in range(group):
            upper_half = o * capacity + capacity // 2
            pair = total[o * capacity : upper_half], total[upper_half : (o + 1) * capacity]
            store(first + o, jnp.where(low(pair[0].shape), *pair))


def prepare(
    by_xor,
    fslot_hbm, oslot_hbm, count_hbm, observed_hbm, weight_hbm, flux_hbm, h_hbm,
    pick_flux_ref, target_ref, slot_obs_ref, pick_obs_ref, index_ref, observed_out, weight_out, flux_ref, h_ref,
    fslot_ref, oslot_ref, count_ref, observed_ref, weight_ref, sems, h_sems,
):
    me = lax.axis_index("cell")
    owners, capacity = fslot_ref.shape[2:]
    pairs = (
        (fslot_hbm, fslot_ref),
        (oslot_hbm, oslot_ref),
        (count_hbm, count_ref),
        (observed_hbm, observed_ref),
        (weight_hbm, weight_ref),
        (flux_hbm, flux_ref),
    )
    small = [pltpu.make_async_copy(src, dst, sems.at[i]) for i, (src, dst) in enumerate(pairs)]
    large = [
        pltpu.make_async_copy(h_hbm.at[:, :, o], h_ref.at[:, :, o], h_sems.at[o])
        for o in range(owners)
    ]
    for copy in small + large:
        copy.start()
    for copy in small:
        copy.wait()
    slots = owners * capacity
    eye = iota((capacity, capacity), 0) == iota((capacity, capacity), 1)

    def column(ref):
        return jnp.concatenate(
            [
                jnp.sum(
                    jnp.where(eye, jnp.broadcast_to(ref[0, 0, o : o + 1, :], eye.shape), 0),
                    axis=1,
                    keepdims=True,
                )
                for o in range(owners)
            ],
            axis=0,
        )

    fslot, oslot = column(fslot_ref), column(oslot_ref)
    counts = jnp.concatenate(
        [
            jnp.broadcast_to(count_ref[0, 0:1, o : o + 1], (capacity, 1))
            for o in range(owners)
        ],
        axis=0,
    )
    slot = iota((slots, 1), 0)
    owner = slot // capacity
    live = (slot - owner * capacity) < counts
    oslot = jnp.where(live, oslot, OBLK_DEV)
    target = owner * BLOCKS + fslot
    target_ref[...] = jnp.broadcast_to(target.astype(F32), target_ref.shape)

    depth = owners * BLOCKS // 2
    row = ((owner ^ me) if by_xor else owner) * (BLOCKS // 2) + ((fslot & 7) >> 1) * WIN_DEV + (fslot >> 3)
    pick_flux_ref[...] = one_hot(iota((slots, 3 * depth), 1) % depth == row)
    slot_obs_ref[...] = one_hot((iota((slots, 3 * OBLK_DEV), 1) % OBLK_DEV) == oslot)

    eye3 = iota((slots, 3 * slots), 1) % slots == iota((slots, 3 * slots), 0)
    obs_row = jnp.sum(jnp.where(eye3, oslot, 0), axis=0, keepdims=True)
    pick_obs_ref[...] = one_hot(iota((16, 3 * slots), 0) == obs_row) * one_hot(
        iota((16, 3 * slots), 0) < OBLK_DEV
    )

    half = slots // 2
    count = max(1, half // LANES)
    index_ref[...] = jnp.zeros(index_ref.shape, F32)
    for part in range(2):
        for q in range(count):
            r = (iota((slots, LANES), 1) + LANES * q) % half
            at = (r // (capacity // 2)) * capacity + r % (capacity // 2) + part * (capacity // 2)
            index_ref[pl.ds(part * count + q, 1), :] = jnp.sum(
                jnp.where(iota((slots, LANES), 0) == at, target.astype(F32), 0.0),
                axis=0,
                keepdims=True,
            )
    observed_out[...] = spread_obs(observed_ref[...])
    weight_out[...] = spread_obs(weight_ref[...])
    for copy in large:
        copy.wait()


def first_model(ops, order, *refs):
    parts = 1 + len(order)
    h_ref, pick_flux_ref, target_ref, pick_obs_ref, m_ref, x_ref = refs[parts:]
    flux = jnp.concatenate(
        [
            read((slice(None), slice(LANES * t, LANES * (t + 1))))
            for read in readers(in_turn(refs, order), ops, lax.axis_index("cell"))
            for t in range(CBLK_DEV // 2)
        ],
        axis=0,
    )
    pair = pick_rows(pick_flux_ref[...], flux)
    odd = (target_ref[...].astype(jnp.int32) & 1) == 1
    x = jnp.where(odd != low(pair.shape), pair, half_swap(pair))
    x_ref[...] = x
    m_ref[...] = forward(h_ref, pick_obs_ref[...], x)


def first_adjoint(parts, *refs):
    observed_ref, weight_ref, slot_obs_ref, index_ref, h_ref, message_ref, d_ref = refs[parts:]
    d = weight_ref[...] * (tree_sum([m[...] for m in refs[:parts]]) - observed_ref[...])
    d_ref[...] = d
    rows = h_ref.shape[3] // 2
    half = h_ref.shape[2] * rows

    def store(o, block):
        message_ref[o * rows : (o + 1) * rows, :] = block

    adjoint(h_ref, slot_obs_ref[...], d, store)
    message_ref[half:, :] = index_ref[...]


def second_model(ops, order, *refs):
    parts = 1 + len(order)
    messages = readers(in_turn(refs, order), ops, lax.axis_index("cell"))
    cells = len(messages)
    target_ref, x_ref, h_ref, pick_obs_ref, m_ref = refs[parts:]
    slots = target_ref.shape[0]
    half = slots // 2
    count = max(1, half // LANES)
    group = max(1, min(cells, LANES // half))
    total = None
    for first in range(0, cells, group):
        members = messages[first : first + group]
        picks = []
        for part in range(2):
            rows = []
            for q in range(count):
                at = half + part * count + q
                row = jnp.zeros((1, LANES), F32)
                for k, read in enumerate(members):
                    row = jnp.where(iota((1, LANES), 1) // half % group == k, read(slice(at, at + 1)), row)
                rows.append(one_hot(target_ref[...] == row))
            picks.append(jnp.concatenate(rows, axis=1)[:, : group * half])
        pick = jnp.concatenate(picks, axis=0)
        values = jnp.concatenate([read(slice(0, half)) for read in members], axis=0)
        found = pick_rows(jnp.concatenate([pick] * 3, axis=1), values)
        total = found if total is None else total + found
    change = jnp.where(low((slots, LANES)), total[:slots], total[slots:])
    m_ref[...] = forward(h_ref, pick_obs_ref[...], x_ref[...] - 0.5 * (change + half_swap(change)))


def second_adjoint(ops, parts, *refs):
    observed_ref, weight_ref, first_ref, slot_obs_ref, h_ref = refs[parts : parts + 5]
    *outs, d_ref, block_scr = refs[parts + 5 :]
    me = lax.axis_index("cell")
    owners = h_ref.shape[2]
    d = weight_ref[...] * (tree_sum([m[...] for m in refs[:parts]]) - observed_ref[...])
    d_ref[...] = d

    def store(o, block):
        block_scr[o] = block

    adjoint(h_ref, slot_obs_ref[...], -0.25 * first_ref[...] - 0.5 * d, store)
    for j, out in enumerate(outs):
        if ops is None:
            target = me ^ j
        else:
            target = me
            for src, dst in ops[j - 1] if j else ():
                target = jnp.where(me == src, dst, target)
        out[...] = block_scr[target]


def prepare_increment(ops, order, rows, *refs):
    d_ref, pick_ref, departure_ref = refs[1 + len(order) :]
    me = lax.axis_index("cell")
    messages = readers(in_turn(refs, order), ops, me)
    cells = len(messages)
    half = cells * rows
    count = max(1, half // LANES)
    place = me * rows
    lane = iota((1, LANES), 1)
    row = iota((BLOCKS, LANES), 0)
    block = me * BLOCKS + (row % WIN_DEV) * CBLK_DEV + 2 * ((row // WIN_DEV) % 4) + row // (BLOCKS // 2)
    block = block.astype(F32)
    for part in range(2):
        for first in range(0, half, LANES):
            index = jnp.zeros((1, LANES), F32)
            for k in range(first // rows, min(cells, (first + LANES) // rows)):
                turned = pltpu.roll(
                    messages[k](slice(half, None)), lax.rem(k * rows - place % LANES + 2 * LANES - first, LANES), 1
                )
                chosen = turned[part * count : part * count + 1]
                for q in range(1, count):
                    chosen = jnp.where(
                        place // LANES == q, turned[part * count + q : part * count + q + 1], chosen
                    )
                index = jnp.where((lane // rows) % cells == k - first // rows, chosen, index)
            pick_ref[BLOCKS * part : BLOCKS * (part + 1), first : first + LANES] = one_hot(block == index)
    for t in range(OBLK_DEV // 2):
        departure_ref[:, LANES * t : LANES * (t + 1)] = jnp.where(
            low((1, LANES)), d_ref[2 * t : 2 * t + 1, :], d_ref[2 * t + 1 : 2 * t + 2, :]
        )


def gather_increment(ops, order, *refs):
    *arrays, pick_ref, out_ref = refs
    sources = readers(in_turn(arrays, order), ops, lax.axis_index("cell"))
    values = jnp.concatenate([read(...) for read in sources], axis=0)
    half = values.shape[0]
    terms = three(values)
    pick = pick_ref[...]
    if 3 * half <= LANES:
        terms.append(jnp.zeros((LANES - 3 * half, LANES), BF16))
    else:
        pick = jnp.concatenate([pick[:, :half]] * 3, axis=1)
    found = jnp.dot(pick, jnp.concatenate(terms, axis=0), preferred_element_type=F32)
    found = jnp.where(low((BLOCKS, LANES)), found[:BLOCKS], found[BLOCKS:])
    found = found + half_swap(found)
    for t in range(CBLK_DEV // 2):
        even = found[WIN_DEV * t : WIN_DEV * (t + 1)]
        odd = found[BLOCKS // 2 + WIN_DEV * t : BLOCKS // 2 + WIN_DEV * (t + 1)]
        out_ref[:, LANES * t : LANES * (t + 1)] = jnp.where(low(even.shape), even, odd)


def exchange(own, sent, axis, size):
    return [own] + [
        lax.ppermute(sent, axis, [(i, i ^ k) for i in range(size)]) for k in range(1, size)
    ]


def exchange_by(ops, order, own, sent):
    outs = [
        lax.ppermute(sent[j] if isinstance(sent, list) else sent, "cell", op)
        for j, op in enumerate(ops)
    ]
    return [own] + [outs[j] for j in order]


def make_local(cells, wins):
    def local(prior_flux, observed, obs_weight, footprint, flux_slot, obs_slot, slot_count):
        owners, capacity = footprint.shape[2:4]
        slots = owners * capacity
        half = slots // 2
        xors = [[(i, i ^ k) for i in range(cells)] for k in range(1, cells)]
        rounds = (GATHER_FLUX, GATHER_BLOCKS, SCATTER_BLOCKS) if cells == 4 else (xors,) * 3
        orders = ORDERS if cells == 4 else (list(range(cells - 1)),) * 3
        tables = rounds if cells == 4 else (None,) * 3
        index_rows = -(-2 * max(1, half // LANES) // 8) * 8
        params = pltpu.CompilerParams(vmem_limit_bytes=4 * footprint.size * 4 + 8 * 2**20)
        hbm = pl.BlockSpec(memory_space=pltpu.HBM)

        def call(body, outs, ins, scratch=(), space=VMEM):
            if space is hbm:
                ins = [pltpu.with_memory_space_constraint(value, pltpu.HBM) for value in ins]
                outs_at = [pltpu.VMEM(s, t) for s, t in outs]
            else:
                outs_at = [jax.ShapeDtypeStruct(s, t) for s, t in outs]
            return pl.pallas_call(
                body,
                out_shape=outs_at,
                in_specs=[space] * len(ins),
                out_specs=[VMEM] * len(outs),
                scratch_shapes=list(scratch),
                compiler_params=params,
            )(*ins)

        def like(value):
            return (value.shape, value.dtype)

        obs_tile = ((OBLK_DEV, LANES), F32)
        slot_tile = ((slots, LANES), F32)
        small = (flux_slot, obs_slot, slot_count, observed, obs_weight)
        pick_flux, target, slot_obs, pick_obs, index, observed_t, weight_t, flux, matrices = call(
            functools.partial(prepare, tables[0] is None),
            [
                ((slots, 3 * owners * BLOCKS // 2), BF16),
                slot_tile,
                ((slots, 3 * OBLK_DEV), BF16),
                ((16, 3 * slots), BF16),
                ((index_rows, LANES), F32),
                obs_tile,
                obs_tile,
                like(prior_flux),
                like(footprint),
            ],
            (*small, prior_flux, footprint),
            [
                *(pltpu.VMEM(*like(value)) for value in small),
                pltpu.SemaphoreType.DMA((len(small) + 1,)),
                pltpu.SemaphoreType.DMA((owners,)),
            ],
            hbm,
        )
        m0, x0 = call(
            functools.partial(first_model, tables[0], orders[0]),
            [obs_tile, slot_tile],
            (
                *exchange_by(rounds[0], orders[0], flux, prior_flux),
                *(matrices, pick_flux, target, pick_obs),
            ),
        )
        message, d0 = call(
            functools.partial(first_adjoint, wins),
            [((half + index_rows, LANES), F32), obs_tile],
            (*exchange(m0, m0, "win", wins), observed_t, weight_t, slot_obs, index, matrices),
        )
        messages = exchange_by(rounds[1], orders[1], message, message)
        (m1,) = call(
            functools.partial(second_model, tables[1], orders[1]),
            [obs_tile],
            (*messages, target, x0, matrices, pick_obs),
        )
        *blocks, d1 = call(
            functools.partial(second_adjoint, tables[2], wins),
            [((capacity // 2, LANES), F32)] * (1 + len(rounds[2])) + [obs_tile],
            (*exchange(m1, m1, "win", wins), observed_t, weight_t, d0, slot_obs, matrices),
            [pltpu.VMEM((owners, capacity // 2, LANES), F32)],
        )
        arrays = exchange_by(rounds[2], orders[2], blocks[0], blocks[1:])
        pick, departure = call(
            functools.partial(prepare_increment, tables[1], orders[1], capacity // 2),
            [((2 * BLOCKS, max(LANES, half)), BF16), ((1, OBLK_DEV * OB), F32)],
            (*messages, d1),
        )
        (increment,) = call(
            functools.partial(gather_increment, tables[2], orders[2]),
            [((WIN_DEV, CBLK_DEV * CB), F32)],
            (*arrays, pick),
        )
        return increment, departure

    return local


def solution(mesh):
    placed = (
        P(("ens", "win"), "cell"),
        P(("ens", "cell"), None),
        P(("ens", "cell"), None),
        P("cell", "win", None, None, None),
        P("cell", "win", None, None),
        P("cell", "win", None, None),
        P("cell", "win", None),
    )
    return jax.shard_map(
        make_local(mesh.shape["cell"], mesh.shape["win"]),
        mesh=mesh,
        in_specs=placed,
        out_specs=(P(("ens", "win"), "cell"), P(("ens", "cell"), None)),
        check_vma=False,
    )
```

```python
import functools
import jax
import jax.numpy as jnp
from jax import lax
from jax.experimental import pallas as pl
from jax.experimental.pallas import tpu as pltpu
from jax.sharding import PartitionSpec as P

CB = 64
OB = 64
CBLK_DEV = 8
WIN_DEV = 8
OBLK_DEV = 8
BLOCKS = WIN_DEV * CBLK_DEV
LANES = 128
TILES = OB * CB // LANES

F32 = jnp.float32
BF16 = jnp.bfloat16
VMEM = pl.BlockSpec(memory_space=pltpu.VMEM)

GATHER_FLUX = [[(2, 3), (3, 2), (0, 0), (1, 1)], [(0, 1), (1, 3), (3, 0), (2, 2)], [(0, 3), (1, 2), (2, 0), (3, 1)], [(0, 2), (1, 0), (2, 1), (3, 3)]]
GATHER_BLOCKS = [[(0, 1), (1, 3), (3, 0), (2, 2)], [(0, 3), (1, 2), (2, 0), (3, 1)], [(0, 2), (1, 0), (2, 1), (3, 3)], [(2, 3), (3, 2), (0, 0), (1, 1)]]
SCATTER_BLOCKS = [[(0, 1), (1, 2), (2, 0), (3, 3)], [(0, 3), (3, 0), (1, 1), (2, 2)], [(0, 2), (1, 0), (2, 3), (3, 1)], [(1, 3), (2, 1), (3, 2), (0, 0)]]
ORDERS = ([1, 0, 3, 2], [3, 2, 1, 0], [0, 1, 2, 3])


def iota(shape, dim):
    return lax.broadcasted_iota(jnp.int32, shape, dim)


def one_hot(where):
    return jnp.where(where, 1.0, 0.0).astype(BF16)


def three(value):
    first = value.astype(BF16)
    rest = value - first.astype(F32)
    second = rest.astype(BF16)
    third = (rest - second.astype(F32)).astype(BF16)
    return [first, second, third]


def pick_rows(pick3, value):
    return jnp.dot(pick3, jnp.concatenate(three(value), axis=0), preferred_element_type=F32)


def swap(value, distance):
    return jnp.take_along_axis(
        value, iota(value.shape, 1) ^ distance, axis=1, mode="promise_in_bounds"
    )


def half_swap(value):
    return pltpu.roll(value, LANES // 2, 1)


def low(shape):
    return iota(shape, 1) < LANES // 2


def in_turn(refs, order):
    return [refs[0]] + [refs[1 + order.index(j)] for j in range(len(order))]


def readers(refs, ops, me):
    if ops is None:
        return [functools.partial(lambda ref, at: ref[at], ref) for ref in refs]

    def read(source, at):
        value = refs[0][at]
        for ref, op in zip(refs[1:], ops):
            for src, dst in op:
                if src == source and src != dst:
                    value = jnp.where(me == dst, ref[at], value)
        return value

    cells = 1 + max(src for op in ops for src, _ in op)
    return [functools.partial(read, c) for c in range(cells)]


def tree_sum(parts):
    parts = list(parts)
    while len(parts) > 1:
        parts = [sum(parts[i + 1 : i + 2], parts[i]) for i in range(0, len(parts), 2)]
    return parts[0]


def spread_obs(row):
    out = jnp.zeros((OBLK_DEV, LANES), F32)
    block = iota((OBLK_DEV, LANES), 0)
    lower = low((OBLK_DEV, LANES))
    for t in range(OBLK_DEV // 2):
        tile = jnp.broadcast_to(row[:, LANES * t : LANES * (t + 1)], (OBLK_DEV, LANES))
        turned = half_swap(tile)
        out = jnp.where(block == 2 * t, jnp.where(lower, tile, turned), out)
        out = jnp.where(block == 2 * t + 1, jnp.where(lower, turned, tile), out)
    return out


def merge_tree(tiles):
    distance = 2
    while len(tiles) > 1:
        clear = (iota(tiles[0].shape, 1) & distance) == 0
        tiles = [
            jnp.where(clear, a, b) + swap(jnp.where(clear, b, a), distance)
            for a, b in zip(tiles[::2], tiles[1::2])
        ]
        distance *= 2
    return tiles[0]


def h_columns(h_ref, first, last, start, size):
    return jnp.concatenate([h_ref[0, 0, o, :, start : start + size] for o in range(first, last)], axis=0)


def forward(h_ref, pick_obs, x):
    x = jnp.concatenate([x, x], axis=1)
    tiles = []
    for t in range(TILES // 2):
        sums = pick_rows(pick_obs, h_columns(h_ref, 0, h_ref.shape[2], 2 * LANES * t, 2 * LANES) * x)
        tiles += [sums[:OBLK_DEV, :LANES], sums[:OBLK_DEV, LANES:]]
    m = merge_tree(tiles)
    m = m + swap(m, 1)
    even = (iota(m.shape, 1) & 1) == 0
    return jnp.where(even == low(m.shape), m, half_swap(m))


def adjoint(h_ref, slot_obs, d, store):
    owners, capacity = h_ref.shape[2], h_ref.shape[3]
    upper = jnp.where(low(d.shape), 0, 1)
    spread = jnp.concatenate(
        [
            jnp.take_along_axis(d, upper + 2 * t, axis=1, mode="promise_in_bounds")
            for t in range(TILES)
        ],
        axis=1,
    )
    spread = jnp.concatenate([term.astype(F32) for term in three(spread)], axis=0).astype(BF16)
    group = min(owners, 4)
    for first in range(0, owners, group):
        rows = slice(first * capacity, (first + group) * capacity)
        total = None
        for t in range(TILES // 2):
            columns = slice(2 * LANES * t, 2 * LANES * (t + 1))
            given = jnp.dot(slot_obs[rows], spread[:, columns], preferred_element_type=F32)
            terms = h_columns(h_ref, first, first + group, 2 * LANES * t, 2 * LANES) * given
            total = terms if total is None else total + terms
        total = total[:, :LANES] + total[:, LANES:]
        total = total + half_swap(total)
        for o in range(group):
            upper_half = o * capacity + capacity // 2
            pair = total[o * capacity : upper_half], total[upper_half : (o + 1) * capacity]
            store(first + o, jnp.where(low(pair[0].shape), *pair))


def prepare(
    by_xor,
    fslot_hbm, oslot_hbm, count_hbm, observed_hbm, weight_hbm, flux_hbm, h_hbm,
    pick_flux_ref, target_ref, slot_obs_ref, pick_obs_ref, index_ref, observed_out, weight_out, flux_ref, h_ref,
    fslot_ref, oslot_ref, count_ref, observed_ref, weight_ref, sems, h_sems,
):
    me = lax.axis_index("cell")
    owners, capacity = fslot_ref.shape[2:]
    pairs = (
        (fslot_hbm, fslot_ref),
        (oslot_hbm, oslot_ref),
        (count_hbm, count_ref),
        (observed_hbm, observed_ref),
        (weight_hbm, weight_ref),
        (flux_hbm, flux_ref),
    )
    small = [pltpu.make_async_copy(src, dst, sems.at[i]) for i, (src, dst) in enumerate(pairs)]
    large = [
        pltpu.make_async_copy(h_hbm.at[:, :, o], h_ref.at[:, :, o], h_sems.at[o])
        for o in range(owners)
    ]
    for copy in small + large:
        copy.start()
    for copy in small:
        copy.wait()
    slots = owners * capacity
    eye = iota((capacity, capacity), 0) == iota((capacity, capacity), 1)

    def column(ref):
        return jnp.concatenate(
            [
                jnp.sum(
                    jnp.where(eye, jnp.broadcast_to(ref[0, 0, o : o + 1, :], eye.shape), 0),
                    axis=1,
                    keepdims=True,
                )
                for o in range(owners)
            ],
            axis=0,
        )

    fslot, oslot = column(fslot_ref), column(oslot_ref)
    counts = jnp.concatenate(
        [
            jnp.broadcast_to(count_ref[0, 0:1, o : o + 1], (capacity, 1))
            for o in range(owners)
        ],
        axis=0,
    )
    slot = iota((slots, 1), 0)
    owner = slot // capacity
    live = (slot - owner * capacity) < counts
    oslot = jnp.where(live, oslot, OBLK_DEV)
    target = owner * BLOCKS + fslot
    target_ref[...] = jnp.broadcast_to(target.astype(F32), target_ref.shape)

    depth = owners * BLOCKS // 2
    row = ((owner ^ me) if by_xor else owner) * (BLOCKS // 2) + ((fslot & 7) >> 1) * WIN_DEV + (fslot >> 3)
    pick_flux_ref[...] = one_hot(iota((slots, 3 * depth), 1) % depth == row)
    slot_obs_ref[...] = one_hot((iota((slots, 3 * OBLK_DEV), 1) % OBLK_DEV) == oslot)

    eye3 = iota((slots, 3 * slots), 1) % slots == iota((slots, 3 * slots), 0)
    obs_row = jnp.sum(jnp.where(eye3, oslot, 0), axis=0, keepdims=True)
    pick_obs_ref[...] = one_hot(iota((16, 3 * slots), 0) == obs_row) * one_hot(
        iota((16, 3 * slots), 0) < OBLK_DEV
    )

    half = slots // 2
    count = max(1, half // LANES)
    index_ref[...] = jnp.zeros(index_ref.shape, F32)
    for part in range(2):
        for q in range(count):
            r = (iota((slots, LANES), 1) + LANES * q) % half
            at = (r // (capacity // 2)) * capacity + r % (capacity // 2) + part * (capacity // 2)
            index_ref[pl.ds(part * count + q, 1), :] = jnp.sum(
                jnp.where(iota((slots, LANES), 0) == at, target.astype(F32), 0.0),
                axis=0,
                keepdims=True,
            )
    observed_out[...] = spread_obs(observed_ref[...])
    weight_out[...] = spread_obs(weight_ref[...])
    for copy in large:
        copy.wait()


def first_model(ops, order, *refs):
    parts = 1 + len(order)
    h_ref, pick_flux_ref, target_ref, pick_obs_ref, m_ref, x_ref = refs[parts:]
    flux = jnp.concatenate(
        [
            read((slice(None), slice(LANES * t, LANES * (t + 1))))
            for read in readers(in_turn(refs, order), ops, lax.axis_index("cell"))
            for t in range(CBLK_DEV // 2)
        ],
        axis=0,
    )
    pair = pick_rows(pick_flux_ref[...], flux)
    odd = (target_ref[...].astype(jnp.int32) & 1) == 1
    x = jnp.where(odd != low(pair.shape), pair, half_swap(pair))
    x_ref[...] = x
    m_ref[...] = forward(h_ref, pick_obs_ref[...], x)


def first_adjoint(parts, *refs):
    observed_ref, weight_ref, slot_obs_ref, index_ref, h_ref, message_ref, d_ref = refs[parts:]
    d = weight_ref[...] * (tree_sum([m[...] for m in refs[:parts]]) - observed_ref[...])
    d_ref[...] = d
    rows = h_ref.shape[3] // 2
    half = h_ref.shape[2] * rows

    def store(o, block):
        message_ref[o * rows : (o + 1) * rows, :] = block

    adjoint(h_ref, slot_obs_ref[...], d, store)
    message_ref[half:, :] = index_ref[...]


def second_model(ops, order, *refs):
    parts = 1 + len(order)
    messages = readers(in_turn(refs, order), ops, lax.axis_index("cell"))
    cells = len(messages)
    target_ref, x_ref, h_ref, pick_obs_ref, m_ref = refs[parts:]
    slots = target_ref.shape[0]
    half = slots // 2
    count = max(1, half // LANES)
    group = max(1, min(cells, LANES // half))
    total = None
    for first in range(0, cells, group):
        members = messages[first : first + group]
        picks = []
        for part in range(2):
            rows = []
            for q in range(count):
                at = half + part * count + q
                row = jnp.zeros((1, LANES), F32)
                for k, read in enumerate(members):
                    row = jnp.where(iota((1, LANES), 1) // half % group == k, read(slice(at, at + 1)), row)
                rows.append(one_hot(target_ref[...] == row))
            picks.append(jnp.concatenate(rows, axis=1)[:, : group * half])
        pick = jnp.concatenate(picks, axis=0)
        values = jnp.concatenate([read(slice(0, half)) for read in members], axis=0)
        found = pick_rows(jnp.concatenate([pick] * 3, axis=1), values)
        total = found if total is None else total + found
    change = jnp.where(low((slots, LANES)), total[:slots], total[slots:])
    m_ref[...] = forward(h_ref, pick_obs_ref[...], x_ref[...] - 0.5 * (change + half_swap(change)))


def second_adjoint(ops, parts, *refs):
    observed_ref, weight_ref, first_ref, slot_obs_ref, h_ref = refs[parts : parts + 5]
    *outs, d_ref, block_scr = refs[parts + 5 :]
    me = lax.axis_index("cell")
    owners = h_ref.shape[2]
    d = weight_ref[...] * (tree_sum([m[...] for m in refs[:parts]]) - observed_ref[...])
    d_ref[...] = d

    def store(o, block):
        block_scr[o] = block

    adjoint(h_ref, slot_obs_ref[...], -0.25 * first_ref[...] - 0.5 * d, store)
    for j, out in enumerate(outs):
        if ops is None:
            target = me ^ j
        else:
            target = me
            for src, dst in ops[j - 1] if j else ():
                target = jnp.where(me == src, dst, target)
        out[...] = block_scr[target]


def prepare_increment(ops, order, rows, *refs):
    d_ref, pick_ref, departure_ref = refs[1 + len(order) :]
    me = lax.axis_index("cell")
    messages = readers(in_turn(refs, order), ops, me)
    cells = len(messages)
    half = cells * rows
    count = max(1, half // LANES)
    place = me * rows
    lane = iota((1, LANES), 1)
    row = iota((BLOCKS, LANES), 0)
    block = me * BLOCKS + (row % WIN_DEV) * CBLK_DEV + 2 * ((row // WIN_DEV) % 4) + row // (BLOCKS // 2)
    block = block.astype(F32)
    for part in range(2):
        for first in range(0, half, LANES):
            index = jnp.zeros((1, LANES), F32)
            for k in range(first // rows, min(cells, (first + LANES) // rows)):
                turned = pltpu.roll(
                    messages[k](slice(half, None)), lax.rem(k * rows - place % LANES + 2 * LANES - first, LANES), 1
                )
                chosen = turned[part * count : part * count + 1]
                for q in range(1, count):
                    chosen = jnp.where(
                        place // LANES == q, turned[part * count + q : part * count + q + 1], chosen
                    )
                index = jnp.where((lane // rows) % cells == k - first // rows, chosen, index)
            pick_ref[BLOCKS * part : BLOCKS * (part + 1), first : first + LANES] = one_hot(block == index)
    for t in range(OBLK_DEV // 2):
        departure_ref[:, LANES * t : LANES * (t + 1)] = jnp.where(
            low((1, LANES)), d_ref[2 * t : 2 * t + 1, :], d_ref[2 * t + 1 : 2 * t + 2, :]
        )


def gather_increment(ops, order, *refs):
    *arrays, pick_ref, out_ref = refs
    sources = readers(in_turn(arrays, order), ops, lax.axis_index("cell"))
    values = jnp.concatenate([read(...) for read in sources], axis=0)
    half = values.shape[0]
    terms = three(values)
    pick = pick_ref[...]
    if 3 * half <= LANES:
        terms.append(jnp.zeros((LANES - 3 * half, LANES), BF16))
    else:
        pick = jnp.concatenate([pick[:, :half]] * 3, axis=1)
    found = jnp.dot(pick, jnp.concatenate(terms, axis=0), preferred_element_type=F32)
    found = jnp.where(low((BLOCKS, LANES)), found[:BLOCKS], found[BLOCKS:])
    found = found + half_swap(found)
    for t in range(CBLK_DEV // 2):
        even = found[WIN_DEV * t : WIN_DEV * (t + 1)]
        odd = found[BLOCKS // 2 + WIN_DEV * t : BLOCKS // 2 + WIN_DEV * (t + 1)]
        out_ref[:, LANES * t : LANES * (t + 1)] = jnp.where(low(even.shape), even, odd)


def exchange(own, sent, axis, size):
    return [own] + [
        lax.ppermute(sent, axis, [(i, i ^ k) for i in range(size)]) for k in range(1, size)
    ]


def exchange_by(ops, order, own, sent):
    outs = [
        lax.ppermute(sent[j] if isinstance(sent, list) else sent, "cell", op)
        for j, op in enumerate(ops)
    ]
    return [own] + [outs[j] for j in order]


def make_local(cells, wins):
    def local(prior_flux, observed, obs_weight, footprint, flux_slot, obs_slot, slot_count):
        owners, capacity = footprint.shape[2:4]
        slots = owners * capacity
        half = slots // 2
        xors = [[(i, i ^ k) for i in range(cells)] for k in range(1, cells)]
        rounds = (GATHER_FLUX, GATHER_BLOCKS, SCATTER_BLOCKS) if cells == 4 else (xors,) * 3
        orders = ORDERS if cells == 4 else (list(range(cells - 1)),) * 3
        tables = rounds if cells == 4 else (None,) * 3
        index_rows = -(-2 * max(1, half // LANES) // 8) * 8
        params = pltpu.CompilerParams(vmem_limit_bytes=4 * footprint.size * 4 + 8 * 2**20)
        hbm = pl.BlockSpec(memory_space=pltpu.HBM)

        def call(body, outs, ins, scratch=(), space=VMEM):
            if space is hbm:
                ins = [pltpu.with_memory_space_constraint(value, pltpu.HBM) for value in ins]
                outs_at = [pltpu.VMEM(s, t) for s, t in outs]
            else:
                outs_at = [jax.ShapeDtypeStruct(s, t) for s, t in outs]
            return pl.pallas_call(
                body,
                out_shape=outs_at,
                in_specs=[space] * len(ins),
                out_specs=[VMEM] * len(outs),
                scratch_shapes=list(scratch),
                compiler_params=params,
            )(*ins)

        def like(value):
            return (value.shape, value.dtype)

        obs_tile = ((OBLK_DEV, LANES), F32)
        slot_tile = ((slots, LANES), F32)
        small = (flux_slot, obs_slot, slot_count, observed, obs_weight)
        pick_flux, target, slot_obs, pick_obs, index, observed_t, weight_t, flux, matrices = call(
            functools.partial(prepare, tables[0] is None),
            [
                ((slots, 3 * owners * BLOCKS // 2), BF16),
                slot_tile,
                ((slots, 3 * OBLK_DEV), BF16),
                ((16, 3 * slots), BF16),
                ((index_rows, LANES), F32),
                obs_tile,
                obs_tile,
                like(prior_flux),
                like(footprint),
            ],
            (*small, prior_flux, footprint),
            [
                *(pltpu.VMEM(*like(value)) for value in small),
                pltpu.SemaphoreType.DMA((len(small) + 1,)),
                pltpu.SemaphoreType.DMA((owners,)),
            ],
            hbm,
        )
        m0, x0 = call(
            functools.partial(first_model, tables[0], orders[0]),
            [obs_tile, slot_tile],
            (
                *exchange_by(rounds[0], orders[0], flux, prior_flux),
                *(matrices, pick_flux, target, pick_obs),
            ),
        )
        message, d0 = call(
            functools.partial(first_adjoint, wins),
            [((half + index_rows, LANES), F32), obs_tile],
            (*exchange(m0, m0, "win", wins), observed_t, weight_t, slot_obs, index, matrices),
        )
        messages = exchange_by(rounds[1], orders[1], message, message)
        (m1,) = call(
            functools.partial(second_model, tables[1], orders[1]),
            [obs_tile],
            (*messages, target, x0, matrices, pick_obs),
        )
        *blocks, d1 = call(
            functools.partial(second_adjoint, tables[2], wins),
            [((capacity // 2, LANES), F32)] * (1 + len(rounds[2])) + [obs_tile],
            (*exchange(m1, m1, "win", wins), observed_t, weight_t, d0, slot_obs, matrices),
            [pltpu.VMEM((owners, capacity // 2, LANES), F32)],
        )
        arrays = exchange_by(rounds[2], orders[2], blocks[0], blocks[1:])
        pick, departure = call(
            functools.partial(prepare_increment, tables[1], orders[1], capacity // 2),
            [((2 * BLOCKS, max(LANES, half)), BF16), ((1, OBLK_DEV * OB), F32)],
            (*messages, d1),
        )
        (increment,) = call(
            functools.partial(gather_increment, tables[2], orders[2]),
            [((WIN_DEV, CBLK_DEV * CB), F32)],
            (*arrays, pick),
        )
        return increment, departure

    return local


def solution(mesh):
    placed = (
        P(("ens", "win"), "cell"),
        P(("ens", "cell"), None),
        P(("ens", "cell"), None),
        P("cell", "win", None, None, None),
        P("cell", "win", None, None),
        P("cell", "win", None, None),
        P("cell", "win", None),
    )
    return jax.shard_map(
        make_local(mesh.shape["cell"], mesh.shape["win"]),
        mesh=mesh,
        in_specs=placed,
        out_specs=(P(("ens", "win"), "cell"), P(("ens", "cell"), None)),
        check_vma=False,
    )
```

```python
import functools
import jax
import jax.numpy as jnp
from jax import lax
from jax.experimental import pallas as pl
from jax.experimental.pallas import tpu as pltpu
from jax.sharding import PartitionSpec as P

CB = 64
OB = 64
CBLK_DEV = 8
WIN_DEV = 8
OBLK_DEV = 8
BLOCKS = WIN_DEV * CBLK_DEV
LANES = 128
TILES = OB * CB // LANES

F32 = jnp.float32
BF16 = jnp.bfloat16
VMEM = pl.BlockSpec(memory_space=pltpu.VMEM)


def iota(shape, dim):
    return lax.broadcasted_iota(jnp.int32, shape, dim)


def one_hot(where):
    return jnp.where(where, 1.0, 0.0).astype(BF16)


def three(value):
    first = value.astype(BF16)
    rest = value - first.astype(F32)
    second = rest.astype(BF16)
    third = (rest - second.astype(F32)).astype(BF16)
    return [first, second, third]


def pick_rows(pick3, value):
    return jnp.dot(pick3, jnp.concatenate(three(value), axis=0), preferred_element_type=F32)


def swap(value, distance):
    return jnp.take_along_axis(
        value, iota(value.shape, 1) ^ distance, axis=1, mode="promise_in_bounds"
    )


def half_swap(value):
    return pltpu.roll(value, LANES // 2, 1)


def low(shape):
    return iota(shape, 1) < LANES // 2


def tree_sum(parts):
    parts = list(parts)
    while len(parts) > 1:
        parts = [sum(parts[i + 1 : i + 2], parts[i]) for i in range(0, len(parts), 2)]
    return parts[0]


def spread_obs(row):
    out = jnp.zeros((OBLK_DEV, LANES), F32)
    block = iota((OBLK_DEV, LANES), 0)
    lower = low((OBLK_DEV, LANES))
    for t in range(OBLK_DEV // 2):
        tile = jnp.broadcast_to(row[:, LANES * t : LANES * (t + 1)], (OBLK_DEV, LANES))
        turned = half_swap(tile)
        out = jnp.where(block == 2 * t, jnp.where(lower, tile, turned), out)
        out = jnp.where(block == 2 * t + 1, jnp.where(lower, turned, tile), out)
    return out


def merge_tree(tiles):
    distance = 2
    while len(tiles) > 1:
        clear = (iota(tiles[0].shape, 1) & distance) == 0
        tiles = [
            jnp.where(clear, a, b) + swap(jnp.where(clear, b, a), distance)
            for a, b in zip(tiles[::2], tiles[1::2])
        ]
        distance *= 2
    return tiles[0]


def h_columns(h_ref, first, last, start, size):
    return jnp.concatenate([h_ref[0, 0, o, :, start : start + size] for o in range(first, last)], axis=0)


def forward(g_ref, obs_ref, x, x_scr, sums):
    slots = x.shape[0]
    sets = len(sums)
    x_scr[...] = x
    for ref in sums:
        ref[...] = jnp.zeros(ref.shape, F32)

    def add(s, ref):
        block = obs_ref[s]
        ref[block] = ref[block] + g_ref[s] * x_scr[pl.ds(s, 1), :]

    def step(j, carry):
        for n, ref in enumerate(sums):
            add(n * (slots // sets) + j, ref)
        return carry

    lax.fori_loop(0, slots // sets, step, 0, unroll=min(slots // sets, 16))
    rows = OBLK_DEV * TILES // 8
    tiles = []
    for q in range(rows):
        at = (q // 4, slice(8 * (q % 4), 8 * (q % 4) + 8))
        tiles.append(tree_sum([ref[at] for ref in sums]))
    m = merge_tree(tiles)
    m = m + swap(m, 1)
    lane = iota((OBLK_DEV, LANES), 1) & (OB - 1)
    place = (lane & 1) * OB + 2 * (4 * iota(lane.shape, 0) + (lane >> 4))
    out = jnp.zeros(m.shape, F32)
    for u in range(8):
        row = jnp.broadcast_to(m[u : u + 1], m.shape)
        found = jnp.take_along_axis(row, place, axis=1, mode="promise_in_bounds")
        out = jnp.where((lane & 15) >> 1 == u, found, out)
    return out


def adjoint(h_ref, slot_obs, d, store):
    owners, capacity = h_ref.shape[2], h_ref.shape[3]
    upper = jnp.where(low(d.shape), 0, 1)
    spread = jnp.concatenate(
        [
            jnp.take_along_axis(d, upper + 2 * t, axis=1, mode="promise_in_bounds")
            for t in range(TILES)
        ],
        axis=1,
    )
    spread = jnp.concatenate([term.astype(F32) for term in three(spread)], axis=0).astype(BF16)
    group = min(owners, 4)
    for first in range(0, owners, group):
        rows = slice(first * capacity, (first + group) * capacity)
        total = None
        for t in range(TILES // 2):
            columns = slice(2 * LANES * t, 2 * LANES * (t + 1))
            given = jnp.dot(slot_obs[rows], spread[:, columns], preferred_element_type=F32)
            terms = h_columns(h_ref, first, first + group, 2 * LANES * t, 2 * LANES) * given
            total = terms if total is None else total + terms
        total = total[:, :LANES] + total[:, LANES:]
        total = total + half_swap(total)
        for o in range(group):
            upper_half = o * capacity + capacity // 2
            pair = total[o * capacity : upper_half], total[upper_half : (o + 1) * capacity]
            store(first + o, jnp.where(low(pair[0].shape), *pair))


def prepare(
    fslot_hbm, oslot_hbm, count_hbm, observed_hbm, weight_hbm, flux_hbm, h_hbm, g_hbm,
    pick_flux_ref, target_ref, slot_obs_ref, index_ref, observed_out, weight_out, flux_ref, h_ref, g_ref, obs_ref,
    fslot_ref, oslot_ref, count_ref, observed_ref, weight_ref, oslot_scalars, count_scalars, sems, h_sems, g_sems,
):
    me = lax.axis_index("cell")
    owners, capacity = fslot_ref.shape[2:]
    pairs = (
        (fslot_hbm, fslot_ref),
        (oslot_hbm, oslot_ref),
        (count_hbm, count_ref),
        (observed_hbm, observed_ref),
        (weight_hbm, weight_ref),
        (flux_hbm, flux_ref),
        (oslot_hbm, oslot_scalars),
        (count_hbm, count_scalars),
    )
    small = [pltpu.make_async_copy(src, dst, sems.at[i]) for i, (src, dst) in enumerate(pairs)]
    large = [
        pltpu.make_async_copy(h_hbm.at[:, :, o], h_ref.at[:, :, o], h_sems.at[o])
        for o in range(owners)
    ]
    for copy in small + large:
        copy.start()

    def turned(n, r):
        return pltpu.make_async_copy(g_hbm.at[n, :, r], g_ref.at[8 * n + r], g_sems.at[8 * n + r])

    def each_turned(action):
        def step(n, carry):
            for r in range(8):
                action(turned(n, r))
            return carry

        lax.fori_loop(0, owners * capacity // 8, step, 0, unroll=owners <= 4)

    each_turned(lambda copy: copy.start())
    for copy in small:
        copy.wait()

    def scalar_step(o, carry):
        for j in range(capacity):
            obs_ref[o * capacity + j] = jnp.where(
                j < count_scalars[0, 0, o], oslot_scalars[0, 0, o, j], OBLK_DEV
            )
        return carry

    lax.fori_loop(0, owners, scalar_step, 0, unroll=owners <= 4)
    slots = owners * capacity
    eye = iota((capacity, capacity), 0) == iota((capacity, capacity), 1)

    def column(ref):
        return jnp.concatenate(
            [
                jnp.sum(
                    jnp.where(eye, jnp.broadcast_to(ref[0, 0, o : o + 1, :], eye.shape), 0),
                    axis=1,
                    keepdims=True,
                )
                for o in range(owners)
            ],
            axis=0,
        )

    fslot, oslot = column(fslot_ref), column(oslot_ref)
    counts = jnp.concatenate(
        [
            jnp.broadcast_to(count_ref[0, 0:1, o : o + 1], (capacity, 1))
            for o in range(owners)
        ],
        axis=0,
    )
    slot = iota((slots, 1), 0)
    owner = slot // capacity
    live = (slot - owner * capacity) < counts
    oslot = jnp.where(live, oslot, OBLK_DEV)
    target = owner * BLOCKS + fslot
    target_ref[...] = jnp.broadcast_to(target.astype(F32), target_ref.shape)

    depth = owners * BLOCKS // 2
    row = (owner ^ me) * (BLOCKS // 2) + ((fslot & 7) >> 1) * WIN_DEV + (fslot >> 3)
    pick_flux_ref[...] = one_hot(iota((slots, 3 * depth), 1) % depth == row)
    slot_obs_ref[...] = one_hot((iota((slots, 3 * OBLK_DEV), 1) % OBLK_DEV) == oslot)

    half = slots // 2
    count = max(1, half // LANES)
    index_ref[...] = jnp.zeros(index_ref.shape, F32)
    for part in range(2):
        for q in range(count):
            r = (iota((slots, LANES), 1) + LANES * q) % half
            at = (r // (capacity // 2)) * capacity + r % (capacity // 2) + part * (capacity // 2)
            index_ref[pl.ds(part * count + q, 1), :] = jnp.sum(
                jnp.where(iota((slots, LANES), 0) == at, target.astype(F32), 0.0),
                axis=0,
                keepdims=True,
            )
    observed_out[...] = spread_obs(observed_ref[...])
    weight_out[...] = spread_obs(weight_ref[...])
    for copy in large:
        copy.wait()
    each_turned(lambda copy: copy.wait())


def first_model(order, *refs):
    parts = len(order)
    g_ref, pick_flux_ref, target_ref, obs_ref, m_ref, x_ref, x_scr, *sums = refs[parts:]
    flux = jnp.concatenate(
        [
            ref[:, LANES * t : LANES * (t + 1)]
            for ref in [refs[order.index(k)] for k in range(parts)]
            for t in range(CBLK_DEV // 2)
        ],
        axis=0,
    )
    pair = pick_rows(pick_flux_ref[...], flux)
    odd = (target_ref[...].astype(jnp.int32) & 1) == 1
    x = jnp.where(odd != low(pair.shape), pair, half_swap(pair))
    x_ref[...] = x
    m_ref[...] = forward(g_ref, obs_ref, x, x_scr, sums)


def first_adjoint(parts, *refs):
    observed_ref, weight_ref, slot_obs_ref, index_ref, h_ref, message_ref, d_ref = refs[parts:]
    d = weight_ref[...] * (tree_sum([m[...] for m in refs[:parts]]) - observed_ref[...])
    d_ref[...] = d
    rows = h_ref.shape[3] // 2
    half = h_ref.shape[2] * rows

    def store(o, block):
        message_ref[o * rows : (o + 1) * rows, :] = block

    adjoint(h_ref, slot_obs_ref[...], d, store)
    message_ref[half:, :] = index_ref[...]


def second_model(parts, *refs):
    messages = refs[:parts]
    cells = parts
    target_ref, x_ref, g_ref, obs_ref, m_ref, x_scr, *sums = refs[parts:]
    slots = target_ref.shape[0]
    half = slots // 2
    count = max(1, half // LANES)
    group = max(1, min(cells, LANES // half))
    total = None
    for first in range(0, cells, group):
        members = messages[first : first + group]
        picks = []
        for part in range(2):
            rows = []
            for q in range(count):
                at = half + part * count + q
                row = jnp.zeros((1, LANES), F32)
                for k, ref in enumerate(members):
                    row = jnp.where(iota((1, LANES), 1) // half % group == k, ref[at : at + 1, :], row)
                rows.append(one_hot(target_ref[...] == row))
            picks.append(jnp.concatenate(rows, axis=1)[:, : group * half])
        pick = jnp.concatenate(picks, axis=0)
        values = jnp.concatenate([ref[:half, :] for ref in members], axis=0)
        found = pick_rows(jnp.concatenate([pick] * 3, axis=1), values)
        total = found if total is None else total + found
    change = jnp.where(low((slots, LANES)), total[:slots], total[slots:])
    x = x_ref[...] - 0.5 * (change + half_swap(change))
    m_ref[...] = forward(g_ref, obs_ref, x, x_scr, sums)


def second_adjoint(parts, *refs):
    observed_ref, weight_ref, first_ref, slot_obs_ref, h_ref = refs[parts : parts + 5]
    *outs, d_ref, block_scr = refs[parts + 5 :]
    me = lax.axis_index("cell")
    owners = h_ref.shape[2]
    d = weight_ref[...] * (tree_sum([m[...] for m in refs[:parts]]) - observed_ref[...])
    d_ref[...] = d

    def store(o, block):
        block_scr[o] = block

    adjoint(h_ref, slot_obs_ref[...], -0.25 * first_ref[...] - 0.5 * d, store)
    for k in range(owners):
        outs[owners - 1 - k][...] = block_scr[me ^ k]


def prepare_increment(parts, rows, *refs):
    d_ref, pick_ref, departure_ref = refs[parts:]
    messages = refs[:parts]
    cells = parts
    me = lax.axis_index("cell")
    half = cells * rows
    count = max(1, half // LANES)
    place = me * rows
    lane = iota((1, LANES), 1)
    row = iota((BLOCKS, LANES), 0)
    block = me * BLOCKS + (row % WIN_DEV) * CBLK_DEV + 2 * ((row // WIN_DEV) % 4) + row // (BLOCKS // 2)
    block = block.astype(F32)
    for part in range(2):
        for first in range(0, half, LANES):
            index = jnp.zeros((1, LANES), F32)
            for k in range(first // rows, min(cells, (first + LANES) // rows)):
                turned = pltpu.roll(
                    messages[k][half:, :], lax.rem(k * rows - place % LANES + 2 * LANES - first, LANES), 1
                )
                chosen = turned[part * count : part * count + 1]
                for q in range(1, count):
                    chosen = jnp.where(
                        place // LANES == q, turned[part * count + q : part * count + q + 1], chosen
                    )
                index = jnp.where((lane // rows) % cells == k - first // rows, chosen, index)
            pick_ref[BLOCKS * part : BLOCKS * (part + 1), first : first + LANES] = one_hot(block == index)
    for t in range(OBLK_DEV // 2):
        departure_ref[:, LANES * t : LANES * (t + 1)] = jnp.where(
            low((1, LANES)), d_ref[2 * t : 2 * t + 1, :], d_ref[2 * t + 1 : 2 * t + 2, :]
        )


def gather_increment(*refs):
    *arrays, pick_ref, out_ref = refs
    values = jnp.concatenate([ref[...] for ref in arrays[::-1]], axis=0)
    half = values.shape[0]
    terms = three(values)
    pick = pick_ref[...]
    if 3 * half <= LANES:
        terms.append(jnp.zeros((LANES - 3 * half, LANES), BF16))
    else:
        pick = jnp.concatenate([pick[:, :half]] * 3, axis=1)
    found = jnp.dot(pick, jnp.concatenate(terms, axis=0), preferred_element_type=F32)
    found = jnp.where(low((BLOCKS, LANES)), found[:BLOCKS], found[BLOCKS:])
    found = found + half_swap(found)
    for t in range(CBLK_DEV // 2):
        even = found[WIN_DEV * t : WIN_DEV * (t + 1)]
        odd = found[BLOCKS // 2 + WIN_DEV * t : BLOCKS // 2 + WIN_DEV * (t + 1)]
        out_ref[:, LANES * t : LANES * (t + 1)] = jnp.where(low(even.shape), even, odd)


def send(value, axis, size, k):
    return lax.ppermute(value, axis, [(i, i ^ k) for i in range(size)])


def exchange(own, sent, axis, size):
    return [own] + [send(sent, axis, size, k) for k in range(size - 1, 0, -1)][::-1]


def make_local(cells, wins):
    def local(prior_flux, observed, obs_weight, footprint, flux_slot, obs_slot, slot_count):
        owners, capacity = footprint.shape[2:4]
        slots = owners * capacity
        half = slots // 2
        index_rows = -(-2 * max(1, half // LANES) // 8) * 8
        params = pltpu.CompilerParams(vmem_limit_bytes=footprint.size * 4 + 16 * 2**20)
        hbm = pl.BlockSpec(memory_space=pltpu.HBM)
        smem = pl.BlockSpec(memory_space=pltpu.SMEM)
        obs, obs_out = None, pltpu.SMEM((slots,), jnp.int32)

        def call(body, outs, ins, scratch=(), space=VMEM):
            if space is hbm:
                ins = [pltpu.with_memory_space_constraint(value, pltpu.HBM) for value in ins]
                outs_at = [pltpu.VMEM(s, t) for s, t in outs[:-1]] + [obs_out]
            else:
                outs_at = [jax.ShapeDtypeStruct(s, t) for s, t in outs]
            return pl.pallas_call(
                body,
                out_shape=outs_at,
                in_specs=[smem if value is obs else space for value in ins],
                out_specs=[smem if outs_at[n] is obs_out else VMEM for n in range(len(outs))],
                scratch_shapes=list(scratch),
                compiler_params=params,
            )(*ins)

        def like(value):
            return (value.shape, value.dtype)

        obs_tile = ((OBLK_DEV, LANES), F32)
        slot_tile = ((slots, LANES), F32)
        sum_scratch = [pltpu.VMEM(*slot_tile)] + [pltpu.VMEM((OBLK_DEV + 1, TILES, LANES), F32)] * 4
        small = (flux_slot, obs_slot, slot_count, observed, obs_weight)
        turned = footprint.reshape(slots // 8, 8, TILES, LANES).transpose(0, 2, 1, 3)
        pick_flux, target, slot_obs, index, observed_t, weight_t, flux, matrices, by_slot, obs = call(
            prepare,
            [
                ((slots, 3 * owners * BLOCKS // 2), BF16),
                slot_tile,
                ((slots, 3 * OBLK_DEV), BF16),
                ((index_rows, LANES), F32),
                obs_tile,
                obs_tile,
                like(prior_flux),
                like(footprint),
                ((slots, TILES, LANES), F32),
                ((slots,), jnp.int32),
            ],
            (*small, prior_flux, footprint, turned),
            [
                *(pltpu.VMEM(*like(value)) for value in small),
                pltpu.SMEM(*like(obs_slot)),
                pltpu.SMEM(*like(slot_count)),
                pltpu.SemaphoreType.DMA((len(small) + 3,)),
                pltpu.SemaphoreType.DMA((owners,)),
                pltpu.SemaphoreType.DMA((slots,)),
            ],
            hbm,
        )
        order = [0, cells // 2, *range(1, cells // 2), *range(cells // 2 + 1, cells)]
        fluxes = exchange(flux, prior_flux, "cell", cells)
        m0, x0 = call(
            functools.partial(first_model, order),
            [obs_tile, slot_tile],
            (*(fluxes[k] for k in order), by_slot, pick_flux, target, obs),
            sum_scratch,
        )
        message, d0 = call(
            functools.partial(first_adjoint, wins),
            [((half + index_rows, LANES), F32), obs_tile],
            (*exchange(m0, m0, "win", wins), observed_t, weight_t, slot_obs, index, matrices),
        )
        messages = exchange(message, message, "cell", cells)
        (m1,) = call(
            functools.partial(second_model, cells),
            [obs_tile],
            (*messages, target, x0, by_slot, obs),
            sum_scratch,
        )
        *blocks, d1 = call(
            functools.partial(second_adjoint, wins),
            [((capacity // 2, LANES), F32)] * owners + [obs_tile],
            (*exchange(m1, m1, "win", wins), observed_t, weight_t, d0, slot_obs, matrices),
            [pltpu.VMEM((owners, capacity // 2, LANES), F32)],
        )
        arrays = [send(block, "cell", cells, cells - 1 - i) for i, block in enumerate(blocks[:-1])]
        arrays = [blocks[-1]] + arrays[::-1]
        pick, departure = call(
            functools.partial(prepare_increment, cells, capacity // 2),
            [((2 * BLOCKS, max(LANES, half)), BF16), ((1, OBLK_DEV * OB), F32)],
            (*messages, d1),
        )
        (increment,) = call(
            gather_increment,
            [((WIN_DEV, CBLK_DEV * CB), F32)],
            (*arrays[::-1], pick),
        )
        return increment, departure

    return local


def solution(mesh):
    placed = (
        P(("ens", "win"), "cell"),
        P(("ens", "cell"), None),
        P(("ens", "cell"), None),
        P("cell", "win", None, None, None),
        P("cell", "win", None, None),
        P("cell", "win", None, None),
        P("cell", "win", None),
    )
    return jax.shard_map(
        make_local(mesh.shape["cell"], mesh.shape["win"]),
        mesh=mesh,
        in_specs=placed,
        out_specs=(P(("ens", "win"), "cell"), P(("ens", "cell"), None)),
        check_vma=False,
    )
```

```python
import functools
import jax
import jax.numpy as jnp
from jax import lax
from jax.experimental import pallas as pl
from jax.experimental.pallas import tpu as pltpu
from jax.sharding import PartitionSpec as P

CB = 64
OB = 64
CBLK_DEV = 8
WIN_DEV = 8
OBLK_DEV = 8
BLOCKS = WIN_DEV * CBLK_DEV
LANES = 128
TILES = OB * CB // LANES

F32 = jnp.float32
BF16 = jnp.bfloat16
VMEM = pl.BlockSpec(memory_space=pltpu.VMEM)


def iota(shape, dim):
    return lax.broadcasted_iota(jnp.int32, shape, dim)


def one_hot(where):
    return jnp.where(where, 1.0, 0.0).astype(BF16)


def three(value):
    first = value.astype(BF16)
    rest = value - first.astype(F32)
    second = rest.astype(BF16)
    third = (rest - second.astype(F32)).astype(BF16)
    return [first, second, third]


def pick_rows(pick3, value):
    return jnp.dot(pick3, jnp.concatenate(three(value), axis=0), preferred_element_type=F32)


def swap(value, distance):
    return jnp.take_along_axis(
        value, iota(value.shape, 1) ^ distance, axis=1, mode="promise_in_bounds"
    )


def half_swap(value):
    return pltpu.roll(value, LANES // 2, 1)


def low(shape):
    return iota(shape, 1) < LANES // 2


def tree_sum(parts):
    parts = list(parts)
    while len(parts) > 1:
        parts = [sum(parts[i + 1 : i + 2], parts[i]) for i in range(0, len(parts), 2)]
    return parts[0]


def pack_obs(row):
    lane = iota((8, LANES), 1)
    block = (lane >> 1) & 31
    place = 16 * (block & 7) + 2 * iota(lane.shape, 0) + (lane >> 6)
    out = jnp.zeros(lane.shape, F32)
    for t in range(OBLK_DEV // 2):
        tile = jnp.broadcast_to(row[:, LANES * t : LANES * (t + 1)], lane.shape)
        found = jnp.take_along_axis(tile, place, axis=1, mode="promise_in_bounds")
        out = jnp.where(block >> 3 == t, found, out)
    return out


def unpack_obs(packed, t):
    lane = iota(packed.shape, 1)
    place = (lane & 1) * OB + 2 * (8 * t + (lane >> 4))
    found = jnp.take_along_axis(packed, place, axis=1, mode="promise_in_bounds")
    here = (lane & 15) >> 1 == iota(packed.shape, 0)
    return jnp.sum(jnp.where(here, found, 0.0), axis=0, keepdims=True)


def merge_tree(tiles):
    distance = 2
    while len(tiles) > 1:
        clear = (iota(tiles[0].shape, 1) & distance) == 0
        tiles = [
            jnp.where(clear, a, b) + swap(jnp.where(clear, b, a), distance)
            for a, b in zip(tiles[::2], tiles[1::2])
        ]
        distance *= 2
    return tiles[0]


def h_columns(h_ref, first, last, start, size):
    return jnp.concatenate([h_ref[0, 0, o, :, start : start + size] for o in range(first, last)], axis=0)


def forward(g_ref, obs_ref, x, x_scr, sums):
    slots = x.shape[0]
    sets = len(sums)
    x_scr[...] = x
    for ref in sums:
        ref[...] = jnp.zeros(ref.shape, F32)

    def add(s, ref):
        block = obs_ref[s]
        ref[block] = ref[block] + g_ref[s] * x_scr[pl.ds(s, 1), :]

    def step(j, carry):
        for n, ref in enumerate(sums):
            add(n * (slots // sets) + j, ref)
        return carry

    lax.fori_loop(0, slots // sets, step, 0, unroll=min(slots // sets, 16))
    rows = OBLK_DEV * TILES // 8
    tiles = []
    for q in range(rows):
        at = (q // 4, slice(8 * (q % 4), 8 * (q % 4) + 8))
        tiles.append(tree_sum([ref[at] for ref in sums]))
    m = merge_tree(tiles)
    return m + swap(m, 1)


def adjoint(h_ref, slot_obs, d, store):
    owners, capacity = h_ref.shape[2], h_ref.shape[3]
    place = (iota(d.shape, 1) & OB) + 8 * iota(d.shape, 0)
    spread = jnp.concatenate(
        [
            jnp.take_along_axis(
                jnp.broadcast_to(d[t % 8 : t % 8 + 1], d.shape),
                place + 2 * (t // 8),
                axis=1,
                mode="promise_in_bounds",
            )
            for t in range(TILES)
        ],
        axis=1,
    )
    spread = jnp.concatenate([term.astype(F32) for term in three(spread)], axis=0).astype(BF16)
    group = min(owners, 4)
    for first in range(0, owners, group):
        rows = slice(first * capacity, (first + group) * capacity)
        total = None
        for t in range(TILES // 2):
            columns = slice(2 * LANES * t, 2 * LANES * (t + 1))
            given = jnp.dot(slot_obs[rows], spread[:, columns], preferred_element_type=F32)
            terms = h_columns(h_ref, first, first + group, 2 * LANES * t, 2 * LANES) * given
            total = terms if total is None else total + terms
        total = total[:, :LANES] + total[:, LANES:]
        total = total + half_swap(total)
        for o in range(group):
            upper_half = o * capacity + capacity // 2
            pair = total[o * capacity : upper_half], total[upper_half : (o + 1) * capacity]
            store(first + o, jnp.where(low(pair[0].shape), *pair))


def prepare(
    fslot_hbm, oslot_hbm, count_hbm, observed_hbm, weight_hbm, flux_hbm, h_hbm, g_hbm,
    pick_flux_ref, target_ref, slot_obs_ref, index_ref, observed_out, weight_out, flux_ref, h_ref, g_ref, obs_ref,
    fslot_ref, oslot_ref, count_ref, observed_ref, weight_ref, oslot_scalars, count_scalars, sems, h_sems, g_sems,
):
    me = lax.axis_index("cell")
    owners, capacity = fslot_ref.shape[2:]
    pairs = (
        (fslot_hbm, fslot_ref),
        (oslot_hbm, oslot_ref),
        (count_hbm, count_ref),
        (observed_hbm, observed_ref),
        (weight_hbm, weight_ref),
        (flux_hbm, flux_ref),
        (oslot_hbm, oslot_scalars),
        (count_hbm, count_scalars),
    )
    small = [pltpu.make_async_copy(src, dst, sems.at[i]) for i, (src, dst) in enumerate(pairs)]
    large = [
        pltpu.make_async_copy(h_hbm.at[:, :, o], h_ref.at[:, :, o], h_sems.at[o])
        for o in range(owners)
    ]
    for copy in small + large:
        copy.start()

    def turned(n, r):
        return pltpu.make_async_copy(g_hbm.at[n, :, r], g_ref.at[8 * n + r], g_sems.at[8 * n + r])

    def each_turned(action):
        def step(n, carry):
            for r in range(8):
                action(turned(n, r))
            return carry

        lax.fori_loop(0, owners * capacity // 8, step, 0, unroll=owners <= 4)

    each_turned(lambda copy: copy.start())
    for copy in small:
        copy.wait()

    def scalar_step(o, carry):
        for j in range(capacity):
            obs_ref[o * capacity + j] = jnp.where(
                j < count_scalars[0, 0, o], oslot_scalars[0, 0, o, j], OBLK_DEV
            )
        return carry

    lax.fori_loop(0, owners, scalar_step, 0, unroll=owners <= 4)
    slots = owners * capacity
    eye = iota((capacity, capacity), 0) == iota((capacity, capacity), 1)

    def column(ref):
        return jnp.concatenate(
            [
                jnp.sum(
                    jnp.where(eye, jnp.broadcast_to(ref[0, 0, o : o + 1, :], eye.shape), 0),
                    axis=1,
                    keepdims=True,
                )
                for o in range(owners)
            ],
            axis=0,
        )

    fslot, oslot = column(fslot_ref), column(oslot_ref)
    counts = jnp.concatenate(
        [
            jnp.broadcast_to(count_ref[0, 0:1, o : o + 1], (capacity, 1))
            for o in range(owners)
        ],
        axis=0,
    )
    slot = iota((slots, 1), 0)
    owner = slot // capacity
    live = (slot - owner * capacity) < counts
    oslot = jnp.where(live, oslot, OBLK_DEV)
    target = owner * BLOCKS + fslot
    target_ref[...] = jnp.broadcast_to(target.astype(F32), target_ref.shape)

    depth = owners * BLOCKS // 2
    row = (owner ^ me) * (BLOCKS // 2) + ((fslot & 7) >> 1) * WIN_DEV + (fslot >> 3)
    pick_flux_ref[...] = one_hot(iota((slots, 3 * depth), 1) % depth == row)
    slot_obs_ref[...] = one_hot((iota((slots, 3 * OBLK_DEV), 1) % OBLK_DEV) == oslot)

    half = slots // 2
    count = max(1, half // LANES)
    index_ref[...] = jnp.zeros(index_ref.shape, F32)
    for part in range(2):
        for q in range(count):
            r = (iota((slots, LANES), 1) + LANES * q) % half
            at = (r // (capacity // 2)) * capacity + r % (capacity // 2) + part * (capacity // 2)
            index_ref[pl.ds(part * count + q, 1), :] = jnp.sum(
                jnp.where(iota((slots, LANES), 0) == at, target.astype(F32), 0.0),
                axis=0,
                keepdims=True,
            )
    observed_out[...] = pack_obs(observed_ref[...])
    weight_out[...] = pack_obs(weight_ref[...])
    for copy in large:
        copy.wait()
    each_turned(lambda copy: copy.wait())


def first_model(order, *refs):
    parts = len(order)
    g_ref, pick_flux_ref, target_ref, obs_ref, m_ref, x_ref, x_scr, *sums = refs[parts:]
    flux = jnp.concatenate(
        [
            ref[:, LANES * t : LANES * (t + 1)]
            for ref in [refs[order.index(k)] for k in range(parts)]
            for t in range(CBLK_DEV // 2)
        ],
        axis=0,
    )
    pair = pick_rows(pick_flux_ref[...], flux)
    odd = (target_ref[...].astype(jnp.int32) & 1) == 1
    x = jnp.where(odd != low(pair.shape), pair, half_swap(pair))
    x_ref[...] = x
    m_ref[...] = forward(g_ref, obs_ref, x, x_scr, sums)


def first_adjoint(parts, *refs):
    observed_ref, weight_ref, slot_obs_ref, index_ref, h_ref, message_ref, d_ref = refs[parts:]
    d = weight_ref[...] * (tree_sum([m[...] for m in refs[:parts]]) - observed_ref[...])
    d_ref[...] = d
    rows = h_ref.shape[3] // 2
    half = h_ref.shape[2] * rows

    def store(o, block):
        message_ref[o * rows : (o + 1) * rows, :] = block

    adjoint(h_ref, slot_obs_ref[...], d, store)
    message_ref[half:, :] = index_ref[...]


def second_model(parts, *refs):
    messages = refs[:parts]
    cells = parts
    target_ref, x_ref, g_ref, obs_ref, m_ref, x_scr, *sums = refs[parts:]
    slots = target_ref.shape[0]
    half = slots // 2
    count = max(1, half // LANES)
    group = max(1, min(cells, LANES // half))
    total = None
    for first in range(0, cells, group):
        members = messages[first : first + group]
        picks = []
        for part in range(2):
            rows = []
            for q in range(count):
                at = half + part * count + q
                row = jnp.zeros((1, LANES), F32)
                for k, ref in enumerate(members):
                    row = jnp.where(iota((1, LANES), 1) // half % group == k, ref[at : at + 1, :], row)
                rows.append(one_hot(target_ref[...] == row))
            picks.append(jnp.concatenate(rows, axis=1)[:, : group * half])
        pick = jnp.concatenate(picks, axis=0)
        values = jnp.concatenate([ref[:half, :] for ref in members], axis=0)
        found = pick_rows(jnp.concatenate([pick] * 3, axis=1), values)
        total = found if total is None else total + found
    change = jnp.where(low((slots, LANES)), total[:slots], total[slots:])
    x = x_ref[...] - 0.5 * (change + half_swap(change))
    m_ref[...] = forward(g_ref, obs_ref, x, x_scr, sums)


def second_adjoint(parts, *refs):
    observed_ref, weight_ref, first_ref, slot_obs_ref, h_ref = refs[parts : parts + 5]
    *outs, d_ref, block_scr = refs[parts + 5 :]
    me = lax.axis_index("cell")
    owners = h_ref.shape[2]
    d = weight_ref[...] * (tree_sum([m[...] for m in refs[:parts]]) - observed_ref[...])
    d_ref[...] = d

    def store(o, block):
        block_scr[o] = block

    adjoint(h_ref, slot_obs_ref[...], -0.25 * first_ref[...] - 0.5 * d, store)
    for k in range(owners):
        outs[owners - 1 - k][...] = block_scr[me ^ k]


def prepare_increment(parts, rows, *refs):
    d_ref, pick_ref, departure_ref = refs[parts:]
    messages = refs[:parts]
    cells = parts
    me = lax.axis_index("cell")
    half = cells * rows
    count = max(1, half // LANES)
    place = me * rows
    lane = iota((1, LANES), 1)
    row = iota((BLOCKS, LANES), 0)
    block = me * BLOCKS + (row % WIN_DEV) * CBLK_DEV + 2 * ((row // WIN_DEV) % 4) + row // (BLOCKS // 2)
    block = block.astype(F32)
    for part in range(2):
        for first in range(0, half, LANES):
            index = jnp.zeros((1, LANES), F32)
            for k in range(first // rows, min(cells, (first + LANES) // rows)):
                turned = pltpu.roll(
                    messages[k][half:, :], lax.rem(k * rows - place % LANES + 2 * LANES - first, LANES), 1
                )
                chosen = turned[part * count : part * count + 1]
                for q in range(1, count):
                    chosen = jnp.where(
                        place // LANES == q, turned[part * count + q : part * count + q + 1], chosen
                    )
                index = jnp.where((lane // rows) % cells == k - first // rows, chosen, index)
            pick_ref[BLOCKS * part : BLOCKS * (part + 1), first : first + LANES] = one_hot(block == index)
    for t in range(OBLK_DEV // 2):
        departure_ref[:, LANES * t : LANES * (t + 1)] = unpack_obs(d_ref[...], t)


def gather_increment(*refs):
    *arrays, pick_ref, out_ref = refs
    values = jnp.concatenate([ref[...] for ref in arrays[::-1]], axis=0)
    half = values.shape[0]
    terms = three(values)
    pick = pick_ref[...]
    if 3 * half <= LANES:
        terms.append(jnp.zeros((LANES - 3 * half, LANES), BF16))
    else:
        pick = jnp.concatenate([pick[:, :half]] * 3, axis=1)
    found = jnp.dot(pick, jnp.concatenate(terms, axis=0), preferred_element_type=F32)
    found = jnp.where(low((BLOCKS, LANES)), found[:BLOCKS], found[BLOCKS:])
    found = found + half_swap(found)
    for t in range(CBLK_DEV // 2):
        even = found[WIN_DEV * t : WIN_DEV * (t + 1)]
        odd = found[BLOCKS // 2 + WIN_DEV * t : BLOCKS // 2 + WIN_DEV * (t + 1)]
        out_ref[:, LANES * t : LANES * (t + 1)] = jnp.where(low(even.shape), even, odd)


def send(value, axis, size, k):
    return lax.ppermute(value, axis, [(i, i ^ k) for i in range(size)])


def exchange(own, sent, axis, size):
    return [own] + [send(sent, axis, size, k) for k in range(size - 1, 0, -1)][::-1]


def make_local(cells, wins):
    def local(prior_flux, observed, obs_weight, footprint, flux_slot, obs_slot, slot_count):
        owners, capacity = footprint.shape[2:4]
        slots = owners * capacity
        half = slots // 2
        index_rows = -(-2 * max(1, half // LANES) // 8) * 8
        params = pltpu.CompilerParams(vmem_limit_bytes=footprint.size * 4 + 16 * 2**20)
        hbm = pl.BlockSpec(memory_space=pltpu.HBM)
        smem = pl.BlockSpec(memory_space=pltpu.SMEM)
        obs, obs_out = None, pltpu.SMEM((slots,), jnp.int32)

        def call(body, outs, ins, scratch=(), space=VMEM):
            if space is hbm:
                ins = [pltpu.with_memory_space_constraint(value, pltpu.HBM) for value in ins]
                outs_at = [pltpu.VMEM(s, t) for s, t in outs[:-1]] + [obs_out]
            else:
                outs_at = [jax.ShapeDtypeStruct(s, t) for s, t in outs]
            return pl.pallas_call(
                body,
                out_shape=outs_at,
                in_specs=[smem if value is obs else space for value in ins],
                out_specs=[smem if outs_at[n] is obs_out else VMEM for n in range(len(outs))],
                scratch_shapes=list(scratch),
                compiler_params=params,
            )(*ins)

        def like(value):
            return (value.shape, value.dtype)

        obs_tile = ((OBLK_DEV, LANES), F32)
        slot_tile = ((slots, LANES), F32)
        sum_scratch = [pltpu.VMEM(*slot_tile)] + [pltpu.VMEM((OBLK_DEV + 1, TILES, LANES), F32)] * 4
        small = (flux_slot, obs_slot, slot_count, observed, obs_weight)
        turned = footprint.reshape(slots // 8, 8, TILES, LANES).transpose(0, 2, 1, 3)
        pick_flux, target, slot_obs, index, observed_t, weight_t, flux, matrices, by_slot, obs = call(
            prepare,
            [
                ((slots, 3 * owners * BLOCKS // 2), BF16),
                slot_tile,
                ((slots, 3 * OBLK_DEV), BF16),
                ((index_rows, LANES), F32),
                obs_tile,
                obs_tile,
                like(prior_flux),
                like(footprint),
                ((slots, TILES, LANES), F32),
                ((slots,), jnp.int32),
            ],
            (*small, prior_flux, footprint, turned),
            [
                *(pltpu.VMEM(*like(value)) for value in small),
                pltpu.SMEM(*like(obs_slot)),
                pltpu.SMEM(*like(slot_count)),
                pltpu.SemaphoreType.DMA((len(small) + 3,)),
                pltpu.SemaphoreType.DMA((owners,)),
                pltpu.SemaphoreType.DMA((slots,)),
            ],
            hbm,
        )
        order = [0, cells // 2, *range(1, cells // 2), *range(cells // 2 + 1, cells)]
        fluxes = exchange(flux, prior_flux, "cell", cells)
        m0, x0 = call(
            functools.partial(first_model, order),
            [obs_tile, slot_tile],
            (*(fluxes[k] for k in order), by_slot, pick_flux, target, obs),
            sum_scratch,
        )
        message, d0 = call(
            functools.partial(first_adjoint, wins),
            [((half + index_rows, LANES), F32), obs_tile],
            (*exchange(m0, m0, "win", wins), observed_t, weight_t, slot_obs, index, matrices),
        )
        messages = exchange(message, message, "cell", cells)
        (m1,) = call(
            functools.partial(second_model, cells),
            [obs_tile],
            (*messages, target, x0, by_slot, obs),
            sum_scratch,
        )
        *blocks, d1 = call(
            functools.partial(second_adjoint, wins),
            [((capacity // 2, LANES), F32)] * owners + [obs_tile],
            (*exchange(m1, m1, "win", wins), observed_t, weight_t, d0, slot_obs, matrices),
            [pltpu.VMEM((owners, capacity // 2, LANES), F32)],
        )
        arrays = [send(block, "cell", cells, cells - 1 - i) for i, block in enumerate(blocks[:-1])]
        arrays = [blocks[-1]] + arrays[::-1]
        pick, departure = call(
            functools.partial(prepare_increment, cells, capacity // 2),
            [((2 * BLOCKS, max(LANES, half)), BF16), ((1, OBLK_DEV * OB), F32)],
            (*messages, d1),
        )
        (increment,) = call(
            gather_increment,
            [((WIN_DEV, CBLK_DEV * CB), F32)],
            (*arrays[::-1], pick),
        )
        return increment, departure

    return local


def solution(mesh):
    placed = (
        P(("ens", "win"), "cell"),
        P(("ens", "cell"), None),
        P(("ens", "cell"), None),
        P("cell", "win", None, None, None),
        P("cell", "win", None, None),
        P("cell", "win", None, None),
        P("cell", "win", None),
    )
    return jax.shard_map(
        make_local(mesh.shape["cell"], mesh.shape["win"]),
        mesh=mesh,
        in_specs=placed,
        out_specs=(P(("ens", "win"), "cell"), P(("ens", "cell"), None)),
        check_vma=False,
    )
```

```python
import functools
import jax
import jax.numpy as jnp
from jax import lax
from jax.experimental import pallas as pl
from jax.experimental.pallas import tpu as pltpu
from jax.sharding import PartitionSpec as P

CB = 64
OB = 64
CBLK_DEV = 8
WIN_DEV = 8
OBLK_DEV = 8
BLOCKS = WIN_DEV * CBLK_DEV
LANES = 128
TILES = OB * CB // LANES

F32 = jnp.float32
BF16 = jnp.bfloat16
VMEM = pl.BlockSpec(memory_space=pltpu.VMEM)


def iota(shape, dim):
    return lax.broadcasted_iota(jnp.int32, shape, dim)


def one_hot(where):
    return jnp.where(where, 1.0, 0.0).astype(BF16)


def three(value):
    first = value.astype(BF16)
    rest = value - first.astype(F32)
    second = rest.astype(BF16)
    third = (rest - second.astype(F32)).astype(BF16)
    return [first, second, third]


def pick_rows(pick3, value):
    return jnp.dot(pick3, jnp.concatenate(three(value), axis=0), preferred_element_type=F32)


def swap(value, distance):
    return jnp.take_along_axis(
        value, iota(value.shape, 1) ^ distance, axis=1, mode="promise_in_bounds"
    )


def half_swap(value):
    return pltpu.roll(value, LANES // 2, 1)


def low(shape):
    return iota(shape, 1) < LANES // 2


def tree_sum(parts):
    parts = list(parts)
    while len(parts) > 1:
        parts = [sum(parts[i + 1 : i + 2], parts[i]) for i in range(0, len(parts), 2)]
    return parts[0]


def pack_obs(row):
    lane = iota((8, LANES), 1)
    block = (lane >> 1) & 31
    place = 16 * (block & 7) + 2 * iota(lane.shape, 0) + (lane >> 6)
    out = jnp.zeros(lane.shape, F32)
    for t in range(OBLK_DEV // 2):
        tile = jnp.broadcast_to(row[:, LANES * t : LANES * (t + 1)], lane.shape)
        found = jnp.take_along_axis(tile, place, axis=1, mode="promise_in_bounds")
        out = jnp.where(block >> 3 == t, found, out)
    return out


def unpack_obs(packed, t):
    lane = iota(packed.shape, 1)
    place = (lane & 1) * OB + 2 * (8 * t + (lane >> 4))
    found = jnp.take_along_axis(packed, place, axis=1, mode="promise_in_bounds")
    here = (lane & 15) >> 1 == iota(packed.shape, 0)
    return jnp.sum(jnp.where(here, found, 0.0), axis=0, keepdims=True)


def merge_tree(tiles):
    distance = 2
    while len(tiles) > 1:
        clear = (iota(tiles[0].shape, 1) & distance) == 0
        tiles = [
            jnp.where(clear, a, b) + swap(jnp.where(clear, b, a), distance)
            for a, b in zip(tiles[::2], tiles[1::2])
        ]
        distance *= 2
    return tiles[0]


def h_columns(h_ref, first, last, start, size):
    return jnp.concatenate([h_ref[0, 0, o, :, start : start + size] for o in range(first, last)], axis=0)


def forward(g_ref, obs_ref, x, x_scr, sums):
    slots = x.shape[0]
    sets = len(sums)
    x_scr[...] = x
    for ref in sums:
        ref[...] = jnp.zeros(ref.shape, F32)

    steps = slots // sets
    run = min(steps, 16)

    def products(j):
        at = [n * steps + j for n in range(sets)]
        return [(obs_ref[s], g_ref[s] * x_scr[pl.ds(s, 1), :]) for s in at]

    def step(first, carry):
        coming = products(first * run)
        for j in range(run):
            now = coming
            totals = [ref[block] + value for ref, (block, value) in zip(sums, now)]
            if j + 1 < run:
                coming = products(first * run + j + 1)
            for ref, (block, _), total in zip(sums, now, totals):
                ref[block] = total
        return carry

    lax.fori_loop(0, steps // run, step, 0)
    rows = OBLK_DEV * TILES // 8
    tiles = []
    for q in range(rows):
        at = (q // 4, slice(8 * (q % 4), 8 * (q % 4) + 8))
        tiles.append(tree_sum([ref[at] for ref in sums]))
    m = merge_tree(tiles)
    return m + swap(m, 1)


def adjoint(h_ref, slot_obs, d, store):
    owners, capacity = h_ref.shape[2], h_ref.shape[3]
    place = (iota(d.shape, 1) & OB) + 8 * iota(d.shape, 0)
    spread = jnp.concatenate(
        [
            jnp.take_along_axis(
                jnp.broadcast_to(d[t % 8 : t % 8 + 1], d.shape),
                place + 2 * (t // 8),
                axis=1,
                mode="promise_in_bounds",
            )
            for t in range(TILES)
        ],
        axis=1,
    )
    spread = jnp.concatenate([term.astype(F32) for term in three(spread)], axis=0).astype(BF16)
    group = min(owners, 4)
    for first in range(0, owners, group):
        rows = slice(first * capacity, (first + group) * capacity)
        total = None
        for t in range(TILES // 2):
            columns = slice(2 * LANES * t, 2 * LANES * (t + 1))
            given = jnp.dot(slot_obs[rows], spread[:, columns], preferred_element_type=F32)
            terms = h_columns(h_ref, first, first + group, 2 * LANES * t, 2 * LANES) * given
            total = terms if total is None else total + terms
        total = total[:, :LANES] + total[:, LANES:]
        total = total + half_swap(total)
        for o in range(group):
            upper_half = o * capacity + capacity // 2
            pair = total[o * capacity : upper_half], total[upper_half : (o + 1) * capacity]
            store(first + o, jnp.where(low(pair[0].shape), *pair))


def prepare(
    fslot_hbm, oslot_hbm, count_hbm, observed_hbm, weight_hbm, flux_hbm, h_hbm, g_hbm,
    pick_flux_ref, target_ref, slot_obs_ref, index_ref, observed_out, weight_out, flux_ref, h_ref, g_ref, obs_ref,
    fslot_ref, oslot_ref, count_ref, observed_ref, weight_ref, oslot_scalars, count_scalars, sems, h_sems, g_sems,
):
    me = lax.axis_index("cell")
    owners, capacity = fslot_ref.shape[2:]
    pairs = (
        (fslot_hbm, fslot_ref),
        (oslot_hbm, oslot_ref),
        (count_hbm, count_ref),
        (observed_hbm, observed_ref),
        (weight_hbm, weight_ref),
        (flux_hbm, flux_ref),
        (oslot_hbm, oslot_scalars),
        (count_hbm, count_scalars),
    )
    small = [pltpu.make_async_copy(src, dst, sems.at[i]) for i, (src, dst) in enumerate(pairs)]
    large = [
        pltpu.make_async_copy(h_hbm.at[:, :, o], h_ref.at[:, :, o], h_sems.at[o])
        for o in range(owners)
    ]
    for copy in small + large:
        copy.start()

    def turned(n, r):
        return pltpu.make_async_copy(g_hbm.at[n, :, r], g_ref.at[8 * n + r], g_sems.at[8 * n + r])

    def each_turned(action):
        def step(n, carry):
            for r in range(8):
                action(turned(n, r))
            return carry

        lax.fori_loop(0, owners * capacity // 8, step, 0, unroll=owners <= 4)

    each_turned(lambda copy: copy.start())
    for copy in small:
        copy.wait()

    def scalar_step(o, carry):
        for j in range(capacity):
            obs_ref[o * capacity + j] = jnp.where(
                j < count_scalars[0, 0, o], oslot_scalars[0, 0, o, j], OBLK_DEV
            )
        return carry

    lax.fori_loop(0, owners, scalar_step, 0, unroll=owners <= 4)
    slots = owners * capacity
    eye = iota((capacity, capacity), 0) == iota((capacity, capacity), 1)

    def column(ref):
        return jnp.concatenate(
            [
                jnp.sum(
                    jnp.where(eye, jnp.broadcast_to(ref[0, 0, o : o + 1, :], eye.shape), 0),
                    axis=1,
                    keepdims=True,
                )
                for o in range(owners)
            ],
            axis=0,
        )

    fslot, oslot = column(fslot_ref), column(oslot_ref)
    counts = jnp.concatenate(
        [
            jnp.broadcast_to(count_ref[0, 0:1, o : o + 1], (capacity, 1))
            for o in range(owners)
        ],
        axis=0,
    )
    slot = iota((slots, 1), 0)
    owner = slot // capacity
    live = (slot - owner * capacity) < counts
    oslot = jnp.where(live, oslot, OBLK_DEV)
    target = owner * BLOCKS + fslot
    target_ref[...] = jnp.broadcast_to(target.astype(F32), target_ref.shape)

    depth = owners * BLOCKS // 2
    row = (owner ^ me) * (BLOCKS // 2) + ((fslot & 7) >> 1) * WIN_DEV + (fslot >> 3)
    pick_flux_ref[...] = one_hot(iota((slots, 3 * depth), 1) % depth == row)
    slot_obs_ref[...] = one_hot((iota((slots, 3 * OBLK_DEV), 1) % OBLK_DEV) == oslot)

    half = slots // 2
    count = max(1, half // LANES)
    index_ref[...] = jnp.zeros(index_ref.shape, F32)
    for part in range(2):
        for q in range(count):
            r = (iota((slots, LANES), 1) + LANES * q) % half
            at = (r // (capacity // 2)) * capacity + r % (capacity // 2) + part * (capacity // 2)
            index_ref[pl.ds(part * count + q, 1), :] = jnp.sum(
                jnp.where(iota((slots, LANES), 0) == at, target.astype(F32), 0.0),
                axis=0,
                keepdims=True,
            )
    observed_out[...] = pack_obs(observed_ref[...])
    weight_out[...] = pack_obs(weight_ref[...])
    for copy in large:
        copy.wait()
    each_turned(lambda copy: copy.wait())


def first_model(order, *refs):
    parts = len(order)
    g_ref, pick_flux_ref, target_ref, obs_ref, m_ref, x_ref, x_scr, *sums = refs[parts:]
    flux = jnp.concatenate(
        [
            ref[:, LANES * t : LANES * (t + 1)]
            for ref in [refs[order.index(k)] for k in range(parts)]
            for t in range(CBLK_DEV // 2)
        ],
        axis=0,
    )
    pair = pick_rows(pick_flux_ref[...], flux)
    odd = (target_ref[...].astype(jnp.int32) & 1) == 1
    x = jnp.where(odd != low(pair.shape), pair, half_swap(pair))
    x_ref[...] = x
    m_ref[...] = forward(g_ref, obs_ref, x, x_scr, sums)


def first_adjoint(parts, *refs):
    observed_ref, weight_ref, slot_obs_ref, index_ref, h_ref, message_ref, d_ref = refs[parts:]
    d = weight_ref[...] * (tree_sum([m[...] for m in refs[:parts]]) - observed_ref[...])
    d_ref[...] = d
    rows = h_ref.shape[3] // 2
    half = h_ref.shape[2] * rows

    def store(o, block):
        message_ref[o * rows : (o + 1) * rows, :] = block

    adjoint(h_ref, slot_obs_ref[...], d, store)
    message_ref[half:, :] = index_ref[...]


def second_model(parts, *refs):
    messages = refs[:parts]
    cells = parts
    target_ref, x_ref, g_ref, obs_ref, m_ref, x_scr, *sums = refs[parts:]
    slots = target_ref.shape[0]
    half = slots // 2
    count = max(1, half // LANES)
    group = max(1, min(cells, LANES // half))
    total = None
    for first in range(0, cells, group):
        members = messages[first : first + group]
        picks = []
        for part in range(2):
            rows = []
            for q in range(count):
                at = half + part * count + q
                row = jnp.zeros((1, LANES), F32)
                for k, ref in enumerate(members):
                    row = jnp.where(iota((1, LANES), 1) // half % group == k, ref[at : at + 1, :], row)
                rows.append(one_hot(target_ref[...] == row))
            picks.append(jnp.concatenate(rows, axis=1)[:, : group * half])
        pick = jnp.concatenate(picks, axis=0)
        values = jnp.concatenate([ref[:half, :] for ref in members], axis=0)
        found = pick_rows(jnp.concatenate([pick] * 3, axis=1), values)
        total = found if total is None else total + found
    change = jnp.where(low((slots, LANES)), total[:slots], total[slots:])
    x = x_ref[...] - 0.5 * (change + half_swap(change))
    m_ref[...] = forward(g_ref, obs_ref, x, x_scr, sums)


def second_adjoint(parts, *refs):
    observed_ref, weight_ref, first_ref, slot_obs_ref, h_ref = refs[parts : parts + 5]
    *outs, d_ref, block_scr = refs[parts + 5 :]
    me = lax.axis_index("cell")
    owners = h_ref.shape[2]
    d = weight_ref[...] * (tree_sum([m[...] for m in refs[:parts]]) - observed_ref[...])
    d_ref[...] = d

    def store(o, block):
        block_scr[o] = block

    adjoint(h_ref, slot_obs_ref[...], -0.25 * first_ref[...] - 0.5 * d, store)
    for k in range(owners):
        outs[owners - 1 - k][...] = block_scr[me ^ k]


def prepare_increment(parts, rows, *refs):
    d_ref, pick_ref, departure_ref = refs[parts:]
    messages = refs[:parts]
    cells = parts
    me = lax.axis_index("cell")
    half = cells * rows
    count = max(1, half // LANES)
    place = me * rows
    lane = iota((1, LANES), 1)
    row = iota((BLOCKS, LANES), 0)
    block = me * BLOCKS + (row % WIN_DEV) * CBLK_DEV + 2 * ((row // WIN_DEV) % 4) + row // (BLOCKS // 2)
    block = block.astype(F32)
    for part in range(2):
        for first in range(0, half, LANES):
            index = jnp.zeros((1, LANES), F32)
            for k in range(first // rows, min(cells, (first + LANES) // rows)):
                turned = pltpu.roll(
                    messages[k][half:, :], lax.rem(k * rows - place % LANES + 2 * LANES - first, LANES), 1
                )
                chosen = turned[part * count : part * count + 1]
                for q in range(1, count):
                    chosen = jnp.where(
                        place // LANES == q, turned[part * count + q : part * count + q + 1], chosen
                    )
                index = jnp.where((lane // rows) % cells == k - first // rows, chosen, index)
            pick_ref[BLOCKS * part : BLOCKS * (part + 1), first : first + LANES] = one_hot(block == index)
    for t in range(OBLK_DEV // 2):
        departure_ref[:, LANES * t : LANES * (t + 1)] = unpack_obs(d_ref[...], t)


def gather_increment(*refs):
    *arrays, pick_ref, out_ref = refs
    values = jnp.concatenate([ref[...] for ref in arrays[::-1]], axis=0)
    half = values.shape[0]
    terms = three(values)
    pick = pick_ref[...]
    if 3 * half <= LANES:
        terms.append(jnp.zeros((LANES - 3 * half, LANES), BF16))
    else:
        pick = jnp.concatenate([pick[:, :half]] * 3, axis=1)
    found = jnp.dot(pick, jnp.concatenate(terms, axis=0), preferred_element_type=F32)
    found = jnp.where(low((BLOCKS, LANES)), found[:BLOCKS], found[BLOCKS:])
    found = found + half_swap(found)
    for t in range(CBLK_DEV // 2):
        even = found[WIN_DEV * t : WIN_DEV * (t + 1)]
        odd = found[BLOCKS // 2 + WIN_DEV * t : BLOCKS // 2 + WIN_DEV * (t + 1)]
        out_ref[:, LANES * t : LANES * (t + 1)] = jnp.where(low(even.shape), even, odd)


def send(value, axis, size, k):
    return lax.ppermute(value, axis, [(i, i ^ k) for i in range(size)])


def exchange(own, sent, axis, size):
    return [own] + [send(sent, axis, size, k) for k in range(size - 1, 0, -1)][::-1]


def make_local(cells, wins):
    def local(prior_flux, observed, obs_weight, footprint, flux_slot, obs_slot, slot_count):
        owners, capacity = footprint.shape[2:4]
        slots = owners * capacity
        half = slots // 2
        index_rows = -(-2 * max(1, half // LANES) // 8) * 8
        params = pltpu.CompilerParams(vmem_limit_bytes=footprint.size * 4 + 16 * 2**20)
        hbm = pl.BlockSpec(memory_space=pltpu.HBM)
        smem = pl.BlockSpec(memory_space=pltpu.SMEM)
        obs, obs_out = None, pltpu.SMEM((slots,), jnp.int32)

        def call(body, outs, ins, scratch=(), space=VMEM):
            if space is hbm:
                ins = [pltpu.with_memory_space_constraint(value, pltpu.HBM) for value in ins]
                outs_at = [pltpu.VMEM(s, t) for s, t in outs[:-1]] + [obs_out]
            else:
                outs_at = [jax.ShapeDtypeStruct(s, t) for s, t in outs]
            return pl.pallas_call(
                body,
                out_shape=outs_at,
                in_specs=[smem if value is obs else space for value in ins],
                out_specs=[smem if outs_at[n] is obs_out else VMEM for n in range(len(outs))],
                scratch_shapes=list(scratch),
                compiler_params=params,
            )(*ins)

        def like(value):
            return (value.shape, value.dtype)

        obs_tile = ((OBLK_DEV, LANES), F32)
        slot_tile = ((slots, LANES), F32)
        sum_scratch = [pltpu.VMEM(*slot_tile)] + [pltpu.VMEM((OBLK_DEV + 1, TILES, LANES), F32)] * 4
        small = (flux_slot, obs_slot, slot_count, observed, obs_weight)
        turned = footprint.reshape(slots // 8, 8, TILES, LANES).transpose(0, 2, 1, 3)
        pick_flux, target, slot_obs, index, observed_t, weight_t, flux, matrices, by_slot, obs = call(
            prepare,
            [
                ((slots, 3 * owners * BLOCKS // 2), BF16),
                slot_tile,
                ((slots, 3 * OBLK_DEV), BF16),
                ((index_rows, LANES), F32),
                obs_tile,
                obs_tile,
                like(prior_flux),
                like(footprint),
                ((slots, TILES, LANES), F32),
                ((slots,), jnp.int32),
            ],
            (*small, prior_flux, footprint, turned),
            [
                *(pltpu.VMEM(*like(value)) for value in small),
                pltpu.SMEM(*like(obs_slot)),
                pltpu.SMEM(*like(slot_count)),
                pltpu.SemaphoreType.DMA((len(small) + 3,)),
                pltpu.SemaphoreType.DMA((owners,)),
                pltpu.SemaphoreType.DMA((slots,)),
            ],
            hbm,
        )
        order = [0, cells // 2, *range(1, cells // 2), *range(cells // 2 + 1, cells)]
        fluxes = exchange(flux, prior_flux, "cell", cells)
        m0, x0 = call(
            functools.partial(first_model, order),
            [obs_tile, slot_tile],
            (*(fluxes[k] for k in order), by_slot, pick_flux, target, obs),
            sum_scratch,
        )
        message, d0 = call(
            functools.partial(first_adjoint, wins),
            [((half + index_rows, LANES), F32), obs_tile],
            (*exchange(m0, m0, "win", wins), observed_t, weight_t, slot_obs, index, matrices),
        )
        messages = exchange(message, message, "cell", cells)
        (m1,) = call(
            functools.partial(second_model, cells),
            [obs_tile],
            (*messages, target, x0, by_slot, obs),
            sum_scratch,
        )
        *blocks, d1 = call(
            functools.partial(second_adjoint, wins),
            [((capacity // 2, LANES), F32)] * owners + [obs_tile],
            (*exchange(m1, m1, "win", wins), observed_t, weight_t, d0, slot_obs, matrices),
            [pltpu.VMEM((owners, capacity // 2, LANES), F32)],
        )
        arrays = [send(block, "cell", cells, cells - 1 - i) for i, block in enumerate(blocks[:-1])]
        arrays = [blocks[-1]] + arrays[::-1]
        pick, departure = call(
            functools.partial(prepare_increment, cells, capacity // 2),
            [((2 * BLOCKS, max(LANES, half)), BF16), ((1, OBLK_DEV * OB), F32)],
            (*messages, d1),
        )
        (increment,) = call(
            gather_increment,
            [((WIN_DEV, CBLK_DEV * CB), F32)],
            (*arrays[::-1], pick),
        )
        return increment, departure

    return local


def solution(mesh):
    placed = (
        P(("ens", "win"), "cell"),
        P(("ens", "cell"), None),
        P(("ens", "cell"), None),
        P("cell", "win", None, None, None),
        P("cell", "win", None, None),
        P("cell", "win", None, None),
        P("cell", "win", None),
    )
    return jax.shard_map(
        make_local(mesh.shape["cell"], mesh.shape["win"]),
        mesh=mesh,
        in_specs=placed,
        out_specs=(P(("ens", "win"), "cell"), P(("ens", "cell"), None)),
        check_vma=False,
    )
```

```python
import functools
import jax
import jax.numpy as jnp
from jax import lax
from jax.experimental import pallas as pl
from jax.experimental.pallas import tpu as pltpu
from jax.sharding import PartitionSpec as P

CB = 64
OB = 64
CBLK_DEV = 8
WIN_DEV = 8
OBLK_DEV = 8
BLOCKS = WIN_DEV * CBLK_DEV
LANES = 128
TILES = OB * CB // LANES

F32 = jnp.float32
BF16 = jnp.bfloat16
VMEM = pl.BlockSpec(memory_space=pltpu.VMEM)


def iota(shape, dim):
    return lax.broadcasted_iota(jnp.int32, shape, dim)


def one_hot(where):
    return jnp.where(where, 1.0, 0.0).astype(BF16)


def three(value):
    first = value.astype(BF16)
    rest = value - first.astype(F32)
    second = rest.astype(BF16)
    third = (rest - second.astype(F32)).astype(BF16)
    return [first, second, third]


def pick_rows(pick3, value):
    return jnp.dot(pick3, jnp.concatenate(three(value), axis=0), preferred_element_type=F32)


def half_swap(value):
    return pltpu.roll(value, LANES // 2, 1)


def low(shape):
    return iota(shape, 1) < LANES // 2


def tree_sum(parts):
    parts = list(parts)
    while len(parts) > 1:
        parts = [sum(parts[i + 1 : i + 2], parts[i]) for i in range(0, len(parts), 2)]
    return parts[0]


def pack_obs(row):
    lane = iota((8, LANES), 1)
    block = (lane >> 1) & 31
    place = 16 * (block & 7) + 2 * iota(lane.shape, 0) + (lane >> 6)
    out = jnp.zeros(lane.shape, F32)
    for t in range(OBLK_DEV // 2):
        tile = jnp.broadcast_to(row[:, LANES * t : LANES * (t + 1)], lane.shape)
        found = jnp.take_along_axis(tile, place, axis=1, mode="promise_in_bounds")
        out = jnp.where(block >> 3 == t, found, out)
    return out


def unpack_obs(packed, t):
    lane = iota(packed.shape, 1)
    place = (lane & 1) * OB + 2 * (8 * t + (lane >> 4))
    found = jnp.take_along_axis(packed, place, axis=1, mode="promise_in_bounds")
    here = (lane & 15) >> 1 == iota(packed.shape, 0)
    return jnp.sum(jnp.where(here, found, 0.0), axis=0, keepdims=True)


def lane_sums(tiles):
    terms = jnp.concatenate(three(jnp.concatenate(tiles, axis=0)), axis=1)
    shape = (3 * LANES, LANES)
    ones = one_hot((iota(shape, 0) // OB) % 2 == iota(shape, 1) // OB)
    sums = jnp.dot(terms, ones, preferred_element_type=F32)
    out = sums[:8]
    tile = (iota(out.shape, 1) >> 1) & 31
    for q in range(1, len(tiles)):
        out = jnp.where(tile == q, sums[8 * q : 8 * q + 8], out)
    return out


def h_columns(h_ref, first, last, start, size):
    return jnp.concatenate([h_ref[0, 0, o, :, start : start + size] for o in range(first, last)], axis=0)


def forward(g_ref, obs_ref, x, x_scr, sums):
    slots = x.shape[0]
    sets = len(sums)
    x_scr[...] = x
    for ref in sums:
        ref[...] = jnp.zeros(ref.shape, F32)

    steps = slots // sets
    run = min(steps, 16)

    def products(j):
        at = [n * steps + j for n in range(sets)]
        return [(obs_ref[s], g_ref[s] * x_scr[pl.ds(s, 1), :]) for s in at]

    def step(first, carry):
        coming = products(first * run)
        for j in range(run):
            now = coming
            totals = [ref[block] + value for ref, (block, value) in zip(sums, now)]
            if j + 1 < run:
                coming = products(first * run + j + 1)
            for ref, (block, _), total in zip(sums, now, totals):
                ref[block] = total
        return carry

    lax.fori_loop(0, steps // run, step, 0)
    rows = OBLK_DEV * TILES // 8
    tiles = []
    for q in range(rows):
        at = (q // 4, slice(8 * (q % 4), 8 * (q % 4) + 8))
        tiles.append(tree_sum([ref[at] for ref in sums]))
    return lane_sums(tiles)


def adjoint(h_ref, slot_obs, d, store):
    owners, capacity = h_ref.shape[2], h_ref.shape[3]
    place = (iota(d.shape, 1) & OB) + 8 * iota(d.shape, 0)
    spread = jnp.concatenate(
        [
            jnp.take_along_axis(
                jnp.broadcast_to(d[t % 8 : t % 8 + 1], d.shape),
                place + 2 * (t // 8),
                axis=1,
                mode="promise_in_bounds",
            )
            for t in range(TILES)
        ],
        axis=1,
    )
    spread = jnp.concatenate([term.astype(F32) for term in three(spread)], axis=0).astype(BF16)
    group = min(owners, 4)
    for first in range(0, owners, group):
        rows = slice(first * capacity, (first + group) * capacity)
        total = None
        for t in range(TILES // 2):
            columns = slice(2 * LANES * t, 2 * LANES * (t + 1))
            given = jnp.dot(slot_obs[rows], spread[:, columns], preferred_element_type=F32)
            terms = h_columns(h_ref, first, first + group, 2 * LANES * t, 2 * LANES) * given
            total = terms if total is None else total + terms
        total = total[:, :LANES] + total[:, LANES:]
        total = total + half_swap(total)
        for o in range(group):
            upper_half = o * capacity + capacity // 2
            pair = total[o * capacity : upper_half], total[upper_half : (o + 1) * capacity]
            store(first + o, jnp.where(low(pair[0].shape), *pair))


def prepare(
    fslot_hbm, oslot_hbm, count_hbm, observed_hbm, weight_hbm, flux_hbm, h_hbm, g_hbm,
    pick_flux_ref, target_ref, slot_obs_ref, index_ref, observed_out, weight_out, flux_ref, h_ref, g_ref, obs_ref,
    fslot_ref, oslot_ref, count_ref, observed_ref, weight_ref, oslot_scalars, count_scalars, sems, h_sems, g_sems,
):
    me = lax.axis_index("cell")
    owners, capacity = fslot_ref.shape[2:]
    pairs = (
        (fslot_hbm, fslot_ref),
        (oslot_hbm, oslot_ref),
        (count_hbm, count_ref),
        (observed_hbm, observed_ref),
        (weight_hbm, weight_ref),
        (flux_hbm, flux_ref),
        (oslot_hbm, oslot_scalars),
        (count_hbm, count_scalars),
    )
    small = [pltpu.make_async_copy(src, dst, sems.at[i]) for i, (src, dst) in enumerate(pairs)]
    large = [
        pltpu.make_async_copy(h_hbm.at[:, :, o], h_ref.at[:, :, o], h_sems.at[o])
        for o in range(owners)
    ]
    for copy in small + large:
        copy.start()

    def turned(n, r):
        return pltpu.make_async_copy(g_hbm.at[n, :, r], g_ref.at[8 * n + r], g_sems.at[8 * n + r])

    def each_turned(action):
        def step(n, carry):
            for r in range(8):
                action(turned(n, r))
            return carry

        lax.fori_loop(0, owners * capacity // 8, step, 0, unroll=owners <= 4)

    each_turned(lambda copy: copy.start())
    for copy in small:
        copy.wait()

    def scalar_step(o, carry):
        for j in range(capacity):
            obs_ref[o * capacity + j] = jnp.where(
                j < count_scalars[0, 0, o], oslot_scalars[0, 0, o, j], OBLK_DEV
            )
        return carry

    lax.fori_loop(0, owners, scalar_step, 0, unroll=owners <= 4)
    slots = owners * capacity
    eye = iota((capacity, capacity), 0) == iota((capacity, capacity), 1)

    def column(ref):
        return jnp.concatenate(
            [
                jnp.sum(
                    jnp.where(eye, jnp.broadcast_to(ref[0, 0, o : o + 1, :], eye.shape), 0),
                    axis=1,
                    keepdims=True,
                )
                for o in range(owners)
            ],
            axis=0,
        )

    fslot, oslot = column(fslot_ref), column(oslot_ref)
    counts = jnp.concatenate(
        [
            jnp.broadcast_to(count_ref[0, 0:1, o : o + 1], (capacity, 1))
            for o in range(owners)
        ],
        axis=0,
    )
    slot = iota((slots, 1), 0)
    owner = slot // capacity
    live = (slot - owner * capacity) < counts
    oslot = jnp.where(live, oslot, OBLK_DEV)
    target = owner * BLOCKS + fslot
    target_ref[...] = jnp.broadcast_to(target.astype(F32), target_ref.shape)

    depth = owners * BLOCKS // 2
    row = (owner ^ me) * (BLOCKS // 2) + ((fslot & 7) >> 1) * WIN_DEV + (fslot >> 3)
    pick_flux_ref[...] = one_hot(iota((slots, 3 * depth), 1) % depth == row)
    slot_obs_ref[...] = one_hot((iota((slots, 3 * OBLK_DEV), 1) % OBLK_DEV) == oslot)

    half = slots // 2
    count = max(1, half // LANES)
    index_ref[...] = jnp.zeros(index_ref.shape, F32)
    for part in range(2):
        for q in range(count):
            r = (iota((slots, LANES), 1) + LANES * q) % half
            at = (r // (capacity // 2)) * capacity + r % (capacity // 2) + part * (capacity // 2)
            index_ref[pl.ds(part * count + q, 1), :] = jnp.sum(
                jnp.where(iota((slots, LANES), 0) == at, target.astype(F32), 0.0),
                axis=0,
                keepdims=True,
            )
    observed_out[...] = pack_obs(observed_ref[...])
    weight_out[...] = pack_obs(weight_ref[...])
    for copy in large:
        copy.wait()
    each_turned(lambda copy: copy.wait())


def first_model(order, *refs):
    parts = len(order)
    g_ref, pick_flux_ref, target_ref, obs_ref, m_ref, x_ref, x_scr, *sums = refs[parts:]
    flux = jnp.concatenate(
        [
            ref[:, LANES * t : LANES * (t + 1)]
            for ref in [refs[order.index(k)] for k in range(parts)]
            for t in range(CBLK_DEV // 2)
        ],
        axis=0,
    )
    pair = pick_rows(pick_flux_ref[...], flux)
    odd = (target_ref[...].astype(jnp.int32) & 1) == 1
    x = jnp.where(odd != low(pair.shape), pair, half_swap(pair))
    x_ref[...] = x
    m_ref[...] = forward(g_ref, obs_ref, x, x_scr, sums)


def first_adjoint(parts, *refs):
    observed_ref, weight_ref, slot_obs_ref, index_ref, h_ref, message_ref, d_ref = refs[parts:]
    d = weight_ref[...] * (tree_sum([m[...] for m in refs[:parts]]) - observed_ref[...])
    d_ref[...] = d
    rows = h_ref.shape[3] // 2
    half = h_ref.shape[2] * rows

    def store(o, block):
        message_ref[o * rows : (o + 1) * rows, :] = block

    adjoint(h_ref, slot_obs_ref[...], d, store)
    message_ref[half:, :] = index_ref[...]


def second_model(parts, *refs):
    messages = refs[:parts]
    cells = parts
    target_ref, x_ref, g_ref, obs_ref, m_ref, x_scr, *sums = refs[parts:]
    slots = target_ref.shape[0]
    half = slots // 2
    count = max(1, half // LANES)
    group = max(1, min(cells, LANES // half))
    total = None
    for first in range(0, cells, group):
        members = messages[first : first + group]
        picks = []
        for part in range(2):
            rows = []
            for q in range(count):
                at = half + part * count + q
                row = jnp.zeros((1, LANES), F32)
                for k, ref in enumerate(members):
                    row = jnp.where(iota((1, LANES), 1) // half % group == k, ref[at : at + 1, :], row)
                rows.append(one_hot(target_ref[...] == row))
            picks.append(jnp.concatenate(rows, axis=1)[:, : group * half])
        pick = jnp.concatenate(picks, axis=0)
        values = jnp.concatenate([ref[:half, :] for ref in members], axis=0)
        found = pick_rows(jnp.concatenate([pick] * 3, axis=1), values)
        total = found if total is None else total + found
    change = jnp.where(low((slots, LANES)), total[:slots], total[slots:])
    x = x_ref[...] - 0.5 * (change + half_swap(change))
    m_ref[...] = forward(g_ref, obs_ref, x, x_scr, sums)


def second_adjoint(parts, *refs):
    observed_ref, weight_ref, first_ref, slot_obs_ref, h_ref = refs[parts : parts + 5]
    *outs, d_ref, block_scr = refs[parts + 5 :]
    me = lax.axis_index("cell")
    owners = h_ref.shape[2]
    d = weight_ref[...] * (tree_sum([m[...] for m in refs[:parts]]) - observed_ref[...])
    d_ref[...] = d

    def store(o, block):
        block_scr[o] = block

    adjoint(h_ref, slot_obs_ref[...], -0.25 * first_ref[...] - 0.5 * d, store)
    for k in range(owners):
        outs[owners - 1 - k][...] = block_scr[me ^ k]


def prepare_increment(parts, rows, *refs):
    d_ref, pick_ref, departure_ref = refs[parts:]
    messages = refs[:parts]
    cells = parts
    me = lax.axis_index("cell")
    half = cells * rows
    count = max(1, half // LANES)
    place = me * rows
    lane = iota((1, LANES), 1)
    row = iota((BLOCKS, LANES), 0)
    block = me * BLOCKS + (row % WIN_DEV) * CBLK_DEV + 2 * ((row // WIN_DEV) % 4) + row // (BLOCKS // 2)
    block = block.astype(F32)
    for part in range(2):
        for first in range(0, half, LANES):
            index = jnp.zeros((1, LANES), F32)
            for k in range(first // rows, min(cells, (first + LANES) // rows)):
                turned = pltpu.roll(
                    messages[k][half:, :], lax.rem(k * rows - place % LANES + 2 * LANES - first, LANES), 1
                )
                chosen = turned[part * count : part * count + 1]
                for q in range(1, count):
                    chosen = jnp.where(
                        place // LANES == q, turned[part * count + q : part * count + q + 1], chosen
                    )
                index = jnp.where((lane // rows) % cells == k - first // rows, chosen, index)
            pick_ref[BLOCKS * part : BLOCKS * (part + 1), first : first + LANES] = one_hot(block == index)
    for t in range(OBLK_DEV // 2):
        departure_ref[:, LANES * t : LANES * (t + 1)] = unpack_obs(d_ref[...], t)


def gather_increment(*refs):
    *arrays, pick_ref, out_ref = refs
    values = jnp.concatenate([ref[...] for ref in arrays[::-1]], axis=0)
    half = values.shape[0]
    terms = three(values)
    pick = pick_ref[...]
    if 3 * half <= LANES:
        terms.append(jnp.zeros((LANES - 3 * half, LANES), BF16))
    else:
        pick = jnp.concatenate([pick[:, :half]] * 3, axis=1)
    found = jnp.dot(pick, jnp.concatenate(terms, axis=0), preferred_element_type=F32)
    found = jnp.where(low((BLOCKS, LANES)), found[:BLOCKS], found[BLOCKS:])
    found = found + half_swap(found)
    for t in range(CBLK_DEV // 2):
        even = found[WIN_DEV * t : WIN_DEV * (t + 1)]
        odd = found[BLOCKS // 2 + WIN_DEV * t : BLOCKS // 2 + WIN_DEV * (t + 1)]
        out_ref[:, LANES * t : LANES * (t + 1)] = jnp.where(low(even.shape), even, odd)


def send(value, axis, size, k):
    return lax.ppermute(value, axis, [(i, i ^ k) for i in range(size)])


def exchange(own, sent, axis, size):
    return [own] + [send(sent, axis, size, k) for k in range(size - 1, 0, -1)][::-1]


def make_local(cells, wins):
    def local(prior_flux, observed, obs_weight, footprint, flux_slot, obs_slot, slot_count):
        owners, capacity = footprint.shape[2:4]
        slots = owners * capacity
        half = slots // 2
        index_rows = -(-2 * max(1, half // LANES) // 8) * 8
        params = pltpu.CompilerParams(vmem_limit_bytes=footprint.size * 4 + 16 * 2**20)
        hbm = pl.BlockSpec(memory_space=pltpu.HBM)
        smem = pl.BlockSpec(memory_space=pltpu.SMEM)
        obs, obs_out = None, pltpu.SMEM((slots,), jnp.int32)

        def call(body, outs, ins, scratch=(), space=VMEM):
            if space is hbm:
                ins = [pltpu.with_memory_space_constraint(value, pltpu.HBM) for value in ins]
                outs_at = [pltpu.VMEM(s, t) for s, t in outs[:-1]] + [obs_out]
            else:
                outs_at = [jax.ShapeDtypeStruct(s, t) for s, t in outs]
            return pl.pallas_call(
                body,
                out_shape=outs_at,
                in_specs=[smem if value is obs else space for value in ins],
                out_specs=[smem if outs_at[n] is obs_out else VMEM for n in range(len(outs))],
                scratch_shapes=list(scratch),
                compiler_params=params,
            )(*ins)

        def like(value):
            return (value.shape, value.dtype)

        obs_tile = ((OBLK_DEV, LANES), F32)
        slot_tile = ((slots, LANES), F32)
        sum_scratch = [pltpu.VMEM(*slot_tile)] + [pltpu.VMEM((OBLK_DEV + 1, TILES, LANES), F32)] * 4
        small = (flux_slot, obs_slot, slot_count, observed, obs_weight)
        turned = footprint.reshape(slots // 8, 8, TILES, LANES).transpose(0, 2, 1, 3)
        pick_flux, target, slot_obs, index, observed_t, weight_t, flux, matrices, by_slot, obs = call(
            prepare,
            [
                ((slots, 3 * owners * BLOCKS // 2), BF16),
                slot_tile,
                ((slots, 3 * OBLK_DEV), BF16),
                ((index_rows, LANES), F32),
                obs_tile,
                obs_tile,
                like(prior_flux),
                like(footprint),
                ((slots, TILES, LANES), F32),
                ((slots,), jnp.int32),
            ],
            (*small, prior_flux, footprint, turned),
            [
                *(pltpu.VMEM(*like(value)) for value in small),
                pltpu.SMEM(*like(obs_slot)),
                pltpu.SMEM(*like(slot_count)),
                pltpu.SemaphoreType.DMA((len(small) + 3,)),
                pltpu.SemaphoreType.DMA((owners,)),
                pltpu.SemaphoreType.DMA((slots,)),
            ],
            hbm,
        )
        order = [0, cells // 2, *range(1, cells // 2), *range(cells // 2 + 1, cells)]
        fluxes = exchange(flux, prior_flux, "cell", cells)
        m0, x0 = call(
            functools.partial(first_model, order),
            [obs_tile, slot_tile],
            (*(fluxes[k] for k in order), by_slot, pick_flux, target, obs),
            sum_scratch,
        )
        message, d0 = call(
            functools.partial(first_adjoint, wins),
            [((half + index_rows, LANES), F32), obs_tile],
            (*exchange(m0, m0, "win", wins), observed_t, weight_t, slot_obs, index, matrices),
        )
        messages = exchange(message, message, "cell", cells)
        (m1,) = call(
            functools.partial(second_model, cells),
            [obs_tile],
            (*messages, target, x0, by_slot, obs),
            sum_scratch,
        )
        *blocks, d1 = call(
            functools.partial(second_adjoint, wins),
            [((capacity // 2, LANES), F32)] * owners + [obs_tile],
            (*exchange(m1, m1, "win", wins), observed_t, weight_t, d0, slot_obs, matrices),
            [pltpu.VMEM((owners, capacity // 2, LANES), F32)],
        )
        arrays = [send(block, "cell", cells, cells - 1 - i) for i, block in enumerate(blocks[:-1])]
        arrays = [blocks[-1]] + arrays[::-1]
        pick, departure = call(
            functools.partial(prepare_increment, cells, capacity // 2),
            [((2 * BLOCKS, max(LANES, half)), BF16), ((1, OBLK_DEV * OB), F32)],
            (*messages, d1),
        )
        (increment,) = call(
            gather_increment,
            [((WIN_DEV, CBLK_DEV * CB), F32)],
            (*arrays[::-1], pick),
        )
        return increment, departure

    return local


def solution(mesh):
    placed = (
        P(("ens", "win"), "cell"),
        P(("ens", "cell"), None),
        P(("ens", "cell"), None),
        P("cell", "win", None, None, None),
        P("cell", "win", None, None),
        P("cell", "win", None, None),
        P("cell", "win", None),
    )
    return jax.shard_map(
        make_local(mesh.shape["cell"], mesh.shape["win"]),
        mesh=mesh,
        in_specs=placed,
        out_specs=(P(("ens", "win"), "cell"), P(("ens", "cell"), None)),
        check_vma=False,
    )
```

```python
import functools
import jax
import jax.numpy as jnp
from jax import lax
from jax.experimental import pallas as pl
from jax.experimental.pallas import tpu as pltpu
from jax.sharding import PartitionSpec as P

CB = 64
OB = 64
CBLK_DEV = 8
WIN_DEV = 8
OBLK_DEV = 8
BLOCKS = WIN_DEV * CBLK_DEV
LANES = 128
TILES = OB * CB // LANES

F32 = jnp.float32
BF16 = jnp.bfloat16
VMEM = pl.BlockSpec(memory_space=pltpu.VMEM)


def iota(shape, dim):
    return lax.broadcasted_iota(jnp.int32, shape, dim)


def one_hot(where):
    return jnp.where(where, 1.0, 0.0).astype(BF16)


def three(value):
    first = value.astype(BF16)
    rest = value - first.astype(F32)
    second = rest.astype(BF16)
    third = (rest - second.astype(F32)).astype(BF16)
    return [first, second, third]


def pick_rows(pick3, value):
    return jnp.dot(pick3, jnp.concatenate(three(value), axis=0), preferred_element_type=F32)


def half_swap(value):
    return pltpu.roll(value, LANES // 2, 1)


def low(shape):
    return iota(shape, 1) < LANES // 2


def tree_sum(parts):
    parts = list(parts)
    while len(parts) > 1:
        parts = [sum(parts[i + 1 : i + 2], parts[i]) for i in range(0, len(parts), 2)]
    return parts[0]


def pack_obs(row):
    lane = iota((8, LANES), 1)
    block = (lane >> 1) & 31
    place = 16 * (block & 7) + 2 * iota(lane.shape, 0) + (lane >> 6)
    out = jnp.zeros(lane.shape, F32)
    for t in range(OBLK_DEV // 2):
        tile = jnp.broadcast_to(row[:, LANES * t : LANES * (t + 1)], lane.shape)
        found = jnp.take_along_axis(tile, place, axis=1, mode="promise_in_bounds")
        out = jnp.where(block >> 3 == t, found, out)
    return out


def unpack_obs(packed, t):
    lane = iota(packed.shape, 1)
    place = (lane & 1) * OB + 2 * (8 * t + (lane >> 4))
    found = jnp.take_along_axis(packed, place, axis=1, mode="promise_in_bounds")
    here = (lane & 15) >> 1 == iota(packed.shape, 0)
    return jnp.sum(jnp.where(here, found, 0.0), axis=0, keepdims=True)


def lane_sums(tiles):
    terms = jnp.concatenate(three(jnp.concatenate(tiles, axis=0)), axis=1)
    shape = (3 * LANES, LANES)
    ones = one_hot((iota(shape, 0) // OB) % 2 == iota(shape, 1) // OB)
    sums = jnp.dot(terms, ones, preferred_element_type=F32)
    out = sums[:8]
    tile = (iota(out.shape, 1) >> 1) & 31
    for q in range(1, len(tiles)):
        out = jnp.where(tile == q, sums[8 * q : 8 * q + 8], out)
    return out


def h_columns(h_ref, first, last, start, size):
    return jnp.concatenate([h_ref[0, 0, o, :, start : start + size] for o in range(first, last)], axis=0)


def forward(g_ref, obs_ref, x, x_scr, sums):
    slots = x.shape[0]
    sets = len(sums)
    x_scr[...] = x
    for ref in sums:
        ref[...] = jnp.zeros(ref.shape, F32)

    steps = slots // sets
    run = min(steps, 16)

    def products(j):
        at = [n * steps + j for n in range(sets)]
        return [(obs_ref[s], g_ref[s // 8, s % 8] * x_scr[pl.ds(s, 1), :]) for s in at]

    def step(first, carry):
        coming = products(first * run)
        for j in range(run):
            now = coming
            totals = [ref[block] + value for ref, (block, value) in zip(sums, now)]
            if j + 1 < run:
                coming = products(first * run + j + 1)
            for ref, (block, _), total in zip(sums, now, totals):
                ref[block] = total
        return carry

    lax.fori_loop(0, steps // run, step, 0)
    rows = OBLK_DEV * TILES // 8
    tiles = []
    for q in range(rows):
        at = (q // 4, slice(8 * (q % 4), 8 * (q % 4) + 8))
        tiles.append(tree_sum([ref[at] for ref in sums]))
    return lane_sums(tiles)


def adjoint(h_ref, slot_obs, d, store):
    owners, capacity = h_ref.shape[2], h_ref.shape[3]
    place = (iota(d.shape, 1) & OB) + 8 * iota(d.shape, 0)
    spread = jnp.concatenate(
        [
            jnp.take_along_axis(
                jnp.broadcast_to(d[t % 8 : t % 8 + 1], d.shape),
                place + 2 * (t // 8),
                axis=1,
                mode="promise_in_bounds",
            )
            for t in range(TILES)
        ],
        axis=1,
    )
    spread = jnp.concatenate([term.astype(F32) for term in three(spread)], axis=0).astype(BF16)
    group = min(owners, 4)
    for first in range(0, owners, group):
        rows = slice(first * capacity, (first + group) * capacity)
        total = None
        for t in range(TILES // 2):
            columns = slice(2 * LANES * t, 2 * LANES * (t + 1))
            given = jnp.dot(slot_obs[rows], spread[:, columns], preferred_element_type=F32)
            terms = h_columns(h_ref, first, first + group, 2 * LANES * t, 2 * LANES) * given
            total = terms if total is None else total + terms
        total = total[:, :LANES] + total[:, LANES:]
        total = total + half_swap(total)
        for o in range(group):
            upper_half = o * capacity + capacity // 2
            pair = total[o * capacity : upper_half], total[upper_half : (o + 1) * capacity]
            store(first + o, jnp.where(low(pair[0].shape), *pair))


def prepare(
    fslot_hbm, oslot_hbm, count_hbm, observed_hbm, weight_hbm, flux_hbm, h_hbm, g_hbm,
    pick_flux_ref, target_ref, slot_obs_ref, index_ref, observed_out, weight_out, flux_ref, h_ref, g_ref, obs_ref,
    fslot_ref, oslot_ref, count_ref, observed_ref, weight_ref, oslot_scalars, count_scalars, sems, h_sems, g_sems,
):
    me = lax.axis_index("cell")
    owners, capacity = fslot_ref.shape[2:]
    pairs = (
        (fslot_hbm, fslot_ref),
        (oslot_hbm, oslot_ref),
        (count_hbm, count_ref),
        (observed_hbm, observed_ref),
        (weight_hbm, weight_ref),
        (flux_hbm, flux_ref),
        (oslot_hbm, oslot_scalars),
        (count_hbm, count_scalars),
    )
    small = [pltpu.make_async_copy(src, dst, sems.at[i]) for i, (src, dst) in enumerate(pairs)]
    large = [
        pltpu.make_async_copy(h_hbm.at[:, :, o], h_ref.at[:, :, o], h_sems.at[o])
        for o in range(owners)
    ]
    for copy in small + large:
        copy.start()

    turned = [
        pltpu.make_async_copy(g_hbm.at[:, :, r], g_ref.at[:, r], g_sems.at[r]) for r in range(8)
    ]
    for copy in turned:
        copy.start()
    for copy in small:
        copy.wait()

    def scalar_step(o, carry):
        for j in range(capacity):
            obs_ref[o * capacity + j] = jnp.where(
                j < count_scalars[0, 0, o], oslot_scalars[0, 0, o, j], OBLK_DEV
            )
        return carry

    lax.fori_loop(0, owners, scalar_step, 0, unroll=owners <= 4)
    slots = owners * capacity
    eye = iota((capacity, capacity), 0) == iota((capacity, capacity), 1)

    def column(ref):
        return jnp.concatenate(
            [
                jnp.sum(
                    jnp.where(eye, jnp.broadcast_to(ref[0, 0, o : o + 1, :], eye.shape), 0),
                    axis=1,
                    keepdims=True,
                )
                for o in range(owners)
            ],
            axis=0,
        )

    fslot, oslot = column(fslot_ref), column(oslot_ref)
    counts = jnp.concatenate(
        [
            jnp.broadcast_to(count_ref[0, 0:1, o : o + 1], (capacity, 1))
            for o in range(owners)
        ],
        axis=0,
    )
    slot = iota((slots, 1), 0)
    owner = slot // capacity
    live = (slot - owner * capacity) < counts
    oslot = jnp.where(live, oslot, OBLK_DEV)
    target = owner * BLOCKS + fslot
    target_ref[...] = jnp.broadcast_to(target.astype(F32), target_ref.shape)

    depth = owners * BLOCKS // 2
    row = (owner ^ me) * (BLOCKS // 2) + ((fslot & 7) >> 1) * WIN_DEV + (fslot >> 3)
    pick_flux_ref[...] = one_hot(iota((slots, 3 * depth), 1) % depth == row)
    slot_obs_ref[...] = one_hot((iota((slots, 3 * OBLK_DEV), 1) % OBLK_DEV) == oslot)

    half = slots // 2
    count = max(1, half // LANES)
    index_ref[...] = jnp.zeros(index_ref.shape, F32)
    for part in range(2):
        for q in range(count):
            r = (iota((slots, LANES), 1) + LANES * q) % half
            at = (r // (capacity // 2)) * capacity + r % (capacity // 2) + part * (capacity // 2)
            index_ref[pl.ds(part * count + q, 1), :] = jnp.sum(
                jnp.where(iota((slots, LANES), 0) == at, target.astype(F32), 0.0),
                axis=0,
                keepdims=True,
            )
    observed_out[...] = pack_obs(observed_ref[...])
    weight_out[...] = pack_obs(weight_ref[...])
    for copy in large + turned:
        copy.wait()


def first_model(order, *refs):
    parts = len(order)
    g_ref, pick_flux_ref, target_ref, obs_ref, m_ref, x_ref, x_scr, *sums = refs[parts:]
    flux = jnp.concatenate(
        [
            ref[:, LANES * t : LANES * (t + 1)]
            for ref in [refs[order.index(k)] for k in range(parts)]
            for t in range(CBLK_DEV // 2)
        ],
        axis=0,
    )
    pair = pick_rows(pick_flux_ref[...], flux)
    odd = (target_ref[...].astype(jnp.int32) & 1) == 1
    x = jnp.where(odd != low(pair.shape), pair, half_swap(pair))
    x_ref[...] = x
    m_ref[...] = forward(g_ref, obs_ref, x, x_scr, sums)


def first_adjoint(parts, *refs):
    observed_ref, weight_ref, slot_obs_ref, index_ref, h_ref, message_ref, d_ref = refs[parts:]
    d = weight_ref[...] * (tree_sum([m[...] for m in refs[:parts]]) - observed_ref[...])
    d_ref[...] = d
    rows = h_ref.shape[3] // 2
    half = h_ref.shape[2] * rows

    def store(o, block):
        message_ref[o * rows : (o + 1) * rows, :] = block

    adjoint(h_ref, slot_obs_ref[...], d, store)
    message_ref[half:, :] = index_ref[...]


def second_model(parts, *refs):
    messages = refs[:parts]
    cells = parts
    target_ref, x_ref, g_ref, obs_ref, m_ref, x_scr, *sums = refs[parts:]
    slots = target_ref.shape[0]
    half = slots // 2
    count = max(1, half // LANES)
    group = max(1, min(cells, LANES // half))
    total = None
    for first in range(0, cells, group):
        members = messages[first : first + group]
        picks = []
        for part in range(2):
            rows = []
            for q in range(count):
                at = half + part * count + q
                row = jnp.zeros((1, LANES), F32)
                for k, ref in enumerate(members):
                    row = jnp.where(iota((1, LANES), 1) // half % group == k, ref[at : at + 1, :], row)
                rows.append(one_hot(target_ref[...] == row))
            picks.append(jnp.concatenate(rows, axis=1)[:, : group * half])
        pick = jnp.concatenate(picks, axis=0)
        values = jnp.concatenate([ref[:half, :] for ref in members], axis=0)
        found = pick_rows(jnp.concatenate([pick] * 3, axis=1), values)
        total = found if total is None else total + found
    change = jnp.where(low((slots, LANES)), total[:slots], total[slots:])
    x = x_ref[...] - 0.5 * (change + half_swap(change))
    m_ref[...] = forward(g_ref, obs_ref, x, x_scr, sums)


def second_adjoint(parts, *refs):
    observed_ref, weight_ref, first_ref, slot_obs_ref, h_ref = refs[parts : parts + 5]
    *outs, d_ref, block_scr = refs[parts + 5 :]
    me = lax.axis_index("cell")
    owners = h_ref.shape[2]
    d = weight_ref[...] * (tree_sum([m[...] for m in refs[:parts]]) - observed_ref[...])
    d_ref[...] = d

    def store(o, block):
        block_scr[o] = block

    adjoint(h_ref, slot_obs_ref[...], -0.25 * first_ref[...] - 0.5 * d, store)
    for k in range(owners):
        outs[owners - 1 - k][...] = block_scr[me ^ k]


def prepare_increment(parts, rows, *refs):
    d_ref, pick_ref, departure_ref = refs[parts:]
    messages = refs[:parts]
    cells = parts
    me = lax.axis_index("cell")
    half = cells * rows
    count = max(1, half // LANES)
    place = me * rows
    lane = iota((1, LANES), 1)
    row = iota((BLOCKS, LANES), 0)
    block = me * BLOCKS + (row % WIN_DEV) * CBLK_DEV + 2 * ((row // WIN_DEV) % 4) + row // (BLOCKS // 2)
    block = block.astype(F32)
    for part in range(2):
        for first in range(0, half, LANES):
            index = jnp.zeros((1, LANES), F32)
            for k in range(first // rows, min(cells, (first + LANES) // rows)):
                turned = pltpu.roll(
                    messages[k][half:, :], lax.rem(k * rows - place % LANES + 2 * LANES - first, LANES), 1
                )
                chosen = turned[part * count : part * count + 1]
                for q in range(1, count):
                    chosen = jnp.where(
                        place // LANES == q, turned[part * count + q : part * count + q + 1], chosen
                    )
                index = jnp.where((lane // rows) % cells == k - first // rows, chosen, index)
            pick_ref[BLOCKS * part : BLOCKS * (part + 1), first : first + LANES] = one_hot(block == index)
    for t in range(OBLK_DEV // 2):
        departure_ref[:, LANES * t : LANES * (t + 1)] = unpack_obs(d_ref[...], t)


def gather_increment(*refs):
    *arrays, pick_ref, out_ref = refs
    values = jnp.concatenate([ref[...] for ref in arrays[::-1]], axis=0)
    half = values.shape[0]
    terms = three(values)
    pick = pick_ref[...]
    if 3 * half <= LANES:
        terms.append(jnp.zeros((LANES - 3 * half, LANES), BF16))
    else:
        pick = jnp.concatenate([pick[:, :half]] * 3, axis=1)
    found = jnp.dot(pick, jnp.concatenate(terms, axis=0), preferred_element_type=F32)
    found = jnp.where(low((BLOCKS, LANES)), found[:BLOCKS], found[BLOCKS:])
    found = found + half_swap(found)
    for t in range(CBLK_DEV // 2):
        even = found[WIN_DEV * t : WIN_DEV * (t + 1)]
        odd = found[BLOCKS // 2 + WIN_DEV * t : BLOCKS // 2 + WIN_DEV * (t + 1)]
        out_ref[:, LANES * t : LANES * (t + 1)] = jnp.where(low(even.shape), even, odd)


def send(value, axis, size, k):
    return lax.ppermute(value, axis, [(i, i ^ k) for i in range(size)])


def exchange(own, sent, axis, size):
    return [own] + [send(sent, axis, size, k) for k in range(size - 1, 0, -1)][::-1]


def make_local(cells, wins):
    def local(prior_flux, observed, obs_weight, footprint, flux_slot, obs_slot, slot_count):
        owners, capacity = footprint.shape[2:4]
        slots = owners * capacity
        half = slots // 2
        index_rows = -(-2 * max(1, half // LANES) // 8) * 8
        params = pltpu.CompilerParams(vmem_limit_bytes=footprint.size * 4 + 16 * 2**20)
        hbm = pl.BlockSpec(memory_space=pltpu.HBM)
        smem = pl.BlockSpec(memory_space=pltpu.SMEM)
        obs, obs_out = None, pltpu.SMEM((slots,), jnp.int32)

        def call(body, outs, ins, scratch=(), space=VMEM):
            if space is hbm:
                ins = [pltpu.with_memory_space_constraint(value, pltpu.HBM) for value in ins]
                outs_at = [pltpu.VMEM(s, t) for s, t in outs[:-1]] + [obs_out]
            else:
                outs_at = [jax.ShapeDtypeStruct(s, t) for s, t in outs]
            return pl.pallas_call(
                body,
                out_shape=outs_at,
                in_specs=[smem if value is obs else space for value in ins],
                out_specs=[smem if outs_at[n] is obs_out else VMEM for n in range(len(outs))],
                scratch_shapes=list(scratch),
                compiler_params=params,
            )(*ins)

        def like(value):
            return (value.shape, value.dtype)

        obs_tile = ((OBLK_DEV, LANES), F32)
        slot_tile = ((slots, LANES), F32)
        sum_scratch = [pltpu.VMEM(*slot_tile)] + [pltpu.VMEM((OBLK_DEV + 1, TILES, LANES), F32)] * 4
        small = (flux_slot, obs_slot, slot_count, observed, obs_weight)
        turned = footprint.reshape(slots // 8, 8, TILES, LANES).transpose(0, 2, 1, 3)
        pick_flux, target, slot_obs, index, observed_t, weight_t, flux, matrices, by_slot, obs = call(
            prepare,
            [
                ((slots, 3 * owners * BLOCKS // 2), BF16),
                slot_tile,
                ((slots, 3 * OBLK_DEV), BF16),
                ((index_rows, LANES), F32),
                obs_tile,
                obs_tile,
                like(prior_flux),
                like(footprint),
                ((slots // 8, 8, TILES, LANES), F32),
                ((slots,), jnp.int32),
            ],
            (*small, prior_flux, footprint, turned),
            [
                *(pltpu.VMEM(*like(value)) for value in small),
                pltpu.SMEM(*like(obs_slot)),
                pltpu.SMEM(*like(slot_count)),
                pltpu.SemaphoreType.DMA((len(small) + 3,)),
                pltpu.SemaphoreType.DMA((owners,)),
                pltpu.SemaphoreType.DMA((8,)),
            ],
            hbm,
        )
        order = [0, cells - 1, *range(1, cells - 1)]
        fluxes = exchange(flux, prior_flux, "cell", cells)
        m0, x0 = call(
            functools.partial(first_model, order),
            [obs_tile, slot_tile],
            (*(fluxes[k] for k in order), by_slot, pick_flux, target, obs),
            sum_scratch,
        )
        message, d0 = call(
            functools.partial(first_adjoint, wins),
            [((half + index_rows, LANES), F32), obs_tile],
            (*exchange(m0, m0, "win", wins), observed_t, weight_t, slot_obs, index, matrices),
        )
        messages = exchange(message, message, "cell", cells)
        (m1,) = call(
            functools.partial(second_model, cells),
            [obs_tile],
            (*messages, target, x0, by_slot, obs),
            sum_scratch,
        )
        *blocks, d1 = call(
            functools.partial(second_adjoint, wins),
            [((capacity // 2, LANES), F32)] * owners + [obs_tile],
            (*exchange(m1, m1, "win", wins), observed_t, weight_t, d0, slot_obs, matrices),
            [pltpu.VMEM((owners, capacity // 2, LANES), F32)],
        )
        arrays = [send(block, "cell", cells, cells - 1 - i) for i, block in enumerate(blocks[:-1])]
        arrays = [blocks[-1]] + arrays[::-1]
        pick, departure = call(
            functools.partial(prepare_increment, cells, capacity // 2),
            [((2 * BLOCKS, max(LANES, half)), BF16), ((1, OBLK_DEV * OB), F32)],
            (*messages, d1),
        )
        (increment,) = call(
            gather_increment,
            [((WIN_DEV, CBLK_DEV * CB), F32)],
            (*arrays[::-1], pick),
        )
        return increment, departure

    return local


def solution(mesh):
    placed = (
        P(("ens", "win"), "cell"),
        P(("ens", "cell"), None),
        P(("ens", "cell"), None),
        P("cell", "win", None, None, None),
        P("cell", "win", None, None),
        P("cell", "win", None, None),
        P("cell", "win", None),
    )
    return jax.shard_map(
        make_local(mesh.shape["cell"], mesh.shape["win"]),
        mesh=mesh,
        in_specs=placed,
        out_specs=(P(("ens", "win"), "cell"), P(("ens", "cell"), None)),
        check_vma=False,
    )
```

```python
import functools
import jax
import jax.numpy as jnp
from jax import lax
from jax.experimental import pallas as pl
from jax.experimental.pallas import tpu as pltpu
from jax.sharding import PartitionSpec as P

CB = 64
OB = 64
CBLK_DEV = 8
WIN_DEV = 8
OBLK_DEV = 8
BLOCKS = WIN_DEV * CBLK_DEV
LANES = 128
TILES = OB * CB // LANES

F32 = jnp.float32
BF16 = jnp.bfloat16
VMEM = pl.BlockSpec(memory_space=pltpu.VMEM)


def iota(shape, dim):
    return lax.broadcasted_iota(jnp.int32, shape, dim)


def one_hot(where):
    return jnp.where(where, 1.0, 0.0).astype(BF16)


def three(value):
    first = value.astype(BF16)
    rest = value - first.astype(F32)
    second = rest.astype(BF16)
    third = (rest - second.astype(F32)).astype(BF16)
    return [first, second, third]


def pick_rows(pick3, value):
    return jnp.dot(pick3, jnp.concatenate(three(value), axis=0), preferred_element_type=F32)


def half_swap(value):
    return pltpu.roll(value, LANES // 2, 1)


def low(shape):
    return iota(shape, 1) < LANES // 2


def in_turn(refs, order):
    return [refs[0]] + [refs[1 + order.index(k)] for k in range(1, 1 + len(order))]


def tree_sum(parts):
    parts = list(parts)
    while len(parts) > 1:
        parts = [sum(parts[i + 1 : i + 2], parts[i]) for i in range(0, len(parts), 2)]
    return parts[0]


def pack_obs(row):
    lane = iota((8, LANES), 1)
    block = (lane >> 1) & 31
    place = 16 * (block & 7) + 2 * iota(lane.shape, 0) + (lane >> 6)
    out = jnp.zeros(lane.shape, F32)
    for t in range(OBLK_DEV // 2):
        tile = jnp.broadcast_to(row[:, LANES * t : LANES * (t + 1)], lane.shape)
        found = jnp.take_along_axis(tile, place, axis=1, mode="promise_in_bounds")
        out = jnp.where(block >> 3 == t, found, out)
    return out


def unpack_obs(packed, t):
    lane = iota(packed.shape, 1)
    place = (lane & 1) * OB + 2 * (8 * t + (lane >> 4))
    found = jnp.take_along_axis(packed, place, axis=1, mode="promise_in_bounds")
    here = (lane & 15) >> 1 == iota(packed.shape, 0)
    return jnp.sum(jnp.where(here, found, 0.0), axis=0, keepdims=True)


def lane_sums(tiles):
    terms = jnp.concatenate(three(jnp.concatenate(tiles, axis=0)), axis=1)
    shape = (3 * LANES, LANES)
    ones = one_hot((iota(shape, 0) // OB) % 2 == iota(shape, 1) // OB)
    sums = jnp.dot(terms, ones, preferred_element_type=F32)
    out = sums[:8]
    tile = (iota(out.shape, 1) >> 1) & 31
    for q in range(1, len(tiles)):
        out = jnp.where(tile == q, sums[8 * q : 8 * q + 8], out)
    return out


def h_columns(h_ref, first, last, start, size):
    return jnp.concatenate([h_ref[0, 0, o, :, start : start + size] for o in range(first, last)], axis=0)


def forward(g_ref, obs_ref, x, x_scr, sums, slot_of):
    slots = x.shape[0]
    sets = len(sums)
    x_scr[...] = x
    for ref in sums:
        ref[...] = jnp.zeros(ref.shape, F32)

    steps = slots // sets
    run = min(steps, 16)

    def products(j):
        at = [n * steps + j for n in range(sets)]
        found = []
        for i in at:
            s = slot_of(i)
            found.append((obs_ref[s], g_ref[s // 8, s % 8] * x_scr[pl.ds(i, 1), :]))
        return found

    def step(first, carry):
        coming = products(first * run)
        for j in range(run):
            now = coming
            totals = [ref[block] + value for ref, (block, value) in zip(sums, now)]
            if j + 1 < run:
                coming = products(first * run + j + 1)
            for ref, (block, _), total in zip(sums, now, totals):
                ref[block] = total
        return carry

    lax.fori_loop(0, steps // run, step, 0)
    rows = OBLK_DEV * TILES // 8
    tiles = []
    for q in range(rows):
        at = (q // 4, slice(8 * (q % 4), 8 * (q % 4) + 8))
        tiles.append(tree_sum([ref[at] for ref in sums]))
    return lane_sums(tiles)


def adjoint(h_ref, slot_obs, d, store):
    owners, capacity = h_ref.shape[2], h_ref.shape[3]
    place = (iota(d.shape, 1) & OB) + 8 * iota(d.shape, 0)
    spread = jnp.concatenate(
        [
            jnp.take_along_axis(
                jnp.broadcast_to(d[t % 8 : t % 8 + 1], d.shape),
                place + 2 * (t // 8),
                axis=1,
                mode="promise_in_bounds",
            )
            for t in range(TILES)
        ],
        axis=1,
    )
    spread = jnp.concatenate([term.astype(F32) for term in three(spread)], axis=0).astype(BF16)
    group = min(owners, 4)
    for first in range(0, owners, group):
        rows = slice(first * capacity, (first + group) * capacity)
        total = None
        for t in range(TILES // 2):
            columns = slice(2 * LANES * t, 2 * LANES * (t + 1))
            given = jnp.dot(slot_obs[rows], spread[:, columns], preferred_element_type=F32)
            terms = h_columns(h_ref, first, first + group, 2 * LANES * t, 2 * LANES) * given
            total = terms if total is None else total + terms
        total = total[:, :LANES] + total[:, LANES:]
        total = total + half_swap(total)
        for o in range(group):
            upper_half = o * capacity + capacity // 2
            pair = total[o * capacity : upper_half], total[upper_half : (o + 1) * capacity]
            store(first + o, jnp.where(low(pair[0].shape), *pair))


def prepare(
    fslot_hbm, oslot_hbm, count_hbm, observed_hbm, weight_hbm, flux_hbm, h_hbm, g_hbm,
    pick_flux_ref, target_ref, slot_obs_ref, index_ref, observed_out, weight_out, flux_ref, h_ref, g_ref, obs_ref,
    fslot_ref, oslot_ref, count_ref, observed_ref, weight_ref, oslot_scalars, count_scalars, sems, h_sems, g_sems,
):
    me = lax.axis_index("cell")
    owners, capacity = fslot_ref.shape[2:]
    pairs = (
        (fslot_hbm, fslot_ref),
        (oslot_hbm, oslot_ref),
        (count_hbm, count_ref),
        (observed_hbm, observed_ref),
        (weight_hbm, weight_ref),
        (flux_hbm, flux_ref),
        (oslot_hbm, oslot_scalars),
        (count_hbm, count_scalars),
    )
    small = [pltpu.make_async_copy(src, dst, sems.at[i]) for i, (src, dst) in enumerate(pairs)]
    large = [
        pltpu.make_async_copy(h_hbm.at[:, :, o], h_ref.at[:, :, o], h_sems.at[o])
        for o in range(owners)
    ]
    for copy in small + large:
        copy.start()

    turned = [
        pltpu.make_async_copy(g_hbm.at[:, :, r], g_ref.at[:, r], g_sems.at[r]) for r in range(8)
    ]
    for copy in turned:
        copy.start()
    for copy in small:
        copy.wait()

    def scalar_step(o, carry):
        for j in range(capacity):
            obs_ref[o * capacity + j] = jnp.where(
                j < count_scalars[0, 0, o], oslot_scalars[0, 0, o, j], OBLK_DEV
            )
        return carry

    lax.fori_loop(0, owners, scalar_step, 0, unroll=owners <= 4)
    slots = owners * capacity
    eye = iota((capacity, capacity), 0) == iota((capacity, capacity), 1)

    def column(ref):
        return jnp.concatenate(
            [
                jnp.sum(
                    jnp.where(eye, jnp.broadcast_to(ref[0, 0, o : o + 1, :], eye.shape), 0),
                    axis=1,
                    keepdims=True,
                )
                for o in range(owners)
            ],
            axis=0,
        )

    fslot, oslot = column(fslot_ref), column(oslot_ref)
    counts = jnp.concatenate(
        [
            jnp.broadcast_to(count_ref[0, 0:1, o : o + 1], (capacity, 1))
            for o in range(owners)
        ],
        axis=0,
    )
    slot = iota((slots, 1), 0)
    owner = slot // capacity
    live = (slot - owner * capacity) < counts
    oslot = jnp.where(live, oslot, OBLK_DEV)
    target = owner * BLOCKS + fslot
    target_ref[...] = jnp.broadcast_to(target.astype(F32), target_ref.shape)

    depth = owners * BLOCKS // 2
    row = (owner ^ me) * (BLOCKS // 2) + ((fslot & 7) >> 1) * WIN_DEV + (fslot >> 3)
    pick_flux_ref[...] = one_hot(iota((slots, 3 * depth), 1) % depth == row)
    slot_obs_ref[...] = one_hot((iota((slots, 3 * OBLK_DEV), 1) % OBLK_DEV) == oslot)

    half = slots // 2
    count = max(1, half // LANES)
    index_ref[...] = jnp.zeros(index_ref.shape, F32)
    for part in range(2):
        for q in range(count):
            r = (iota((slots, LANES), 1) + LANES * q) % half
            at = (r // (capacity // 2)) * capacity + r % (capacity // 2) + part * (capacity // 2)
            index_ref[pl.ds(part * count + q, 1), :] = jnp.sum(
                jnp.where(iota((slots, LANES), 0) == at, target.astype(F32), 0.0),
                axis=0,
                keepdims=True,
            )
    observed_out[...] = pack_obs(observed_ref[...])
    weight_out[...] = pack_obs(weight_ref[...])
    for copy in large + turned:
        copy.wait()


def first_model(half, owners, *refs):
    count = owners // 2
    fluxes, refs = refs[:count], refs[count:]
    if half:
        fluxes = fluxes[::-1]
        before_ref, *refs = refs
    g_ref, pick_flux_ref, target_ref, obs_ref, m_ref, x_ref, x_scr, *sums = refs
    me = lax.axis_index("cell")
    capacity = target_ref.shape[0] // owners
    absent = [jnp.zeros((BLOCKS // 2, LANES), F32)]
    flux = []
    for ref in fluxes:
        rows = [ref[:, LANES * t : LANES * (t + 1)] for t in range(CBLK_DEV // 2)]
        flux += absent + rows if half else rows + absent

    def owner_rows(ref):
        return jnp.concatenate(
            [
                ref[pl.ds(pl.multiple_of((me ^ (2 * n + half)) * capacity, capacity), capacity), :]
                for n in range(count)
            ],
            axis=0,
        )

    pair = pick_rows(owner_rows(pick_flux_ref), jnp.concatenate(flux, axis=0))
    odd = (owner_rows(target_ref).astype(jnp.int32) & 1) == 1
    x = jnp.where(odd != low(pair.shape), pair, half_swap(pair))
    for n in range(count):
        x_ref[n] = x[n * capacity : (n + 1) * capacity]

    def slot_of(i):
        return (me ^ (2 * (i // capacity) + half)) * capacity + i % capacity

    m = forward(g_ref, obs_ref, x, x_scr, sums, slot_of)
    m_ref[...] = m + before_ref[...] if half else m


def first_adjoint(order, *refs):
    parts = 1 + len(order)
    m_parts = in_turn(refs, order)
    observed_ref, weight_ref, slot_obs_ref, index_ref, h_ref, message_ref, d_ref = refs[parts:]
    d = weight_ref[...] * (tree_sum([m[...] for m in m_parts]) - observed_ref[...])
    d_ref[...] = d
    rows = h_ref.shape[3] // 2
    half = h_ref.shape[2] * rows

    def store(o, block):
        message_ref[o * rows : (o + 1) * rows, :] = block

    adjoint(h_ref, slot_obs_ref[...], d, store)
    message_ref[half:, :] = index_ref[...]


def second_model(order, *refs):
    parts = cells = 1 + len(order)
    messages = in_turn(refs, order)
    target_ref, even_ref, odd_ref, g_ref, obs_ref, m_ref, x_scr, *sums = refs[parts:]
    me = lax.axis_index("cell")
    slots = target_ref.shape[0]
    half = slots // 2
    count = max(1, half // LANES)
    group = max(1, min(cells, LANES // half))
    total = None
    for first in range(0, cells, group):
        members = messages[first : first + group]
        picks = []
        for part in range(2):
            rows = []
            for q in range(count):
                at = half + part * count + q
                row = jnp.zeros((1, LANES), F32)
                for k, ref in enumerate(members):
                    row = jnp.where(iota((1, LANES), 1) // half % group == k, ref[at : at + 1, :], row)
                rows.append(one_hot(target_ref[...] == row))
            picks.append(jnp.concatenate(rows, axis=1)[:, : group * half])
        pick = jnp.concatenate(picks, axis=0)
        values = jnp.concatenate([ref[:half, :] for ref in members], axis=0)
        found = pick_rows(jnp.concatenate([pick] * 3, axis=1), values)
        total = found if total is None else total + found
    change = jnp.where(low((slots, LANES)), total[:slots], total[slots:])
    before = []
    for o in range(cells):
        far = me ^ o
        before.append(jnp.where(far % 2 == 1, odd_ref[far // 2], even_ref[far // 2]))
    x = jnp.concatenate(before, axis=0) - 0.5 * (change + half_swap(change))
    m_ref[...] = forward(g_ref, obs_ref, x, x_scr, sums, lambda i: i)


def second_adjoint(order, *refs):
    parts = 1 + len(order)
    m_parts = in_turn(refs, order)
    observed_ref, weight_ref, first_ref, slot_obs_ref, h_ref = refs[parts : parts + 5]
    *outs, d_ref, block_scr = refs[parts + 5 :]
    me = lax.axis_index("cell")
    owners = h_ref.shape[2]
    d = weight_ref[...] * (tree_sum([m[...] for m in m_parts]) - observed_ref[...])
    d_ref[...] = d

    def store(o, block):
        block_scr[o] = block

    adjoint(h_ref, slot_obs_ref[...], -0.25 * first_ref[...] - 0.5 * d, store)
    for k in range(owners):
        outs[owners - 1 - k][...] = block_scr[me ^ k]


def prepare_increment(order, rows, *refs):
    parts = cells = 1 + len(order)
    d_ref, pick_ref, departure_ref = refs[parts:]
    messages = in_turn(refs, order)
    me = lax.axis_index("cell")
    half = cells * rows
    count = max(1, half // LANES)
    place = me * rows
    lane = iota((1, LANES), 1)
    row = iota((BLOCKS, LANES), 0)
    block = me * BLOCKS + (row % WIN_DEV) * CBLK_DEV + 2 * ((row // WIN_DEV) % 4) + row // (BLOCKS // 2)
    block = block.astype(F32)
    for part in range(2):
        for first in range(0, half, LANES):
            index = jnp.zeros((1, LANES), F32)
            for k in range(first // rows, min(cells, (first + LANES) // rows)):
                turned = pltpu.roll(
                    messages[k][half:, :], lax.rem(k * rows - place % LANES + 2 * LANES - first, LANES), 1
                )
                chosen = turned[part * count : part * count + 1]
                for q in range(1, count):
                    chosen = jnp.where(
                        place // LANES == q, turned[part * count + q : part * count + q + 1], chosen
                    )
                index = jnp.where((lane // rows) % cells == k - first // rows, chosen, index)
            pick_ref[BLOCKS * part : BLOCKS * (part + 1), first : first + LANES] = one_hot(block == index)
    for t in range(OBLK_DEV // 2):
        departure_ref[:, LANES * t : LANES * (t + 1)] = unpack_obs(d_ref[...], t)


def gather_increment(*refs):
    *arrays, pick_ref, out_ref = refs
    values = jnp.concatenate([ref[...] for ref in arrays[::-1]], axis=0)
    half = values.shape[0]
    terms = three(values)
    pick = pick_ref[...]
    if 3 * half <= LANES:
        terms.append(jnp.zeros((LANES - 3 * half, LANES), BF16))
    else:
        pick = jnp.concatenate([pick[:, :half]] * 3, axis=1)
    found = jnp.dot(pick, jnp.concatenate(terms, axis=0), preferred_element_type=F32)
    found = jnp.where(low((BLOCKS, LANES)), found[:BLOCKS], found[BLOCKS:])
    found = found + half_swap(found)
    for t in range(CBLK_DEV // 2):
        even = found[WIN_DEV * t : WIN_DEV * (t + 1)]
        odd = found[BLOCKS // 2 + WIN_DEV * t : BLOCKS // 2 + WIN_DEV * (t + 1)]
        out_ref[:, LANES * t : LANES * (t + 1)] = jnp.where(low(even.shape), even, odd)


def send(value, axis, size, k):
    return lax.ppermute(value, axis, [(i, i ^ k) for i in range(size)])


def exchange(own, sent, axis, size, order):
    return [own] + [send(sent, axis, size, k) for k in order]


def make_local(cells, wins):
    def local(prior_flux, observed, obs_weight, footprint, flux_slot, obs_slot, slot_count):
        owners, capacity = footprint.shape[2:4]
        slots = owners * capacity
        half = slots // 2
        index_rows = -(-2 * max(1, half // LANES) // 8) * 8
        params = pltpu.CompilerParams(vmem_limit_bytes=footprint.size * 4 + 16 * 2**20)
        hbm = pl.BlockSpec(memory_space=pltpu.HBM)
        smem = pl.BlockSpec(memory_space=pltpu.SMEM)
        obs, obs_out = None, pltpu.SMEM((slots,), jnp.int32)

        def call(body, outs, ins, scratch=(), space=VMEM):
            if space is hbm:
                ins = [pltpu.with_memory_space_constraint(value, pltpu.HBM) for value in ins]
                outs_at = [pltpu.VMEM(s, t) for s, t in outs[:-1]] + [obs_out]
            else:
                outs_at = [jax.ShapeDtypeStruct(s, t) for s, t in outs]
            return pl.pallas_call(
                body,
                out_shape=outs_at,
                in_specs=[smem if value is obs else space for value in ins],
                out_specs=[smem if outs_at[n] is obs_out else VMEM for n in range(len(outs))],
                scratch_shapes=list(scratch),
                compiler_params=params,
            )(*ins)

        def like(value):
            return (value.shape, value.dtype)

        obs_tile = ((OBLK_DEV, LANES), F32)
        slot_tile = ((slots, LANES), F32)
        sum_scratch = [pltpu.VMEM(*slot_tile)] + [pltpu.VMEM((OBLK_DEV + 1, TILES, LANES), F32)] * 4
        small = (flux_slot, obs_slot, slot_count, observed, obs_weight)
        turned = footprint.reshape(slots // 8, 8, TILES, LANES).transpose(0, 2, 1, 3)
        pick_flux, target, slot_obs, index, observed_t, weight_t, flux, matrices, by_slot, obs = call(
            prepare,
            [
                ((slots, 3 * owners * BLOCKS // 2), BF16),
                slot_tile,
                ((slots, 3 * OBLK_DEV), BF16),
                ((index_rows, LANES), F32),
                obs_tile,
                obs_tile,
                like(prior_flux),
                like(footprint),
                ((slots // 8, 8, TILES, LANES), F32),
                ((slots,), jnp.int32),
            ],
            (*small, prior_flux, footprint, turned),
            [
                *(pltpu.VMEM(*like(value)) for value in small),
                pltpu.SMEM(*like(obs_slot)),
                pltpu.SMEM(*like(slot_count)),
                pltpu.SemaphoreType.DMA((len(small) + 3,)),
                pltpu.SemaphoreType.DMA((owners,)),
                pltpu.SemaphoreType.DMA((8,)),
            ],
            hbm,
        )
        near_cells = list(range(1, cells))
        far_cells, far_wins = near_cells[::-1], list(range(1, wins))[::-1]
        last_wins = far_wins[-1:] + far_wins[:-1]
        fluxes = exchange(flux, prior_flux, "cell", cells, near_cells)
        half_tile = ((cells // 2, capacity, LANES), F32)
        half_scratch = [pltpu.VMEM((slots // 2, LANES), F32)] + sum_scratch[1:]
        m_even, x_even = call(
            functools.partial(first_model, 0, owners),
            [obs_tile, half_tile],
            (*fluxes[::2], by_slot, pick_flux, target, obs),
            half_scratch,
        )
        m0, x_odd = call(
            functools.partial(first_model, 1, owners),
            [obs_tile, half_tile],
            (*fluxes[1::2][::-1], m_even, by_slot, pick_flux, target, obs),
            half_scratch,
        )
        message, d0 = call(
            functools.partial(first_adjoint, far_wins),
            [((half + index_rows, LANES), F32), obs_tile],
            (*exchange(m0, m0, "win", wins, far_wins), observed_t, weight_t, slot_obs, index, matrices),
        )
        messages = exchange(message, message, "cell", cells, far_cells)
        (m1,) = call(
            functools.partial(second_model, far_cells),
            [obs_tile],
            (*messages, target, x_even, x_odd, by_slot, obs),
            sum_scratch,
        )
        *blocks, d1 = call(
            functools.partial(second_adjoint, last_wins),
            [((capacity // 2, LANES), F32)] * owners + [obs_tile],
            (*exchange(m1, m1, "win", wins, last_wins), observed_t, weight_t, d0, slot_obs, matrices),
            [pltpu.VMEM((owners, capacity // 2, LANES), F32)],
        )
        arrays = [send(block, "cell", cells, cells - 1 - i) for i, block in enumerate(blocks[:-1])]
        arrays = [blocks[-1]] + arrays[::-1]
        pick, departure = call(
            functools.partial(prepare_increment, far_cells, capacity // 2),
            [((2 * BLOCKS, max(LANES, half)), BF16), ((1, OBLK_DEV * OB), F32)],
            (*messages, d1),
        )
        (increment,) = call(
            gather_increment,
            [((WIN_DEV, CBLK_DEV * CB), F32)],
            (*arrays[::-1], pick),
        )
        return increment, departure

    return local


def solution(mesh):
    placed = (
        P(("ens", "win"), "cell"),
        P(("ens", "cell"), None),
        P(("ens", "cell"), None),
        P("cell", "win", None, None, None),
        P("cell", "win", None, None),
        P("cell", "win", None, None),
        P("cell", "win", None),
    )
    return jax.shard_map(
        make_local(mesh.shape["cell"], mesh.shape["win"]),
        mesh=mesh,
        in_specs=placed,
        out_specs=(P(("ens", "win"), "cell"), P(("ens", "cell"), None)),
        check_vma=False,
    )
```

```python
import functools
import jax
import jax.numpy as jnp
from jax import lax
from jax.experimental import pallas as pl
from jax.experimental.pallas import tpu as pltpu
from jax.sharding import PartitionSpec as P

CB = 64
OB = 64
CBLK_DEV = 8
WIN_DEV = 8
OBLK_DEV = 8
BLOCKS = WIN_DEV * CBLK_DEV
LANES = 128
TILES = OB * CB // LANES

F32 = jnp.float32
BF16 = jnp.bfloat16
VMEM = pl.BlockSpec(memory_space=pltpu.VMEM)


def iota(shape, dim):
    return lax.broadcasted_iota(jnp.int32, shape, dim)


def one_hot(where):
    return jnp.where(where, 1.0, 0.0).astype(BF16)


def three(value):
    first = value.astype(BF16)
    rest = value - first.astype(F32)
    second = rest.astype(BF16)
    third = (rest - second.astype(F32)).astype(BF16)
    return [first, second, third]


def pick_rows(pick3, value):
    return jnp.dot(pick3, jnp.concatenate(three(value), axis=0), preferred_element_type=F32)


def half_swap(value):
    return pltpu.roll(value, LANES // 2, 1)


def low(shape):
    return iota(shape, 1) < LANES // 2


def tree_sum(parts):
    parts = list(parts)
    while len(parts) > 1:
        parts = [sum(parts[i + 1 : i + 2], parts[i]) for i in range(0, len(parts), 2)]
    return parts[0]


def pack_obs(row):
    lane = iota((8, LANES), 1)
    block = (lane >> 1) & 31
    place = 16 * (block & 7) + 2 * iota(lane.shape, 0) + (lane >> 6)
    out = jnp.zeros(lane.shape, F32)
    for t in range(OBLK_DEV // 2):
        tile = jnp.broadcast_to(row[:, LANES * t : LANES * (t + 1)], lane.shape)
        found = jnp.take_along_axis(tile, place, axis=1, mode="promise_in_bounds")
        out = jnp.where(block >> 3 == t, found, out)
    return out


def unpack_obs(packed, t):
    lane = iota(packed.shape, 1)
    place = (lane & 1) * OB + 2 * (8 * t + (lane >> 4))
    found = jnp.take_along_axis(packed, place, axis=1, mode="promise_in_bounds")
    here = (lane & 15) >> 1 == iota(packed.shape, 0)
    return jnp.sum(jnp.where(here, found, 0.0), axis=0, keepdims=True)


def lane_sums(tiles):
    terms = jnp.concatenate(three(jnp.concatenate(tiles, axis=0)), axis=1)
    shape = (3 * LANES, LANES)
    ones = one_hot((iota(shape, 0) // OB) % 2 == iota(shape, 1) // OB)
    sums = jnp.dot(terms, ones, preferred_element_type=F32)
    out = sums[:8]
    tile = (iota(out.shape, 1) >> 1) & 31
    for q in range(1, len(tiles)):
        out = jnp.where(tile == q, sums[8 * q : 8 * q + 8], out)
    return out


def h_columns(h_ref, first, last, start, size):
    return jnp.concatenate([h_ref[0, 0, o, :, start : start + size] for o in range(first, last)], axis=0)


def forward(g_ref, obs_ref, x, x_scr, sums):
    slots = x.shape[0]
    sets = len(sums)
    x_scr[...] = x
    for ref in sums:
        ref[...] = jnp.zeros(ref.shape, F32)

    steps = slots // sets
    run = min(steps, 32)

    def products(j):
        at = [n * steps + j for n in range(sets)]
        return [(obs_ref[s], g_ref[s // 8, s % 8] * x_scr[pl.ds(s, 1), :]) for s in at]

    def step(first, carry):
        coming = products(first * run)
        for j in range(run):
            now = coming
            totals = [ref[block] + value for ref, (block, value) in zip(sums, now)]
            if j + 1 < run:
                coming = products(first * run + j + 1)
            for ref, (block, _), total in zip(sums, now, totals):
                ref[block] = total
        return carry

    lax.fori_loop(0, steps // run, step, 0)
    rows = OBLK_DEV * TILES // 8
    tiles = []
    for q in range(rows):
        at = (q // 4, slice(8 * (q % 4), 8 * (q % 4) + 8))
        tiles.append(tree_sum([ref[at] for ref in sums]))
    return lane_sums(tiles)


def adjoint(h_ref, slot_obs, d, store):
    owners, capacity = h_ref.shape[2], h_ref.shape[3]
    place = (iota(d.shape, 1) & OB) + 8 * iota(d.shape, 0)
    spread = jnp.concatenate(
        [
            jnp.take_along_axis(
                jnp.broadcast_to(d[t % 8 : t % 8 + 1], d.shape),
                place + 2 * (t // 8),
                axis=1,
                mode="promise_in_bounds",
            )
            for t in range(TILES)
        ],
        axis=1,
    )
    spread = jnp.concatenate([term.astype(F32) for term in three(spread)], axis=0).astype(BF16)
    group = min(owners, 4)
    for first in range(0, owners, group):
        rows = slice(first * capacity, (first + group) * capacity)
        total = None
        for t in range(TILES // 2):
            columns = slice(2 * LANES * t, 2 * LANES * (t + 1))
            given = jnp.dot(slot_obs[rows], spread[:, columns], preferred_element_type=F32)
            terms = h_columns(h_ref, first, first + group, 2 * LANES * t, 2 * LANES) * given
            total = terms if total is None else total + terms
        total = total[:, :LANES] + total[:, LANES:]
        total = total + half_swap(total)
        for o in range(group):
            upper_half = o * capacity + capacity // 2
            pair = total[o * capacity : upper_half], total[upper_half : (o + 1) * capacity]
            store(first + o, jnp.where(low(pair[0].shape), *pair))


def prepare(
    fslot_hbm, oslot_hbm, count_hbm, observed_hbm, weight_hbm, flux_hbm, h_hbm, g_hbm,
    pick_flux_ref, target_ref, slot_obs_ref, index_ref, observed_out, weight_out, flux_ref, h_ref, g_ref, obs_ref,
    fslot_ref, oslot_ref, count_ref, observed_ref, weight_ref, oslot_scalars, count_scalars, sems, h_sems, g_sems,
):
    me = lax.axis_index("cell")
    owners, capacity = fslot_ref.shape[2:]
    pairs = (
        (fslot_hbm, fslot_ref),
        (oslot_hbm, oslot_ref),
        (count_hbm, count_ref),
        (observed_hbm, observed_ref),
        (weight_hbm, weight_ref),
        (flux_hbm, flux_ref),
        (oslot_hbm, oslot_scalars),
        (count_hbm, count_scalars),
    )
    small = [pltpu.make_async_copy(src, dst, sems.at[i]) for i, (src, dst) in enumerate(pairs)]
    large = [
        pltpu.make_async_copy(h_hbm.at[:, :, o], h_ref.at[:, :, o], h_sems.at[o])
        for o in range(owners)
    ]
    for copy in small + large:
        copy.start()

    turned = [
        pltpu.make_async_copy(g_hbm.at[:, :, r], g_ref.at[:, r], g_sems.at[r]) for r in range(8)
    ]
    for copy in turned:
        copy.start()
    for copy in small:
        copy.wait()

    def scalar_step(o, carry):
        for j in range(capacity):
            obs_ref[o * capacity + j] = jnp.where(
                j < count_scalars[0, 0, o], oslot_scalars[0, 0, o, j], OBLK_DEV
            )
        return carry

    lax.fori_loop(0, owners, scalar_step, 0, unroll=owners <= 4)
    slots = owners * capacity
    eye = iota((capacity, capacity), 0) == iota((capacity, capacity), 1)

    def column(ref):
        return jnp.concatenate(
            [
                jnp.sum(
                    jnp.where(eye, jnp.broadcast_to(ref[0, 0, o : o + 1, :], eye.shape), 0),
                    axis=1,
                    keepdims=True,
                )
                for o in range(owners)
            ],
            axis=0,
        )

    fslot, oslot = column(fslot_ref), column(oslot_ref)
    counts = jnp.concatenate(
        [
            jnp.broadcast_to(count_ref[0, 0:1, o : o + 1], (capacity, 1))
            for o in range(owners)
        ],
        axis=0,
    )
    slot = iota((slots, 1), 0)
    owner = slot // capacity
    live = (slot - owner * capacity) < counts
    oslot = jnp.where(live, oslot, OBLK_DEV)
    target = owner * BLOCKS + fslot
    target_ref[...] = jnp.broadcast_to(target.astype(F32), target_ref.shape)

    depth = owners * BLOCKS // 2
    row = (owner ^ me) * (BLOCKS // 2) + ((fslot & 7) >> 1) * WIN_DEV + (fslot >> 3)
    pick_flux_ref[...] = one_hot(iota((slots, 3 * depth), 1) % depth == row)
    slot_obs_ref[...] = one_hot((iota((slots, 3 * OBLK_DEV), 1) % OBLK_DEV) == oslot)

    half = slots // 2
    count = max(1, half // LANES)
    index_ref[...] = jnp.zeros(index_ref.shape, F32)
    for part in range(2):
        for q in range(count):
            r = (iota((slots, LANES), 1) + LANES * q) % half
            at = (r // (capacity // 2)) * capacity + r % (capacity // 2) + part * (capacity // 2)
            index_ref[pl.ds(part * count + q, 1), :] = jnp.sum(
                jnp.where(iota((slots, LANES), 0) == at, target.astype(F32), 0.0),
                axis=0,
                keepdims=True,
            )
    observed_out[...] = pack_obs(observed_ref[...])
    weight_out[...] = pack_obs(weight_ref[...])
    for copy in large + turned:
        copy.wait()


def first_model(order, *refs):
    parts = len(order)
    g_ref, pick_flux_ref, target_ref, obs_ref, m_ref, x_ref, x_scr, *sums = refs[parts:]
    flux = jnp.concatenate(
        [
            ref[:, LANES * t : LANES * (t + 1)]
            for ref in [refs[order.index(k)] for k in range(parts)]
            for t in range(CBLK_DEV // 2)
        ],
        axis=0,
    )
    pair = pick_rows(pick_flux_ref[...], flux)
    odd = (target_ref[...].astype(jnp.int32) & 1) == 1
    x = jnp.where(odd != low(pair.shape), pair, half_swap(pair))
    x_ref[...] = x
    m_ref[...] = forward(g_ref, obs_ref, x, x_scr, sums)


def first_adjoint(parts, *refs):
    observed_ref, weight_ref, slot_obs_ref, index_ref, h_ref, message_ref, d_ref = refs[parts:]
    d = weight_ref[...] * (tree_sum([m[...] for m in refs[:parts]]) - observed_ref[...])
    d_ref[...] = d
    rows = h_ref.shape[3] // 2
    half = h_ref.shape[2] * rows

    def store(o, block):
        message_ref[o * rows : (o + 1) * rows, :] = block

    adjoint(h_ref, slot_obs_ref[...], d, store)
    message_ref[half:, :] = index_ref[...]


def second_model(parts, *refs):
    messages = refs[:parts]
    cells = parts
    target_ref, x_ref, g_ref, obs_ref, m_ref, x_scr, *sums = refs[parts:]
    slots = target_ref.shape[0]
    half = slots // 2
    count = max(1, half // LANES)
    group = max(1, min(cells, LANES // half))
    total = None
    for first in range(0, cells, group):
        members = messages[first : first + group]
        picks = []
        for part in range(2):
            rows = []
            for q in range(count):
                at = half + part * count + q
                row = jnp.zeros((1, LANES), F32)
                for k, ref in enumerate(members):
                    row = jnp.where(iota((1, LANES), 1) // half % group == k, ref[at : at + 1, :], row)
                rows.append(one_hot(target_ref[...] == row))
            picks.append(jnp.concatenate(rows, axis=1)[:, : group * half])
        pick = jnp.concatenate(picks, axis=0)
        values = jnp.concatenate([ref[:half, :] for ref in members], axis=0)
        found = pick_rows(jnp.concatenate([pick] * 3, axis=1), values)
        total = found if total is None else total + found
    change = jnp.where(low((slots, LANES)), total[:slots], total[slots:])
    x = x_ref[...] - 0.5 * (change + half_swap(change))
    m_ref[...] = forward(g_ref, obs_ref, x, x_scr, sums)


def second_adjoint(parts, *refs):
    observed_ref, weight_ref, first_ref, slot_obs_ref, h_ref = refs[parts : parts + 5]
    *outs, d_ref, block_scr = refs[parts + 5 :]
    me = lax.axis_index("cell")
    owners = h_ref.shape[2]
    d = weight_ref[...] * (tree_sum([m[...] for m in refs[:parts]]) - observed_ref[...])
    d_ref[...] = d

    def store(o, block):
        block_scr[o] = block

    adjoint(h_ref, slot_obs_ref[...], -0.25 * first_ref[...] - 0.5 * d, store)
    for k in range(owners):
        outs[owners - 1 - k][...] = block_scr[me ^ k]


def prepare_increment(parts, rows, *refs):
    d_ref, pick_ref, departure_ref = refs[parts:]
    messages = refs[:parts]
    cells = parts
    me = lax.axis_index("cell")
    half = cells * rows
    count = max(1, half // LANES)
    place = me * rows
    lane = iota((1, LANES), 1)
    row = iota((BLOCKS, LANES), 0)
    block = me * BLOCKS + (row % WIN_DEV) * CBLK_DEV + 2 * ((row // WIN_DEV) % 4) + row // (BLOCKS // 2)
    block = block.astype(F32)
    for part in range(2):
        for first in range(0, half, LANES):
            index = jnp.zeros((1, LANES), F32)
            for k in range(first // rows, min(cells, (first + LANES) // rows)):
                turned = pltpu.roll(
                    messages[k][half:, :], lax.rem(k * rows - place % LANES + 2 * LANES - first, LANES), 1
                )
                chosen = turned[part * count : part * count + 1]
                for q in range(1, count):
                    chosen = jnp.where(
                        place // LANES == q, turned[part * count + q : part * count + q + 1], chosen
                    )
                index = jnp.where((lane // rows) % cells == k - first // rows, chosen, index)
            pick_ref[BLOCKS * part : BLOCKS * (part + 1), first : first + LANES] = one_hot(block == index)
    for t in range(OBLK_DEV // 2):
        departure_ref[:, LANES * t : LANES * (t + 1)] = unpack_obs(d_ref[...], t)


def gather_increment(*refs):
    *arrays, pick_ref, out_ref = refs
    values = jnp.concatenate([ref[...] for ref in arrays[::-1]], axis=0)
    half = values.shape[0]
    terms = three(values)
    pick = pick_ref[...]
    if 3 * half <= LANES:
        terms.append(jnp.zeros((LANES - 3 * half, LANES), BF16))
    else:
        pick = jnp.concatenate([pick[:, :half]] * 3, axis=1)
    found = jnp.dot(pick, jnp.concatenate(terms, axis=0), preferred_element_type=F32)
    found = jnp.where(low((BLOCKS, LANES)), found[:BLOCKS], found[BLOCKS:])
    found = found + half_swap(found)
    for t in range(CBLK_DEV // 2):
        even = found[WIN_DEV * t : WIN_DEV * (t + 1)]
        odd = found[BLOCKS // 2 + WIN_DEV * t : BLOCKS // 2 + WIN_DEV * (t + 1)]
        out_ref[:, LANES * t : LANES * (t + 1)] = jnp.where(low(even.shape), even, odd)


def send(value, axis, size, k):
    return lax.ppermute(value, axis, [(i, i ^ k) for i in range(size)])


def exchange(own, sent, axis, size):
    return [own] + [send(sent, axis, size, k) for k in range(size - 1, 0, -1)][::-1]


def make_local(cells, wins):
    def local(prior_flux, observed, obs_weight, footprint, flux_slot, obs_slot, slot_count):
        owners, capacity = footprint.shape[2:4]
        slots = owners * capacity
        half = slots // 2
        index_rows = -(-2 * max(1, half // LANES) // 8) * 8
        params = pltpu.CompilerParams(vmem_limit_bytes=footprint.size * 4 + 16 * 2**20)
        hbm = pl.BlockSpec(memory_space=pltpu.HBM)
        smem = pl.BlockSpec(memory_space=pltpu.SMEM)
        obs, obs_out = None, pltpu.SMEM((slots,), jnp.int32)

        def call(body, outs, ins, scratch=(), space=VMEM):
            if space is hbm:
                ins = [pltpu.with_memory_space_constraint(value, pltpu.HBM) for value in ins]
                outs_at = [pltpu.VMEM(s, t) for s, t in outs[:-1]] + [obs_out]
            else:
                outs_at = [jax.ShapeDtypeStruct(s, t) for s, t in outs]
            return pl.pallas_call(
                body,
                out_shape=outs_at,
                in_specs=[smem if value is obs else space for value in ins],
                out_specs=[smem if outs_at[n] is obs_out else VMEM for n in range(len(outs))],
                scratch_shapes=list(scratch),
                compiler_params=params,
            )(*ins)

        def like(value):
            return (value.shape, value.dtype)

        obs_tile = ((OBLK_DEV, LANES), F32)
        slot_tile = ((slots, LANES), F32)
        sum_scratch = [pltpu.VMEM(*slot_tile)] + [pltpu.VMEM((OBLK_DEV + 1, TILES, LANES), F32)] * 2
        small = (flux_slot, obs_slot, slot_count, observed, obs_weight)
        turned = footprint.reshape(slots // 8, 8, TILES, LANES).transpose(0, 2, 1, 3)
        pick_flux, target, slot_obs, index, observed_t, weight_t, flux, matrices, by_slot, obs = call(
            prepare,
            [
                ((slots, 3 * owners * BLOCKS // 2), BF16),
                slot_tile,
                ((slots, 3 * OBLK_DEV), BF16),
                ((index_rows, LANES), F32),
                obs_tile,
                obs_tile,
                like(prior_flux),
                like(footprint),
                ((slots // 8, 8, TILES, LANES), F32),
                ((slots,), jnp.int32),
            ],
            (*small, prior_flux, footprint, turned),
            [
                *(pltpu.VMEM(*like(value)) for value in small),
                pltpu.SMEM(*like(obs_slot)),
                pltpu.SMEM(*like(slot_count)),
                pltpu.SemaphoreType.DMA((len(small) + 3,)),
                pltpu.SemaphoreType.DMA((owners,)),
                pltpu.SemaphoreType.DMA((8,)),
            ],
            hbm,
        )
        order = [0, cells // 2, *range(1, cells // 2), *range(cells // 2 + 1, cells)]
        fluxes = exchange(flux, prior_flux, "cell", cells)
        m0, x0 = call(
            functools.partial(first_model, order),
            [obs_tile, slot_tile],
            (*(fluxes[k] for k in order), by_slot, pick_flux, target, obs),
            sum_scratch,
        )
        message, d0 = call(
            functools.partial(first_adjoint, wins),
            [((half + index_rows, LANES), F32), obs_tile],
            (*exchange(m0, m0, "win", wins), observed_t, weight_t, slot_obs, index, matrices),
        )
        messages = exchange(message, message, "cell", cells)
        (m1,) = call(
            functools.partial(second_model, cells),
            [obs_tile],
            (*messages, target, x0, by_slot, obs),
            sum_scratch,
        )
        *blocks, d1 = call(
            functools.partial(second_adjoint, wins),
            [((capacity // 2, LANES), F32)] * owners + [obs_tile],
            (*exchange(m1, m1, "win", wins), observed_t, weight_t, d0, slot_obs, matrices),
            [pltpu.VMEM((owners, capacity // 2, LANES), F32)],
        )
        arrays = [send(block, "cell", cells, cells - 1 - i) for i, block in enumerate(blocks[:-1])]
        arrays = [blocks[-1]] + arrays[::-1]
        pick, departure = call(
            functools.partial(prepare_increment, cells, capacity // 2),
            [((2 * BLOCKS, max(LANES, half)), BF16), ((1, OBLK_DEV * OB), F32)],
            (*messages, d1),
        )
        (increment,) = call(
            gather_increment,
            [((WIN_DEV, CBLK_DEV * CB), F32)],
            (*arrays[::-1], pick),
        )
        return increment, departure

    return local


def solution(mesh):
    placed = (
        P(("ens", "win"), "cell"),
        P(("ens", "cell"), None),
        P(("ens", "cell"), None),
        P("cell", "win", None, None, None),
        P("cell", "win", None, None),
        P("cell", "win", None, None),
        P("cell", "win", None),
    )
    return jax.shard_map(
        make_local(mesh.shape["cell"], mesh.shape["win"]),
        mesh=mesh,
        in_specs=placed,
        out_specs=(P(("ens", "win"), "cell"), P(("ens", "cell"), None)),
        check_vma=False,
    )
```

```python
import functools
import jax
import jax.numpy as jnp
from jax import lax
from jax.experimental import pallas as pl
from jax.experimental.pallas import tpu as pltpu
from jax.sharding import PartitionSpec as P

CB = 64
OB = 64
CBLK_DEV = 8
WIN_DEV = 8
OBLK_DEV = 8
BLOCKS = WIN_DEV * CBLK_DEV
LANES = 128
TILES = OB * CB // LANES

F32 = jnp.float32
BF16 = jnp.bfloat16
VMEM = pl.BlockSpec(memory_space=pltpu.VMEM)


def iota(shape, dim):
    return lax.broadcasted_iota(jnp.int32, shape, dim)


def one_hot(where):
    return jnp.where(where, 1.0, 0.0).astype(BF16)


def three(value):
    first = value.astype(BF16)
    rest = value - first.astype(F32)
    second = rest.astype(BF16)
    third = (rest - second.astype(F32)).astype(BF16)
    return [first, second, third]


def pick_rows(pick3, value):
    return jnp.dot(pick3, jnp.concatenate(three(value), axis=0), preferred_element_type=F32)


def half_swap(value):
    return pltpu.roll(value, LANES // 2, 1)


def low(shape):
    return iota(shape, 1) < LANES // 2


def tree_sum(parts):
    parts = list(parts)
    while len(parts) > 1:
        parts = [sum(parts[i + 1 : i + 2], parts[i]) for i in range(0, len(parts), 2)]
    return parts[0]


def pack_obs(row):
    lane = iota((8, LANES), 1)
    block = (lane >> 1) & 31
    place = 16 * (block & 7) + 2 * iota(lane.shape, 0) + (lane >> 6)
    out = jnp.zeros(lane.shape, F32)
    for t in range(OBLK_DEV // 2):
        tile = jnp.broadcast_to(row[:, LANES * t : LANES * (t + 1)], lane.shape)
        found = jnp.take_along_axis(tile, place, axis=1, mode="promise_in_bounds")
        out = jnp.where(block >> 3 == t, found, out)
    return out


def unpack_obs(packed, t):
    lane = iota(packed.shape, 1)
    place = (lane & 1) * OB + 2 * (8 * t + (lane >> 4))
    found = jnp.take_along_axis(packed, place, axis=1, mode="promise_in_bounds")
    here = (lane & 15) >> 1 == iota(packed.shape, 0)
    return jnp.sum(jnp.where(here, found, 0.0), axis=0, keepdims=True)


def lane_sums(tiles):
    terms = jnp.concatenate(three(jnp.concatenate(tiles, axis=0)), axis=1)
    shape = (3 * LANES, LANES)
    ones = one_hot((iota(shape, 0) // OB) % 2 == iota(shape, 1) // OB)
    sums = jnp.dot(terms, ones, preferred_element_type=F32)
    out = sums[:8]
    tile = (iota(out.shape, 1) >> 1) & 31
    for q in range(1, len(tiles)):
        out = jnp.where(tile == q, sums[8 * q : 8 * q + 8], out)
    return out


def h_columns(h_ref, first, last, start, size):
    return jnp.concatenate([h_ref[0, 0, o, :, start : start + size] for o in range(first, last)], axis=0)


def forward(g_ref, obs_ref, x, x_scr, sums):
    slots = x.shape[0]
    sets = len(sums)
    x_scr[...] = x
    for ref in sums:
        ref[...] = jnp.zeros(ref.shape, F32)

    steps = slots // sets
    run = min(steps, 32)

    def products(j):
        at = [n * steps + j for n in range(sets)]
        return [(obs_ref[s], g_ref[s // 8, s % 8] * x_scr[pl.ds(s, 1), :]) for s in at]

    def step(first, carry):
        coming = products(first * run)
        for j in range(run):
            now = coming
            totals = [ref[block] + value for ref, (block, value) in zip(sums, now)]
            if j + 1 < run:
                coming = products(first * run + j + 1)
            for ref, (block, _), total in zip(sums, now, totals):
                ref[block] = total
        return carry

    lax.fori_loop(0, steps // run, step, 0)
    rows = OBLK_DEV * TILES // 8
    tiles = []
    for q in range(rows):
        at = (q // 4, slice(8 * (q % 4), 8 * (q % 4) + 8))
        tiles.append(tree_sum([ref[at] for ref in sums]))
    return lane_sums(tiles)


def adjoint(h_ref, slot_obs, d, store):
    owners, capacity = h_ref.shape[2], h_ref.shape[3]
    place = (iota(d.shape, 1) & OB) + 8 * iota(d.shape, 0)
    spread = jnp.concatenate(
        [
            jnp.take_along_axis(
                jnp.broadcast_to(d[t % 8 : t % 8 + 1], d.shape),
                place + 2 * (t // 8),
                axis=1,
                mode="promise_in_bounds",
            )
            for t in range(TILES)
        ],
        axis=1,
    )
    spread = jnp.concatenate([term.astype(F32) for term in three(spread)], axis=0).astype(BF16)
    group = min(owners, 4)
    for first in range(0, owners, group):
        rows = slice(first * capacity, (first + group) * capacity)
        total = None
        for t in range(TILES // 2):
            columns = slice(2 * LANES * t, 2 * LANES * (t + 1))
            given = jnp.dot(slot_obs[rows], spread[:, columns], preferred_element_type=F32)
            terms = h_columns(h_ref, first, first + group, 2 * LANES * t, 2 * LANES) * given
            total = terms if total is None else total + terms
        total = total[:, :LANES] + total[:, LANES:]
        total = total + half_swap(total)
        for o in range(group):
            upper_half = o * capacity + capacity // 2
            pair = total[o * capacity : upper_half], total[upper_half : (o + 1) * capacity]
            store(first + o, jnp.where(low(pair[0].shape), *pair))


def prepare(
    fslot_hbm, oslot_hbm, count_hbm, observed_hbm, weight_hbm, flux_hbm, h_hbm, g_hbm,
    pick_flux_ref, target_ref, slot_obs_ref, index_ref, observed_out, weight_out, flux_ref, h_ref, g_ref, obs_ref,
    fslot_ref, oslot_ref, count_ref, observed_ref, weight_ref, oslot_scalars, count_scalars, sems, h_sems, g_sems,
):
    me = lax.axis_index("cell")
    owners, capacity = fslot_ref.shape[2:]
    pairs = (
        (fslot_hbm, fslot_ref),
        (oslot_hbm, oslot_ref),
        (count_hbm, count_ref),
        (observed_hbm, observed_ref),
        (weight_hbm, weight_ref),
        (flux_hbm, flux_ref),
        (oslot_hbm, oslot_scalars),
        (count_hbm, count_scalars),
    )
    small = [pltpu.make_async_copy(src, dst, sems.at[i]) for i, (src, dst) in enumerate(pairs)]
    large = [
        pltpu.make_async_copy(h_hbm.at[:, :, o], h_ref.at[:, :, o], h_sems.at[o])
        for o in range(owners)
    ]
    for copy in small + large:
        copy.start()

    turned = [
        pltpu.make_async_copy(g_hbm.at[:, :, r], g_ref.at[:, r], g_sems.at[r]) for r in range(8)
    ]
    for copy in turned:
        copy.start()
    for copy in small:
        copy.wait()

    def scalar_step(o, carry):
        for j in range(capacity):
            obs_ref[o * capacity + j] = jnp.where(
                j < count_scalars[0, 0, o], oslot_scalars[0, 0, o, j], OBLK_DEV
            )
        return carry

    lax.fori_loop(0, owners, scalar_step, 0, unroll=owners <= 4)
    slots = owners * capacity
    eye = iota((capacity, capacity), 0) == iota((capacity, capacity), 1)

    def column(ref):
        return jnp.concatenate(
            [
                jnp.sum(
                    jnp.where(eye, jnp.broadcast_to(ref[0, 0, o : o + 1, :], eye.shape), 0),
                    axis=1,
                    keepdims=True,
                )
                for o in range(owners)
            ],
            axis=0,
        )

    fslot, oslot = column(fslot_ref), column(oslot_ref)
    counts = jnp.concatenate(
        [
            jnp.broadcast_to(count_ref[0, 0:1, o : o + 1], (capacity, 1))
            for o in range(owners)
        ],
        axis=0,
    )
    slot = iota((slots, 1), 0)
    owner = slot // capacity
    live = (slot - owner * capacity) < counts
    oslot = jnp.where(live, oslot, OBLK_DEV)
    target = owner * BLOCKS + fslot
    target_ref[...] = jnp.broadcast_to(target.astype(F32), target_ref.shape)

    depth = owners * BLOCKS // 2
    row = (owner ^ me) * (BLOCKS // 2) + ((fslot & 7) >> 1) * WIN_DEV + (fslot >> 3)
    pick_flux_ref[...] = one_hot(iota((slots, 3 * depth), 1) % depth == row)
    slot_obs_ref[...] = one_hot((iota((slots, 3 * OBLK_DEV), 1) % OBLK_DEV) == oslot)

    half = slots // 2
    count = max(1, half // LANES)
    index_ref[...] = jnp.zeros(index_ref.shape, F32)
    for part in range(2):
        for q in range(count):
            r = (iota((slots, LANES), 1) + LANES * q) % half
            at = (r // (capacity // 2)) * capacity + r % (capacity // 2) + part * (capacity // 2)
            index_ref[pl.ds(part * count + q, 1), :] = jnp.sum(
                jnp.where(iota((slots, LANES), 0) == at, target.astype(F32), 0.0),
                axis=0,
                keepdims=True,
            )
    observed_out[...] = pack_obs(observed_ref[...])
    weight_out[...] = pack_obs(weight_ref[...])
    for copy in large + turned:
        copy.wait()


def first_model(order, *refs):
    parts = len(order)
    g_ref, pick_flux_ref, target_ref, obs_ref, m_ref, x_ref, x_scr, *sums = refs[parts:]
    flux = jnp.concatenate(
        [
            ref[:, LANES * t : LANES * (t + 1)]
            for ref in [refs[order.index(k)] for k in range(parts)]
            for t in range(CBLK_DEV // 2)
        ],
        axis=0,
    )
    pair = pick_rows(pick_flux_ref[...], flux)
    odd = (target_ref[...].astype(jnp.int32) & 1) == 1
    x = jnp.where(odd != low(pair.shape), pair, half_swap(pair))
    x_ref[...] = x
    m_ref[...] = forward(g_ref, obs_ref, x, x_scr, sums)


def first_adjoint(parts, *refs):
    observed_ref, weight_ref, slot_obs_ref, index_ref, h_ref, message_ref, d_ref = refs[parts:]
    d = weight_ref[...] * (tree_sum([m[...] for m in refs[:parts]]) - observed_ref[...])
    d_ref[...] = d
    rows = h_ref.shape[3] // 2
    half = h_ref.shape[2] * rows

    def store(o, block):
        message_ref[o * rows : (o + 1) * rows, :] = block

    adjoint(h_ref, slot_obs_ref[...], d, store)
    message_ref[half:, :] = index_ref[...]


def second_model(parts, *refs):
    messages = refs[:parts]
    cells = parts
    target_ref, x_ref, g_ref, obs_ref, m_ref, x_scr, *sums = refs[parts:]
    slots = target_ref.shape[0]
    half = slots // 2
    count = max(1, half // LANES)
    group = max(1, min(cells, LANES // half))
    total = None
    for first in range(0, cells, group):
        members = messages[first : first + group]
        picks = []
        for part in range(2):
            rows = []
            for q in range(count):
                at = half + part * count + q
                row = jnp.zeros((1, LANES), F32)
                for k, ref in enumerate(members):
                    row = jnp.where(iota((1, LANES), 1) // half % group == k, ref[at : at + 1, :], row)
                rows.append(one_hot(target_ref[...] == row))
            picks.append(jnp.concatenate(rows, axis=1)[:, : group * half])
        pick = jnp.concatenate(picks, axis=0)
        values = jnp.concatenate([ref[:half, :] for ref in members], axis=0)
        found = pick_rows(jnp.concatenate([pick] * 3, axis=1), values)
        total = found if total is None else total + found
    change = jnp.where(low((slots, LANES)), total[:slots], total[slots:])
    x = x_ref[...] - 0.5 * (change + half_swap(change))
    m_ref[...] = forward(g_ref, obs_ref, x, x_scr, sums)


def second_adjoint(parts, *refs):
    observed_ref, weight_ref, first_ref, slot_obs_ref, h_ref = refs[parts : parts + 5]
    *outs, d_ref, block_scr = refs[parts + 5 :]
    me = lax.axis_index("cell")
    owners = h_ref.shape[2]
    d = weight_ref[...] * (tree_sum([m[...] for m in refs[:parts]]) - observed_ref[...])
    d_ref[...] = d

    def store(o, block):
        block_scr[o] = block

    adjoint(h_ref, slot_obs_ref[...], -0.25 * first_ref[...] - 0.5 * d, store)
    for k in range(owners):
        outs[owners - 1 - k][...] = block_scr[me ^ k]


def prepare_increment(parts, rows, *refs):
    d_ref, pick_ref, departure_ref = refs[parts:]
    messages = refs[:parts]
    cells = parts
    me = lax.axis_index("cell")
    half = cells * rows
    count = max(1, half // LANES)
    place = me * rows
    lane = iota((1, LANES), 1)
    row = iota((BLOCKS, LANES), 0)
    block = me * BLOCKS + (row % WIN_DEV) * CBLK_DEV + 2 * ((row // WIN_DEV) % 4) + row // (BLOCKS // 2)
    block = block.astype(F32)
    for part in range(2):
        for first in range(0, half, LANES):
            index = jnp.zeros((1, LANES), F32)
            for k in range(first // rows, min(cells, (first + LANES) // rows)):
                turned = pltpu.roll(
                    messages[k][half:, :], lax.rem(k * rows - place % LANES + 2 * LANES - first, LANES), 1
                )
                chosen = turned[part * count : part * count + 1]
                for q in range(1, count):
                    chosen = jnp.where(
                        place // LANES == q, turned[part * count + q : part * count + q + 1], chosen
                    )
                index = jnp.where((lane // rows) % cells == k - first // rows, chosen, index)
            pick_ref[BLOCKS * part : BLOCKS * (part + 1), first : first + LANES] = one_hot(block == index)
    for t in range(OBLK_DEV // 2):
        departure_ref[:, LANES * t : LANES * (t + 1)] = unpack_obs(d_ref[...], t)


def gather_increment(*refs):
    *arrays, pick_ref, out_ref = refs
    values = jnp.concatenate([ref[...] for ref in arrays[::-1]], axis=0)
    half = values.shape[0]
    terms = three(values)
    pick = pick_ref[...]
    if 3 * half <= LANES:
        terms.append(jnp.zeros((LANES - 3 * half, LANES), BF16))
    else:
        pick = jnp.concatenate([pick[:, :half]] * 3, axis=1)
    found = jnp.dot(pick, jnp.concatenate(terms, axis=0), preferred_element_type=F32)
    found = jnp.where(low((BLOCKS, LANES)), found[:BLOCKS], found[BLOCKS:])
    found = found + half_swap(found)
    for t in range(CBLK_DEV // 2):
        even = found[WIN_DEV * t : WIN_DEV * (t + 1)]
        odd = found[BLOCKS // 2 + WIN_DEV * t : BLOCKS // 2 + WIN_DEV * (t + 1)]
        out_ref[:, LANES * t : LANES * (t + 1)] = jnp.where(low(even.shape), even, odd)


def send(value, axis, size, k):
    return lax.ppermute(value, axis, [(i, i ^ k) for i in range(size)])


def exchange(own, sent, axis, size):
    return [own] + [send(sent, axis, size, k) for k in range(size - 1, 0, -1)][::-1]


def make_local(cells, wins):
    def local(prior_flux, observed, obs_weight, footprint, flux_slot, obs_slot, slot_count):
        owners, capacity = footprint.shape[2:4]
        slots = owners * capacity
        half = slots // 2
        index_rows = -(-2 * max(1, half // LANES) // 8) * 8
        params = pltpu.CompilerParams(vmem_limit_bytes=footprint.size * 4 + 16 * 2**20)
        hbm = pl.BlockSpec(memory_space=pltpu.HBM)
        smem = pl.BlockSpec(memory_space=pltpu.SMEM)
        obs, obs_out = None, pltpu.SMEM((slots,), jnp.int32)

        def call(body, outs, ins, scratch=(), space=VMEM):
            if space is hbm:
                ins = [pltpu.with_memory_space_constraint(value, pltpu.HBM) for value in ins]
                outs_at = [pltpu.VMEM(s, t) for s, t in outs[:-1]] + [obs_out]
            else:
                outs_at = [jax.ShapeDtypeStruct(s, t) for s, t in outs]
            return pl.pallas_call(
                body,
                out_shape=outs_at,
                in_specs=[smem if value is obs else space for value in ins],
                out_specs=[smem if outs_at[n] is obs_out else VMEM for n in range(len(outs))],
                scratch_shapes=list(scratch),
                compiler_params=params,
            )(*ins)

        def like(value):
            return (value.shape, value.dtype)

        obs_tile = ((OBLK_DEV, LANES), F32)
        slot_tile = ((slots, LANES), F32)
        sum_scratch = [pltpu.VMEM(*slot_tile)] + [pltpu.VMEM((OBLK_DEV + 1, TILES, LANES), F32)] * 8
        small = (flux_slot, obs_slot, slot_count, observed, obs_weight)
        turned = footprint.reshape(slots // 8, 8, TILES, LANES).transpose(0, 2, 1, 3)
        pick_flux, target, slot_obs, index, observed_t, weight_t, flux, matrices, by_slot, obs = call(
            prepare,
            [
                ((slots, 3 * owners * BLOCKS // 2), BF16),
                slot_tile,
                ((slots, 3 * OBLK_DEV), BF16),
                ((index_rows, LANES), F32),
                obs_tile,
                obs_tile,
                like(prior_flux),
                like(footprint),
                ((slots // 8, 8, TILES, LANES), F32),
                ((slots,), jnp.int32),
            ],
            (*small, prior_flux, footprint, turned),
            [
                *(pltpu.VMEM(*like(value)) for value in small),
                pltpu.SMEM(*like(obs_slot)),
                pltpu.SMEM(*like(slot_count)),
                pltpu.SemaphoreType.DMA((len(small) + 3,)),
                pltpu.SemaphoreType.DMA((owners,)),
                pltpu.SemaphoreType.DMA((8,)),
            ],
            hbm,
        )
        order = [0, cells // 2, *range(1, cells // 2), *range(cells // 2 + 1, cells)]
        fluxes = exchange(flux, prior_flux, "cell", cells)
        m0, x0 = call(
            functools.partial(first_model, order),
            [obs_tile, slot_tile],
            (*(fluxes[k] for k in order), by_slot, pick_flux, target, obs),
            sum_scratch,
        )
        message, d0 = call(
            functools.partial(first_adjoint, wins),
            [((half + index_rows, LANES), F32), obs_tile],
            (*exchange(m0, m0, "win", wins), observed_t, weight_t, slot_obs, index, matrices),
        )
        messages = exchange(message, message, "cell", cells)
        (m1,) = call(
            functools.partial(second_model, cells),
            [obs_tile],
            (*messages, target, x0, by_slot, obs),
            sum_scratch,
        )
        *blocks, d1 = call(
            functools.partial(second_adjoint, wins),
            [((capacity // 2, LANES), F32)] * owners + [obs_tile],
            (*exchange(m1, m1, "win", wins), observed_t, weight_t, d0, slot_obs, matrices),
            [pltpu.VMEM((owners, capacity // 2, LANES), F32)],
        )
        arrays = [send(block, "cell", cells, cells - 1 - i) for i, block in enumerate(blocks[:-1])]
        arrays = [blocks[-1]] + arrays[::-1]
        pick, departure = call(
            functools.partial(prepare_increment, cells, capacity // 2),
            [((2 * BLOCKS, max(LANES, half)), BF16), ((1, OBLK_DEV * OB), F32)],
            (*messages, d1),
        )
        (increment,) = call(
            gather_increment,
            [((WIN_DEV, CBLK_DEV * CB), F32)],
            (*arrays[::-1], pick),
        )
        return increment, departure

    return local


def solution(mesh):
    placed = (
        P(("ens", "win"), "cell"),
        P(("ens", "cell"), None),
        P(("ens", "cell"), None),
        P("cell", "win", None, None, None),
        P("cell", "win", None, None),
        P("cell", "win", None, None),
        P("cell", "win", None),
    )
    return jax.shard_map(
        make_local(mesh.shape["cell"], mesh.shape["win"]),
        mesh=mesh,
        in_specs=placed,
        out_specs=(P(("ens", "win"), "cell"), P(("ens", "cell"), None)),
        check_vma=False,
    )
```
